256 devices in a mesh: dp: 16 (over z, x_lo), pencil: 16 (over x_hi, y, core).
Axes of the slice: x: 4 (x_hi: 2, x_lo: 2; x = x_hi * 2 + x_lo), y: 4, z: 8, core: 2. Of those that a mesh axis runs over, the one named last changes fastest.
Arguments:
- clips: bfloat16 [32, 64, 512, 512], P('dp', None, 'pencil'), may hold values from -6 to 6
- cotangent: bfloat16 [32, 64, 512, 512], P('dp', None, 'pencil'), may hold values from -6 to 6
- spectral_weight: bfloat16 [64, 64, 64, 128], P(None, 'pencil'), may hold values from -3 to 3
- point_weight: bfloat16 [64, 64], replicated, may hold values from -0.75 to 0.75
- bias: bfloat16 [64], replicated, may hold values from -3 to 3
Outputs:
- input_grad: bfloat16 [32, 64, 512, 512], P('dp', None, 'pencil')
- spectral_grad: float32 [64, 64, 64, 128], P('dp', 'pencil')
The draws below stay inside these ranges and needn't reach their ends.
All inputs are finite; a program needn't handle non-finite values.
Results may differ from the reference program's by a relative error of at most 0.029.
Values may be sent and summed in bfloat16 or wider, within the bound.
A program may use at most 192 MiB of HBM per device.

```python
import math
import jax
import jax.numpy as jnp
from jax import lax

CHAN = 64
ROWS = 512
COLS = 512
MODES_R = 64
MODES_C = 64
CLIPS = 32


def steps_of(own_key, dims, cuts, least, largest):
    level = 1.0
    for position, parts in cuts:
        draws = jax.random.uniform(jax.random.fold_in(jax.random.fold_in(own_key, 6), position), (parts,), jnp.float32, least / len(cuts), largest / len(cuts))
        level = level * jnp.repeat(jnp.exp(draws), dims[position] // parts).reshape((-1,) + (1,) * (len(dims) - 1 - position))
    return level


def normal_values(key, shape, scale, limit, pieces=(), kind=jnp.bfloat16):
    array = jax.random.normal(key, shape, jnp.float32) * scale
    if len(pieces) > 0:
        array = steps_of(key, shape, pieces, -0.22, 0.18) * array
    return jnp.clip(array, min=-limit, max=limit).astype(kind)


def setup_inputs(seed: int = 0) -> dict:
    key_of = jax.random.split(jax.random.key(seed), 6)
    return {
        "clips": normal_values(key_of[0], (CLIPS, CHAN, ROWS, COLS), 1.0, 6.0, ((0, 16), (2, 16))),
        "cotangent": normal_values(key_of[1], (CLIPS, CHAN, ROWS, COLS), 1.0, 6.0, ((0, 16), (2, 16))),
        "spectral_weight": normal_values(key_of[2], (MODES_R, MODES_C, CHAN, 2 * CHAN), 0.5, 3.0, ((1, 16),)),
        "point_weight": normal_values(key_of[3], (CHAN, CHAN), CHAN ** -0.5, 0.75),
        "bias": normal_values(key_of[4], (CHAN,), 0.5, 3.0),
    }


TWO_PI = 2.0 * math.pi

def keep_rounded(values):
    return lax.optimization_barrier(values.astype(jnp.bfloat16)).astype(jnp.float32)

def col_tables():
    sample = jnp.arange(COLS, dtype=jnp.int32)[:, None]
    frequency = jnp.arange(MODES_C, dtype=jnp.int32)[None, :]
    phase = (sample * frequency % COLS).astype(jnp.float32) * (TWO_PI / COLS)
    return (keep_rounded(jnp.cos(phase)), keep_rounded(jnp.sin(phase)))

def row_tables():
    sample = jnp.arange(ROWS, dtype=jnp.int32)[:, None]
    modes = jnp.arange(MODES_R, dtype=jnp.int32)
    frequency = jnp.where(modes < MODES_R // 2, modes, ROWS - MODES_R + modes)[None, :]
    phase = (sample * frequency % ROWS).astype(jnp.float32) * (TWO_PI / ROWS)
    return (keep_rounded(jnp.cos(phase)), keep_rounded(jnp.sin(phase)))

def forward_spec(values, tables):
    cos_c, sin_c, cos_r, sin_r = tables
    data = values.astype(jnp.float32)
    col_cos = keep_rounded(jnp.einsum('chw,wk->chk', data, cos_c))
    col_sin = keep_rounded(jnp.einsum('chw,wk->chk', data, sin_c))
    real_part = jnp.einsum('chk,hf->cfk', col_cos, cos_r) - jnp.einsum('chk,hf->cfk', col_sin, sin_r)
    imag_part = -(jnp.einsum('chk,hf->cfk', col_cos, sin_r) + jnp.einsum('chk,hf->cfk', col_sin, cos_r))
    return (real_part, imag_part)

def inverse_spec(real_part, imag_part, tables):
    cos_c, sin_c, cos_r, sin_r = tables
    q_cos = jnp.einsum('cfk,hf->chk', real_part, cos_r) - jnp.einsum('cfk,hf->chk', imag_part, sin_r)
    q_sin = -jnp.einsum('cfk,hf->chk', real_part, sin_r) - jnp.einsum('cfk,hf->chk', imag_part, cos_r)
    q_cos = keep_rounded(q_cos)
    q_sin = keep_rounded(q_sin)
    return jnp.einsum('chk,wk->chw', q_cos, cos_c) + jnp.einsum('chk,wk->chw', q_sin, sin_c)

def reference(clips, cotangent, spectral_weight, point_weight, bias):
    cos_c, sin_c = col_tables()
    cos_r, sin_r = row_tables()
    tables = (cos_c, sin_c, cos_r, sin_r)
    modes = jnp.arange(MODES_C, dtype=jnp.int32)
    mode_scale = jnp.where(modes == 0, 1.0, 2.0).astype(jnp.float32) / (ROWS * COLS)
    w_real = spectral_weight[..., :CHAN].astype(jnp.float32)
    w_imag = spectral_weight[..., CHAN:].astype(jnp.float32)
    point_f32 = point_weight.astype(jnp.float32)
    bias_f32 = bias.astype(jnp.float32)[:, None, None]

    def per_clip(running, inputs_pair):
        values, cot = inputs_pair
        x_real, x_imag = forward_spec(values, tables)
        x_real = keep_rounded(x_real)
        x_imag = keep_rounded(x_imag)
        y_real = jnp.einsum('cfk,fkco->ofk', x_real, w_real) - jnp.einsum('cfk,fkco->ofk', x_imag, w_imag)
        y_imag = jnp.einsum('cfk,fkco->ofk', x_real, w_imag) + jnp.einsum('cfk,fkco->ofk', x_imag, w_real)
        y_real = keep_rounded(y_real * mode_scale)
        y_imag = keep_rounded(y_imag * mode_scale)
        result_field = inverse_spec(y_real, y_imag, tables)
        pre_act = result_field + jnp.einsum('chw,co->ohw', values.astype(jnp.float32), point_f32) + bias_f32
        derivative = 0.5 * (1.0 + lax.erf(pre_act / math.sqrt(2.0))) + pre_act * jnp.exp(-0.5 * pre_act * pre_act) / math.sqrt(TWO_PI)
        act_grad = keep_rounded(cot.astype(jnp.float32) * derivative)
        d_real, d_imag = forward_spec(act_grad, tables)
        g_real = keep_rounded(d_real * mode_scale)
        g_imag = keep_rounded(d_imag * mode_scale)
        part_real = jnp.einsum('cfk,ofk->fkco', x_real, g_real) + jnp.einsum('cfk,ofk->fkco', x_imag, g_imag)
        part_imag = jnp.einsum('cfk,ofk->fkco', x_real, g_imag) - jnp.einsum('cfk,ofk->fkco', x_imag, g_real)
        running = running + jnp.concatenate([part_real, part_imag], axis=-1)
        dx_real = jnp.einsum('fkco,ofk->cfk', w_real, g_real) + jnp.einsum('fkco,ofk->cfk', w_imag, g_imag)
        dx_imag = jnp.einsum('fkco,ofk->cfk', w_real, g_imag) - jnp.einsum('fkco,ofk->cfk', w_imag, g_real)
        spectral_part = inverse_spec(keep_rounded(dx_real), keep_rounded(dx_imag), tables)
        clip_grad = spectral_part + jnp.einsum('ohw,co->chw', act_grad, point_f32)
        return (running, clip_grad.astype(jnp.bfloat16))
    start_sum = jnp.zeros((MODES_R, MODES_C, CHAN, 2 * CHAN), jnp.float32)
    running, grads = lax.scan(per_clip, start_sum, (clips, cotangent))
    return (grads, running)
```

```python
import functools
import math

import jax
import jax.numpy as jnp
import ml_dtypes
import numpy as np
from jax import lax
from jax.experimental import pallas as pl
from jax.experimental.pallas import tpu as pltpu
from jax.sharding import PartitionSpec as P

TWO_PI = 2.0 * math.pi
MESH = pl.DeviceIdType.MESH
BF = jnp.bfloat16
F32 = jnp.float32
GROUP = 8
HALVES = 2
TN = (((0,), (0,)), ((), ()))
NT = (((1,), (1,)), ((), ()))
NN = (((1,), (0,)), ((), ()))


def dot(a, b, dims=NN):
    return lax.dot_general(a, b, dims, preferred_element_type=F32)


def tables():
    w = np.arange(512)
    g, half, j4 = np.meshgrid(np.arange(8), np.arange(2), np.arange(4), indexing="ij")
    j = ((half * 8 + g) * 4 + j4).reshape(8, 8)
    phase = (j[:, :, None] * w % 512) * (TWO_PI / 512)
    col = np.stack([np.cos(phase), np.sin(phase)], axis=1).reshape(128, 512)
    k = np.arange(64)
    f = np.where(k < 32, k, 448 + k)
    h = np.arange(512)
    phase = (h[:, None] * f[None, :] % 512) * (TWO_PI / 512)
    ca, sa = np.cos(phase), np.sin(phase)
    r = np.stack([ca, sa], axis=1).reshape(2, 8, 32, 128)
    eye = np.eye(4)
    fwd = np.einsum("xshn,cd->xschdn", r, eye).reshape(2, 1024, 512)
    first = np.stack([ca, -sa], axis=1)
    second = np.stack([-sa, -ca], axis=1)
    inv = np.stack([first, second], axis=1).reshape(2, 8, 32, 2, 128)
    inv = np.einsum("xshqn,cd->xcnsqdh", inv, eye).reshape(2, 512, 2048)
    perm = np.einsum("ad,be,cf->abcfed", np.eye(4), np.eye(16), np.eye(8)).reshape(512, 512)
    return [np.asarray(t, np.float32).astype(ml_dtypes.bfloat16) for t in (col, fwd, inv, perm)]


def derivative(z):
    a = jnp.abs(z)
    e = jnp.exp(z * z * -0.5)
    t = 1.0 / (1.0 + (0.3275911 / math.sqrt(2.0)) * a)
    poly = 1.061405429 * 0.5
    for c in (-1.453152027, 1.421413741, -0.284496736, 0.254829592):
        poly = poly * t + 0.5 * c
    q = e * (poly * t - a * (1.0 / math.sqrt(TWO_PI)))
    return jnp.where(z >= 0.0, 1.0 - q, q)


def kernel(
    dps,
    clips, cot, weight, pw, bias, col_h, fwd_h, inv_h, perm_h,
    out, sgrad,
    xv, cv, wv, col, fwd, inv, perm,
    send, recv, zs, dz, xp, xr, ya,
    xbf, xb, xbr, gbf, gb, gbr, dd, y3, kf, kb, bcol,
    in_sem, a2a_send, a2a_recv, x_send, x_recv, dp_send, dp_recv, out_sem,
):
    pen = lax.axis_index("pencil")
    dpi = lax.axis_index("dp")
    half = pen // GROUP
    me = pen % GROUP
    other = 1 - half
    partner = other * GROUP + me

    loads = [
        pltpu.make_async_copy(clips.at[0], xv.at[0], in_sem.at[0]),
        pltpu.make_async_copy(col_h, col, in_sem.at[1]),
        pltpu.make_async_copy(clips.at[1], xv.at[1], in_sem.at[2]),
        pltpu.make_async_copy(fwd_h.at[half], fwd, in_sem.at[3]),
        pltpu.make_async_copy(perm_h, perm, in_sem.at[4]),
        pltpu.make_async_copy(weight, wv, in_sem.at[5]),
        pltpu.make_async_copy(inv_h.at[half], inv, in_sem.at[6]),
        pltpu.make_async_copy(cot, cv, in_sem.at[7]),
    ]
    for copy in loads:
        copy.start()

    barrier = pltpu.get_barrier_semaphore()

    def greet_group(r, carry):
        peer = half * GROUP + (me + r) % GROUP
        pl.semaphore_signal(barrier, inc=1, device_id={"pencil": peer}, device_id_type=MESH)
        return carry

    lax.fori_loop(1, GROUP, greet_group, 0)
    pl.semaphore_signal(barrier, inc=1, device_id={"pencil": partner}, device_id_type=MESH)

    def greet_dp(r, carry):
        pl.semaphore_signal(barrier, inc=1, device_id={"dp": (dpi + r) % dps}, device_id_type=MESH)
        return carry

    if dps > 1:
        lax.fori_loop(1, dps, greet_dp, 0)

    lane = lax.broadcasted_iota(jnp.int32, (1, 128), 1)
    low = lane < 64
    sign = jnp.where(low, 1.0, -1.0).astype(F32)

    def columns(values, b, phase):
        def step(n, carry):
            rows = values[b, pl.ds(pl.multiple_of(n * 8, 8), 8)].reshape(256, 512)
            part = dot(col[...], rows, NT)
            for i in range(2):
                piece = part[:, i * 128 : (i + 1) * 128].reshape(8, 16, 128).astype(BF)
                at = pl.multiple_of((2 * n + i) * 16, 16)
                send[phase, b, :, pl.ds(at, 16), :] = piece
            return carry

        lax.fori_loop(0, 8, step, 0)

    def scatter(b, phase):
        def step(r, carry):
            to = (me + r) % GROUP
            pltpu.make_async_remote_copy(
                src_ref=send.at[phase, b, to],
                dst_ref=recv.at[phase, b, me],
                send_sem=a2a_send.at[phase, b],
                recv_sem=a2a_recv.at[phase, b],
                device_id={"pencil": half * GROUP + to},
                device_id_type=MESH,
            ).start()
            return carry

        lax.fori_loop(1, GROUP, step, 0)
        pltpu.make_async_copy(
            send.at[phase, b, me], recv.at[phase, b, me], a2a_recv.at[phase, b]
        ).start()

    def arrived(b, phase):
        whole = recv.at[phase, b]
        pltpu.make_async_copy(whole, whole, a2a_recv.at[phase, b]).wait()

    def rows_forward(b, phase, which):
        arrived(b, phase)
        lhs = jnp.concatenate([recv[phase, b, s] for s in range(GROUP)], axis=1)
        pieces = []
        for c4 in range(4):
            part = dot(lhs, fwd[:, c4 * 128 : (c4 + 1) * 128]).reshape(16, 2, 8, 128)
            cosine = part[:, 0].reshape(128, 128)
            sine = part[:, 1].reshape(128, 128)
            pieces.append((cosine * sign - pltpu.roll(sine, 64, 1)).astype(BF))
        spec = dot(jnp.concatenate(pieces, axis=0), perm[...], TN).astype(BF)
        xp[which, b, 0] = spec[:, :256]
        xp[which, b, 1] = spec[:, 256:]
        pltpu.make_async_remote_copy(
            src_ref=xp.at[which, b, other],
            dst_ref=xr.at[which, b],
            send_sem=x_send.at[which, b],
            recv_sem=x_recv.at[which, b],
            device_id={"pencil": partner},
            device_id_type=MESH,
        ).start()

    def x_wait(which, b, ref):
        pltpu.make_async_copy(ref, ref, x_recv.at[which, b]).wait()

    def spectrum(which, b):
        x_wait(which, b, xr.at[which, b])
        return xp[which, b, half].astype(F32) + xr[which, b].astype(F32)

    def to_owner(src, dst, i):
        def step(r, carry):
            to = (dpi + r) % dps
            pltpu.make_async_remote_copy(
                src_ref=src.at[to],
                dst_ref=dst.at[dpi],
                send_sem=dp_send.at[i],
                recv_sem=dp_recv.at[i],
                device_id={"dp": to},
                device_id_type=MESH,
            ).start()
            return carry

        if dps > 1:
            lax.fori_loop(1, dps, step, 0)
        pltpu.make_async_copy(src.at[dpi], dst.at[dpi], dp_recv.at[i]).start()

    def give_partner(i, b):
        pltpu.make_async_remote_copy(
            src_ref=ya.at[i, b, half],
            dst_ref=ya.at[i, b, half],
            send_sem=x_send.at[2 + i, b],
            recv_sem=x_recv.at[2 + i, b],
            device_id={"pencil": partner},
            device_id_type=MESH,
        ).start()

    def rows_back(i, b, phase):
        x_wait(2 + i, b, ya.at[i, b, other])
        turned = dot(perm[:, :256], ya[i, b, 0], NT) + dot(perm[:, 256:], ya[i, b, 1], NT)
        turned = turned.astype(BF)
        lhs = jnp.concatenate([turned[c * 128 : (c + 1) * 128] for c in range(4)], axis=1)
        for s in range(GROUP):
            lines = dot(lhs, inv[:, s * 256 : (s + 1) * 256])
            both = jnp.concatenate(
                [lines[:, :128].reshape(16, 8, 128), lines[:, 128:].reshape(16, 8, 128)], axis=1
            )
            send[phase, b, s] = both.reshape(256, 128).astype(BF)
        scatter(b, phase)

    def field(b, phase, n):
        at = pl.multiple_of(n * 16, 16)
        lines = recv[phase, b, :, pl.ds(at, 16), :].reshape(128, 128)
        return dot(lines, col[...], TN)

    def mix_points(values, b, matrix, add):
        def step(t, carry):
            at = pl.multiple_of(t * 16, 16)
            for n in range(2):
                lanes = slice(n * 256, (n + 1) * 256)
                tile = values[b, :, pl.ds(at, 16), lanes].astype(F32)
                for i in range(2):
                    rows = tile[:, i * 8 : (i + 1) * 8].reshape(512, 256).astype(BF)
                    got = dot(matrix[...], rows)
                    if add is not None:
                        got = got + jnp.concatenate([add[...]] * 2, axis=1)
                    to = pl.multiple_of(t * 16 + i * 8, 8)
                    zs[b, :, pl.ds(to, 8), lanes] = got.reshape(64, 8, 256)
            return carry

        lax.fori_loop(0, 2, step, 0)

    loads[0].wait()
    loads[1].wait()
    columns(xv, 0, 0)
    pl.semaphore_wait(barrier, GROUP - 1 + 1 + dps - 1)
    scatter(0, 0)
    loads[2].wait()
    columns(xv, 1, 0)
    scatter(1, 0)

    row = lax.broadcasted_iota(jnp.int32, (512, 64), 0)
    lanes64 = lax.broadcasted_iota(jnp.int32, (512, 64), 1)
    spread = jnp.where(row // 8 == lanes64, 1.0, 0.0).astype(BF)
    same = (
        lax.broadcasted_iota(jnp.int32, (512, 512), 0) % 8
        == lax.broadcasted_iota(jnp.int32, (512, 512), 1) % 8
    )
    kf[...] = jnp.where(same, dot(dot(spread, pw[...], NT).astype(BF), spread, NT), 0.0).astype(BF)
    kb[...] = jnp.where(same, dot(dot(spread, pw[...]).astype(BF), spread, NT), 0.0).astype(BF)
    biased = (spread.astype(F32) * bias[...].astype(F32)).astype(BF)
    bcol[...] = dot(biased, jnp.ones((64, 128), BF))
    mix_points(xv, 0, kf, bcol)
    mix_points(xv, 1, kf, bcol)

    loads[3].wait()
    loads[4].wait()
    rows_forward(0, 0, 0)
    rows_forward(1, 0, 0)

    for b in range(2):
        spec = spectrum(0, b)
        for ri in range(2):
            for j in range(4):
                for p in range(2):
                    if p == j // 2:
                        part = spec[ri * 64 : (ri + 1) * 64, p * 128 : (p + 1) * 128]
                        part = jnp.where(low if j % 2 == 0 else jnp.logical_not(low), part, 0.0)
                    else:
                        part = jnp.zeros((64, 128), F32)
                    xbf[p, pl.ds(ri * 8 + j * 2 + b, 64, stride=16), :] = part
    per = 1024 // dps
    for d in range(dps):
        for p in range(2):
            xb[d, :, p * 128 : (p + 1) * 128] = xbf[p, d * per : (d + 1) * per, :].astype(BF)
    to_owner(xb, xbr, 0)

    loads[5].wait()
    row8 = lax.broadcasted_iota(jnp.int32, (8, 128), 0)
    zero_mode = jnp.logical_and(row8 < 2, pen == 0)
    scale8 = jnp.where(zero_mode, 1.0, 2.0).astype(F32) / 262144.0
    kper = 64 // dps

    def mix_step(d, carry):
        for i in range(kper):
            k = d * kper + i
            got = dot(xb[d, i * 16 : (i + 1) * 16, :], wv[k].reshape(256, 128))
            y = got[:8] - sign * pltpu.roll(got[8:], 64, 1)
            y3[pl.ds(pl.multiple_of(k * 8, 8), 8), :] = y * scale8
        return carry

    lax.fori_loop(0, dps, mix_step, 0)
    for b in range(2):
        for p in range(2):
            first = y3[pl.ds(4 * p + b, 64, stride=8), :]
            second = y3[pl.ds(4 * p + 2 + b, 64, stride=8), :]
            real = jnp.where(low, first, pltpu.roll(second, 64, 1))
            imag = jnp.where(low, pltpu.roll(first, 64, 1), second)
            ya[0, b, half, 0:64, p * 128 : (p + 1) * 128] = real.astype(BF)
            ya[0, b, half, 64:128, p * 128 : (p + 1) * 128] = imag.astype(BF)
        give_partner(0, b)
    loads[6].wait()
    rows_back(0, 0, 1)
    rows_back(0, 1, 1)

    loads[7].wait()
    for b in range(2):
        arrived(b, 1)

        def act_step(n, carry, b=b):
            at = pl.ds(pl.multiple_of(n * 4, 4), 4)
            z = field(b, 1, n) + zs[b, at].reshape(128, 512)
            grad = cv[b, at].reshape(128, 512).astype(F32) * derivative(z)
            dz[b, at] = grad.astype(BF).reshape(4, 32, 512)
            return carry

        lax.fori_loop(0, 16, act_step, 0)
        columns(dz, b, 2)
        scatter(b, 2)
    mix_points(dz, 0, kb, None)
    mix_points(dz, 1, kb, None)

    rows_forward(0, 2, 1)
    rows_forward(1, 2, 1)
    scale_lane = jnp.where(jnp.logical_and(low, pen == 0), 1.0, 2.0).astype(F32) / 262144.0
    for b in range(2):
        spec = spectrum(1, b)
        for p in range(2):
            part = spec[:, p * 128 : (p + 1) * 128]
            part = part * (scale_lane if p == 0 else 2.0 / 262144.0)
            real, imag = part[:64], part[64:]
            real_r, imag_r = pltpu.roll(real, 64, 1), pltpu.roll(imag, 64, 1)
            for i, (re, im) in enumerate(
                ((jnp.where(low, real, imag_r), jnp.where(low, imag, real_r)),
                 (jnp.where(low, real_r, imag), jnp.where(low, imag_r, real)))
            ):
                row_at = (2 * p + i) * 2 + b
                gbf[pl.ds(row_at, 64, stride=16), :] = re
                gbf[pl.ds(8 + row_at, 64, stride=16), :] = im * sign
    for d in range(dps):
        gb[d] = gbf[d * per : (d + 1) * per, :].astype(BF)
    to_owner(gb, gbr, 1)

    def back_step(d, carry):
        for i in range(kper):
            k = d * kper + i
            got = dot(gb[d, i * 16 : (i + 1) * 16, :], wv[k].reshape(256, 128), NT)
            at = pl.ds(pl.multiple_of(k * 16, 16), 16)
            dd[0, at, :] = got[:, :128]
            dd[1, at, :] = got[:, 128:]
        return carry

    lax.fori_loop(0, dps, back_step, 0)
    for b in range(2):
        for p in range(2):
            for ri in range(2):
                first = dd[p, pl.ds(ri * 8 + 4 * p + b, 64, stride=16), :]
                second = dd[p, pl.ds(ri * 8 + 4 * p + 2 + b, 64, stride=16), :]
                ya[1, b, half, ri * 64 : (ri + 1) * 64, p * 128 : (p + 1) * 128] = jnp.where(
                    low, first, second
                ).astype(BF)
        give_partner(1, b)
    rows_back(1, 0, 3)
    rows_back(1, 1, 3)

    for i, ref in enumerate((xbr, gbr)):
        pltpu.make_async_copy(ref, ref, dp_recv.at[i]).wait()
    for k in range(kper):
        left = xbr[:, k * 16 : (k + 1) * 16, :].reshape(dps * 16, 256)
        right = gbr[:, k * 16 : (k + 1) * 16, :].reshape(dps * 16, 128)
        sgrad[k] = dot(left, right, TN).reshape(4, 64, 128)

    for b in range(2):
        arrived(b, 3)

        def out_step(n, carry, b=b):
            at = pl.ds(pl.multiple_of(n * 4, 4), 4)
            got = field(b, 3, n) + zs[b, at].reshape(128, 512)
            xv[b, at] = got.astype(BF).reshape(4, 32, 512)
            return carry

        lax.fori_loop(0, 16, out_step, 0)
        pltpu.make_async_copy(xv.at[b], out.at[b], out_sem.at[b]).start()

    for phase in range(4):
        for b in range(2):
            sent = send.at[phase, b, pl.ds(0, GROUP - 1)]
            pltpu.make_async_copy(sent, sent, a2a_send.at[phase, b]).wait()
            ref = xr.at[0, b]
            pltpu.make_async_copy(ref, ref, x_send.at[phase, b]).wait()
    if dps > 1:
        for i, ref in enumerate((xb, gb)):
            sent = ref.at[pl.ds(0, dps - 1)]
            pltpu.make_async_copy(sent, sent, dp_send.at[i]).wait()
    for b in range(2):
        pltpu.make_async_copy(xv.at[b], out.at[b], out_sem.at[b]).wait()


def shards(dps, clips, cotangent, spectral_weight, point_weight, bias):
    col, fwd, inv, perm = [jnp.asarray(t) for t in tables()]
    any_spec = pl.BlockSpec(memory_space=pl.ANY)
    vmem = pl.BlockSpec(memory_space=pltpu.VMEM)
    per = 1024 // dps
    dma = pltpu.SemaphoreType.DMA
    return pl.pallas_call(
        functools.partial(kernel, dps),
        out_shape=(
            jax.ShapeDtypeStruct((2, 64, 32, 512), BF),
            jax.ShapeDtypeStruct((64 // dps, 4, 64, 128), F32),
        ),
        in_specs=[any_spec] * 3 + [vmem] * 2 + [any_spec] * 4,
        out_specs=(any_spec, vmem),
        scratch_shapes=[
            pltpu.VMEM((2, 64, 32, 512), BF),
            pltpu.VMEM((2, 64, 32, 512), BF),
            pltpu.VMEM((64, 4, 64, 128), BF),
            pltpu.VMEM((128, 512), BF),
            pltpu.VMEM((1024, 512), BF),
            pltpu.VMEM((512, 2048), BF),
            pltpu.VMEM((512, 512), BF),
            pltpu.VMEM((4, 2, GROUP, 256, 128), BF),
            pltpu.VMEM((4, 2, GROUP, 256, 128), BF),
            pltpu.VMEM((2, 64, 32, 512), F32),
            pltpu.VMEM((2, 64, 32, 512), BF),
            pltpu.VMEM((2, 2, 2, 128, 256), BF),
            pltpu.VMEM((2, 2, 128, 256), BF),
            pltpu.VMEM((2, 2, 2, 128, 256), BF),
            pltpu.VMEM((2, 1024, 128), F32),
            pltpu.VMEM((dps, per, 256), BF),
            pltpu.VMEM((dps, per, 256), BF),
            pltpu.VMEM((1024, 128), F32),
            pltpu.VMEM((dps, per, 128), BF),
            pltpu.VMEM((dps, per, 128), BF),
            pltpu.VMEM((2, 1024, 128), F32),
            pltpu.VMEM((512, 128), F32),
            pltpu.VMEM((512, 512), BF),
            pltpu.VMEM((512, 512), BF),
            pltpu.VMEM((512, 128), F32),
            dma((8,)),
            dma((4, 2)),
            dma((4, 2)),
            dma((4, 2)),
            dma((4, 2)),
            dma((2,)),
            dma((2,)),
            dma((2,)),
        ],
        compiler_params=pltpu.CompilerParams(
            collective_id=0, has_side_effects=True, vmem_limit_bytes=60 * 1024 * 1024
        ),
        cost_estimate=pl.CostEstimate(
            flops=20_000_000_000, bytes_accessed=20_000_000, transcendentals=4_000_000
        ),
    )(clips, cotangent, spectral_weight, point_weight, bias.reshape(1, 64), col, fwd, inv, perm)


def solution(mesh):
    in_specs = (
        P("dp", None, "pencil", None),
        P("dp", None, "pencil", None),
        P(None, "pencil", None, None),
        P(),
        P(),
    )
    out_specs = (P("dp", None, "pencil", None), P("dp", "pencil", None, None))
    return jax.shard_map(
        functools.partial(shards, mesh.shape["dp"]),
        mesh=mesh,
        in_specs=in_specs,
        out_specs=out_specs,
        check_vma=False,
    )
```

```python
import functools
import math

import jax
import jax.numpy as jnp
import ml_dtypes
import numpy as np
from jax import lax
from jax.experimental import pallas as pl
from jax.experimental.pallas import tpu as pltpu
from jax.sharding import PartitionSpec as P

TWO_PI = 2.0 * math.pi
MESH = pl.DeviceIdType.MESH
BF = jnp.bfloat16
F32 = jnp.float32
GROUP = 8
TN = (((0,), (0,)), ((), ()))
NT = (((1,), (1,)), ((), ()))
NN = (((1,), (0,)), ((), ()))


def dot(a, b, dims=NN):
    return lax.dot_general(a, b, dims, preferred_element_type=F32)


def tables():
    w = np.arange(512)
    g, half, j4 = np.meshgrid(np.arange(8), np.arange(2), np.arange(4), indexing="ij")
    j = ((half * 8 + g) * 4 + j4).reshape(8, 8)
    phase = (j[:, :, None] * w % 512) * (TWO_PI / 512)
    col = np.stack([np.cos(phase), np.sin(phase)], axis=1).reshape(128, 512)
    k = np.arange(64)
    f = np.where(k < 32, k, 448 + k)
    h = np.arange(512)
    phase = (h[:, None] * f[None, :] % 512) * (TWO_PI / 512)
    ca, sa = np.cos(phase), np.sin(phase)
    r = np.stack([ca, sa], axis=1).reshape(2, 8, 32, 128)
    eye = np.eye(4)
    fwd = np.einsum("xshn,cd->xschdn", r, eye).reshape(2, 1024, 512)
    first = np.stack([ca, -sa], axis=1)
    second = np.stack([-sa, -ca], axis=1)
    inv = np.stack([first, second], axis=1).reshape(2, 8, 32, 2, 128)
    inv = np.einsum("xshqn,cd->xcnsqdh", inv, eye).reshape(2, 512, 2048)
    perm = np.einsum("ad,be,cf->abcfed", np.eye(4), np.eye(16), np.eye(8)).reshape(512, 512)
    return [np.asarray(t, np.float32).astype(ml_dtypes.bfloat16) for t in (col, fwd, inv, perm)]


def derivative(z):
    a = jnp.abs(z)
    e = jnp.exp(z * z * -0.5)
    d = 1.0 + (0.3275911 / math.sqrt(2.0)) * a
    t = pl.reciprocal(d, approx=True)
    t = t * (2.0 - d * t)
    poly = 1.061405429 * 0.5
    for c in (-1.453152027, 1.421413741, -0.284496736, 0.254829592):
        poly = poly * t + 0.5 * c
    q = e * (poly * t - a * (1.0 / math.sqrt(TWO_PI)))
    return jnp.where(z >= 0.0, 1.0 - q, q)


PEERS = ((2, 0), (2, 1), (1, 0), (3, 0), (1, 1), (3, 1), (0, 1))


def kernel(
    dps,
    clips, cot, weight, pw, bias, col_h, fwd_h, inv_h, perm_h,
    side, last, sgrad,
    xv, cv, wv, col, fwd, inv, perm,
    send, recv, zs, dz, xp, xr, ya,
    xbf, xb, xbr, gbf, gb, gbr, dd, y3, kf, kb, bcol,
    in_sem, clip_sem, a2a_send, a2a_recv, x_send, x_recv, dp_send, dp_recv, out_sem,
):
    pen = lax.axis_index("pencil")
    dpi = lax.axis_index("dp")
    half = pen // GROUP
    me = pen % GROUP
    other = 1 - half
    partner = other * GROUP + me
    per = 512 // dps
    kper = 64 // dps

    def clip_piece(b, n):
        at = pl.ds(n * 8, 8)
        return pltpu.make_async_copy(clips.at[b, at], xv.at[b, at], clip_sem.at[b, n])

    def load(src, dst, pieces, i):
        size = dst.shape[0] // pieces
        for n in range(pieces):
            at = pl.ds(n * size, size)
            pltpu.make_async_copy(src.at[at], dst.at[at], in_sem.at[i]).start()
        return pltpu.make_async_copy(dst, dst, in_sem.at[i]).wait

    col_wait = load(col_h, col, 1, 0)
    for b in range(2):
        for n in range(8):
            clip_piece(b, n).start()

    def peer_of(dy, dc):
        return (me // 2 + dy) % 4 * 2 + (me % 2 + dc) % 2

    barrier = pltpu.get_barrier_semaphore()
    for dy, dc in PEERS:
        peer = half * GROUP + peer_of(dy, dc)
        pl.semaphore_signal(barrier, inc=1, device_id={"pencil": peer}, device_id_type=MESH)
    pl.semaphore_signal(barrier, inc=1, device_id={"pencil": partner}, device_id_type=MESH)

    def greet_dp(r, carry):
        pl.semaphore_signal(barrier, inc=1, device_id={"dp": (dpi + r) % dps}, device_id_type=MESH)
        return carry

    if dps > 1:
        lax.fori_loop(1, dps, greet_dp, 0)

    lane = lax.broadcasted_iota(jnp.int32, (1, 128), 1)
    low = lane < 64
    sign = jnp.where(low, 1.0, -1.0).astype(F32)

    def slots(b, phase):
        return recv.at[phase, b] if phase < 3 else last.at[b]

    def columns(values, b, phase):
        def step(n, carry):
            if values is xv:
                clip_piece(b, n).wait()
            rows = values[b, pl.ds(pl.multiple_of(n * 8, 8), 8)].reshape(256, 512)
            part = dot(col[...], rows, NT)
            for i in range(2):
                piece = part[:, i * 128 : (i + 1) * 128].reshape(8, 16, 128).astype(BF)
                at = pl.multiple_of((2 * n + i) * 16, 16)
                send[phase, b, :, pl.ds(at, 16), :] = piece
            return carry

        lax.fori_loop(0, 8, step, 0, unroll=2)

    def send_one(b, phase, to):
        pltpu.make_async_remote_copy(
            src_ref=send.at[phase, b, to],
            dst_ref=slots(b, phase).at[me],
            send_sem=a2a_send.at[phase, b],
            recv_sem=a2a_recv.at[phase, b],
            device_id={"pencil": half * GROUP + to},
            device_id_type=MESH,
        ).start()

    def keep_own(b, phase):
        pltpu.make_async_copy(
            send.at[phase, b, me], slots(b, phase).at[me], a2a_recv.at[phase, b]
        ).start()

    def scatter(b, phase):
        for dy, dc in PEERS:
            send_one(b, phase, peer_of(dy, dc))
        keep_own(b, phase)

    def arrived(b, phase):
        whole = slots(b, phase)
        pltpu.make_async_copy(whole, whole, a2a_recv.at[phase, b]).wait()

    def rows_forward(b, phase, which):
        arrived(b, phase)
        lhs = jnp.concatenate([recv[phase, b, s] for s in range(GROUP)], axis=1)
        pieces = []
        for c4 in range(4):
            part = dot(lhs, fwd[:, c4 * 128 : (c4 + 1) * 128]).reshape(16, 2, 8, 128)
            cosine = part[:, 0].reshape(128, 128)
            sine = part[:, 1].reshape(128, 128)
            pieces.append((cosine * sign - pltpu.roll(sine, 64, 1)).astype(BF))
        spec = dot(jnp.concatenate(pieces, axis=0), perm[...], TN).astype(BF)
        xp[which, b, 0] = spec[:, :256]
        xp[which, b, 1] = spec[:, 256:]
        pltpu.make_async_remote_copy(
            src_ref=xp.at[which, b, other],
            dst_ref=xr.at[which, b],
            send_sem=x_send.at[which, b],
            recv_sem=x_recv.at[which, b],
            device_id={"pencil": partner},
            device_id_type=MESH,
        ).start()

    def x_wait(which, b, ref):
        pltpu.make_async_copy(ref, ref, x_recv.at[which, b]).wait()

    def spectrum(which, b):
        x_wait(which, b, xr.at[which, b])
        return xp[which, b, half].astype(F32) + xr[which, b].astype(F32)

    def to_owner(src, dst, i, b):
        def rows_of(d):
            return src.at[b, pl.ds(pl.multiple_of(d * per, per), per)]

        def step(r, carry):
            to = (dpi + r) % dps
            pltpu.make_async_remote_copy(
                src_ref=rows_of(to),
                dst_ref=dst.at[b, dpi],
                send_sem=dp_send.at[i, b],
                recv_sem=dp_recv.at[i, b],
                device_id={"dp": to},
                device_id_type=MESH,
            ).start()
            return carry

        if dps > 1:
            lax.fori_loop(1, dps, step, 0)
        pltpu.make_async_copy(rows_of(dpi), dst.at[b, dpi], dp_recv.at[i, b]).start()

    def give_partner(i, b):
        pltpu.make_async_remote_copy(
            src_ref=ya.at[i, b, half],
            dst_ref=ya.at[i, b, half],
            send_sem=x_send.at[2 + i, b],
            recv_sem=x_recv.at[2 + i, b],
            device_id={"pencil": partner},
            device_id_type=MESH,
        ).start()

    def rows_back(i, b, phase):
        x_wait(2 + i, b, ya.at[i, b, other])
        turned = dot(perm[:, :256], ya[i, b, 0], NT) + dot(perm[:, 256:], ya[i, b, 1], NT)
        turned = turned.astype(BF)
        lhs = jnp.concatenate([turned[c * 128 : (c + 1) * 128] for c in range(4)], axis=1)
        for dy, dc in PEERS + ((0, 0),):
            to = peer_of(dy, dc)
            lines = dot(lhs, inv[:, pl.ds(pl.multiple_of(to * 256, 256), 256)])
            both = jnp.concatenate(
                [lines[:, :128].reshape(16, 8, 128), lines[:, 128:].reshape(16, 8, 128)], axis=1
            )
            send[phase, b, to] = both.reshape(256, 128).astype(BF)
            if (dy, dc) == (0, 0):
                keep_own(b, phase)
            else:
                send_one(b, phase, to)

    def mix_points(values, b, matrix, add, tiles=(0, 2)):
        def step(t, carry):
            at = pl.multiple_of(t * 16, 16)
            for n in range(2):
                lanes = slice(n * 256, (n + 1) * 256)
                tile = values[b, :, pl.ds(at, 16), lanes].astype(F32)
                parts = []
                for i in range(2):
                    rows = tile[:, i * 8 : (i + 1) * 8].reshape(512, 256).astype(BF)
                    got = dot(matrix[...], rows)
                    if add is not None:
                        got = got + jnp.concatenate([add[...]] * 2, axis=1)
                        to = pl.multiple_of(t * 16 + i * 8, 8)
                        zs[b, :, pl.ds(to, 8), lanes] = got.reshape(64, 8, 256)
                    parts.append(got.reshape(64, 8, 256))
                if add is None:
                    xv[b, :, pl.ds(at, 16), lanes] = jnp.concatenate(parts, axis=1).astype(BF)
            return carry

        lax.fori_loop(*tiles, step, 0)

    row16 = lax.broadcasted_iota(jnp.int32, (16, 128), 0)
    scale = jnp.where(pen == 0, 1.0, 2.0).astype(F32) / 262144.0
    scale_lane = jnp.where(jnp.logical_and(low, pen == 0), 1.0, 2.0).astype(F32) / 262144.0

    def mix_modes(b):
        spec = spectrum(0, b)
        for ri in range(2):
            for j in range(4):
                for p in range(2):
                    if p == j // 2:
                        part = spec[ri * 64 : (ri + 1) * 64, p * 128 : (p + 1) * 128]
                        part = jnp.where(low if j % 2 == 0 else jnp.logical_not(low), part, 0.0)
                    else:
                        part = jnp.zeros((64, 128), F32)
                    xbf[p, pl.ds(ri * 4 + j, 64, stride=8), :] = part
        for p in range(2):
            xb[b, :, p * 128 : (p + 1) * 128] = xbf[p].astype(BF)
        to_owner(xb, xbr, 0, b)

        def step(n, carry):
            for i in range(8):
                pair = n * 8 + i
                at = pl.multiple_of(pair * 16, 16)
                both = jnp.concatenate(
                    [wv[2 * pair].reshape(256, 128), wv[2 * pair + 1].reshape(256, 128)], axis=1
                )
                got = dot(xb[b, pl.ds(at, 16), :], both)
                y3[pl.ds(at, 8), :] = got[:8, :128]
                y3[pl.ds(at + 8, 8), :] = got[8:, 128:]
            return carry

        lax.fori_loop(0, 4, step, 0)
        modes = []
        for j in range(4):
            real = y3[pl.ds(j, 64, stride=8), :]
            imag = y3[pl.ds(4 + j, 64, stride=8), :]
            mixed = real - sign * pltpu.roll(imag, 64, 1)
            modes.append(mixed * (scale if j == 0 else 2.0 / 262144.0))
        for p in range(2):
            first, second = modes[2 * p], modes[2 * p + 1]
            real = jnp.where(low, first, pltpu.roll(second, 64, 1))
            imag = jnp.where(low, pltpu.roll(first, 64, 1), second)
            ya[0, b, half, 0:64, p * 128 : (p + 1) * 128] = real.astype(BF)
            ya[0, b, half, 64:128, p * 128 : (p + 1) * 128] = imag.astype(BF)
        give_partner(0, b)

    def grad_modes(b):
        spec = spectrum(1, b)
        for p in range(2):
            part = spec[:, p * 128 : (p + 1) * 128]
            part = part * (scale_lane if p == 0 else 2.0 / 262144.0)
            real, imag = part[:64], part[64:]
            real_r, imag_r = pltpu.roll(real, 64, 1), pltpu.roll(imag, 64, 1)
            for i, (re, im) in enumerate(
                ((jnp.where(low, real, imag_r), jnp.where(low, imag, real_r)),
                 (jnp.where(low, real_r, imag), jnp.where(low, imag_r, real)))
            ):
                gbf[pl.ds(2 * p + i, 64, stride=8), :] = re
                gbf[pl.ds(4 + 2 * p + i, 64, stride=8), :] = im * sign
        gb[b] = gbf[...].astype(BF)
        to_owner(gb, gbr, 1, b)

        def step(n, carry):
            for i in range(8):
                pair = n * 8 + i
                at = pl.multiple_of(pair * 16, 16)
                got = dot(gb[b, pl.ds(at, 16), :], wv[pl.ds(2 * pair, 2)].reshape(512, 128), NT)
                for p in range(2):
                    dd[p, pl.ds(at, 8), :] = got[:8, p * 128 : (p + 1) * 128]
                    dd[p, pl.ds(at + 8, 8), :] = got[8:, 256 + p * 128 : 384 + p * 128]
            return carry

        lax.fori_loop(0, 4, step, 0)
        for p in range(2):
            for ri in range(2):
                first = dd[p, pl.ds(ri * 4 + 2 * p, 64, stride=8), :]
                second = dd[p, pl.ds(ri * 4 + 2 * p + 1, 64, stride=8), :]
                ya[1, b, half, ri * 64 : (ri + 1) * 64, p * 128 : (p + 1) * 128] = jnp.where(
                    low, first, second
                ).astype(BF)
        give_partner(1, b)

    def activation(b, chunks):
        def step(n, carry):
            at = pl.ds(pl.multiple_of(n * 4, 4), 4)
            lines = recv[1, b, :, pl.ds(pl.multiple_of(n * 16, 16), 16), :].reshape(128, 128)
            z = dot(lines, col[...], TN) + zs[b, at].reshape(128, 512)
            grad = cv[b, at].reshape(128, 512).astype(F32) * derivative(z)
            dz[b, at] = grad.astype(BF).reshape(4, 32, 512)
            return carry

        lax.fori_loop(*chunks, step, 0, unroll=4)

    def bypass(b):
        mix_points(dz, b, kb, None)
        pltpu.make_async_copy(xv.at[b], side.at[b], out_sem.at[b]).start()

    def weight_grad(b):
        for i, ref in enumerate((xbr, gbr)):
            pltpu.make_async_copy(ref.at[b], ref.at[b], dp_recv.at[i, b]).wait()
        first_rows = jnp.where(row16 < 8, 1.0, 0.0).astype(F32)
        for pair in range(kper // 2):
            at = slice(pair * 16, (pair + 1) * 16)
            left = xbr[b, :, at, :].reshape(dps * 16, 256)
            right = gbr[b, :, at, :].astype(F32)
            head = (right * first_rows).astype(BF).reshape(dps * 16, 128)
            tail = (right * (1.0 - first_rows)).astype(BF).reshape(dps * 16, 128)
            got = dot(left, jnp.concatenate([head, tail], axis=1), TN)
            for i in range(2):
                part = got[:, i * 128 : (i + 1) * 128].reshape(4, 64, 128)
                sgrad[2 * pair + i] = part if b == 0 else sgrad[2 * pair + i] + part

    col_wait()
    columns(xv, 0, 0)
    pl.semaphore_wait(barrier, GROUP - 1 + 1 + dps - 1)
    scatter(0, 0)
    fwd_wait = load(fwd_h.at[half], fwd, 4, 1)
    perm_wait = load(perm_h, perm, 2, 2)
    columns(xv, 1, 0)
    scatter(1, 0)
    weight_wait = load(weight, wv, 16, 3)
    inv_wait = load(inv_h.at[half], inv, 4, 4)
    cot_waits = [load(cot.at[b], cv.at[b], 8, 5 + b) for b in range(2)]

    row = lax.broadcasted_iota(jnp.int32, (512, 64), 0)
    lanes64 = lax.broadcasted_iota(jnp.int32, (512, 64), 1)
    spread = jnp.where(row // 8 == lanes64, 1.0, 0.0).astype(BF)
    same = (
        lax.broadcasted_iota(jnp.int32, (512, 512), 0) % 8
        == lax.broadcasted_iota(jnp.int32, (512, 512), 1) % 8
    )
    kf[...] = jnp.where(same, dot(dot(spread, pw[...], NT).astype(BF), spread, NT), 0.0).astype(BF)
    kb[...] = jnp.where(same, dot(dot(spread, pw[...]).astype(BF), spread, NT), 0.0).astype(BF)
    biased = (spread.astype(F32) * bias[...].astype(F32)).astype(BF)
    bcol[...] = dot(biased, jnp.ones((64, 128), BF))
    mix_points(xv, 0, kf, bcol)

    fwd_wait()
    perm_wait()
    rows_forward(0, 0, 0)
    mix_points(xv, 1, kf, bcol)
    rows_forward(1, 0, 0)
    weight_wait()
    mix_modes(0)
    mix_modes(1)
    inv_wait()
    rows_back(0, 0, 1)
    rows_back(0, 1, 1)

    arrived(0, 1)
    cot_waits[0]()
    activation(0, (0, 16))
    columns(dz, 0, 2)
    scatter(0, 2)
    arrived(1, 1)
    cot_waits[1]()
    activation(1, (0, 16))
    columns(dz, 1, 2)
    scatter(1, 2)
    bypass(0)
    rows_forward(0, 2, 1)
    bypass(1)
    rows_forward(1, 2, 1)
    grad_modes(0)
    grad_modes(1)
    rows_back(1, 0, 3)
    weight_grad(0)
    rows_back(1, 1, 3)
    weight_grad(1)

    for phase in range(4):
        for b in range(2):
            sent = send.at[phase, b, pl.ds(0, GROUP - 1)]
            pltpu.make_async_copy(sent, sent, a2a_send.at[phase, b]).wait()
            ref = xr.at[0, b]
            pltpu.make_async_copy(ref, ref, x_send.at[phase, b]).wait()
    if dps > 1:
        for i, ref in enumerate((xb, gb)):
            for b in range(2):
                sent = ref.at[b, pl.ds(0, 512 - per)]
                pltpu.make_async_copy(sent, sent, dp_send.at[i, b]).wait()
    for b in range(2):
        pltpu.make_async_copy(xv.at[b], side.at[b], out_sem.at[b]).wait()
        arrived(b, 3)


def finish(side, lines, col_h, sgrad, out, weights_out, sv, lv, col, gv, side_sem, sem):
    def piece(b, n):
        at = pl.ds(n * 8, 8)
        return pltpu.make_async_copy(side.at[b, at], sv.at[b, at], side_sem.at[b, n])

    pltpu.make_async_copy(col_h, col, sem.at[0]).start()
    for b in range(2):
        for s in range(GROUP):
            pltpu.make_async_copy(lines.at[b, s], lv.at[b, s], sem.at[1 + b]).start()
        for n in range(8):
            piece(b, n).start()
    pltpu.make_async_copy(sgrad, gv, sem.at[3]).start()
    pltpu.make_async_copy(col, col, sem.at[0]).wait()
    for b in range(2):
        pltpu.make_async_copy(lv.at[b], lv.at[b], sem.at[1 + b]).wait()

        def step(n, carry, b=b):
            piece(b, n).wait()
            for i in range(2):
                at = pl.ds(pl.multiple_of(n * 8 + i * 4, 4), 4)
                rows = pl.ds(pl.multiple_of((2 * n + i) * 16, 16), 16)
                part = lv[b, :, rows, :].reshape(128, 128)
                got = dot(part, col[...], TN) + sv[b, at].reshape(128, 512).astype(F32)
                sv[b, at] = got.astype(BF).reshape(4, 32, 512)
            at = pl.ds(n * 8, 8)
            pltpu.make_async_copy(sv.at[b, at], out.at[b, at], sem.at[4 + b]).start()
            return carry

        lax.fori_loop(0, 8, step, 0, unroll=2)
    pltpu.make_async_copy(gv, gv, sem.at[3]).wait()
    away = pltpu.make_async_copy(gv, weights_out, sem.at[6])
    away.start()
    for b in range(2):
        pltpu.make_async_copy(sv.at[b], sv.at[b], sem.at[4 + b]).wait()
    away.wait()


def shards(dps, clips, cotangent, spectral_weight, point_weight, bias):
    col, fwd, inv, perm = [jnp.asarray(t) for t in tables()]
    any_spec = pl.BlockSpec(memory_space=pl.ANY)
    vmem = pl.BlockSpec(memory_space=pltpu.VMEM)
    per = 512 // dps
    dma = pltpu.SemaphoreType.DMA
    grad_shape = jax.ShapeDtypeStruct((64 // dps, 4, 64, 128), F32)
    side, last, sgrad = pl.pallas_call(
        functools.partial(kernel, dps),
        out_shape=(
            jax.ShapeDtypeStruct((2, 64, 32, 512), BF),
            jax.ShapeDtypeStruct((2, GROUP, 256, 128), BF),
            grad_shape,
        ),
        in_specs=[any_spec] * 3 + [vmem] * 2 + [any_spec] * 4,
        out_specs=(any_spec, any_spec, vmem),
        scratch_shapes=[
            pltpu.VMEM((2, 64, 32, 512), BF),
            pltpu.VMEM((2, 64, 32, 512), BF),
            pltpu.VMEM((64, 4, 64, 128), BF),
            pltpu.VMEM((128, 512), BF),
            pltpu.VMEM((1024, 512), BF),
            pltpu.VMEM((512, 2048), BF),
            pltpu.VMEM((512, 512), BF),
            pltpu.VMEM((4, 2, GROUP, 256, 128), BF),
            pltpu.VMEM((3, 2, GROUP, 256, 128), BF),
            pltpu.VMEM((2, 64, 32, 512), F32),
            pltpu.VMEM((2, 64, 32, 512), BF),
            pltpu.VMEM((2, 2, 2, 128, 256), BF),
            pltpu.VMEM((2, 2, 128, 256), BF),
            pltpu.VMEM((2, 2, 2, 128, 256), BF),
            pltpu.VMEM((2, 512, 128), F32),
            pltpu.VMEM((2, 512, 256), BF),
            pltpu.VMEM((2, dps, per, 256), BF),
            pltpu.VMEM((512, 128), F32),
            pltpu.VMEM((2, 512, 128), BF),
            pltpu.VMEM((2, dps, per, 128), BF),
            pltpu.VMEM((2, 512, 128), F32),
            pltpu.VMEM((512, 128), F32),
            pltpu.VMEM((512, 512), BF),
            pltpu.VMEM((512, 512), BF),
            pltpu.VMEM((512, 128), F32),
            dma((7,)),
            dma((2, 8)),
            dma((4, 2)),
            dma((4, 2)),
            dma((4, 2)),
            dma((4, 2)),
            dma((2, 2)),
            dma((2, 2)),
            dma((2,)),
        ],
        compiler_params=pltpu.CompilerParams(
            collective_id=0, has_side_effects=True, vmem_limit_bytes=60 * 1024 * 1024
        ),
        cost_estimate=pl.CostEstimate(
            flops=20_000_000_000, bytes_accessed=20_000_000, transcendentals=4_000_000
        ),
    )(clips, cotangent, spectral_weight, point_weight, bias.reshape(1, 64), col, fwd, inv, perm)
    return pl.pallas_call(
        finish,
        out_shape=(jax.ShapeDtypeStruct((2, 64, 32, 512), BF), grad_shape),
        in_specs=[any_spec] * 4,
        out_specs=(any_spec, any_spec),
        scratch_shapes=[
            pltpu.VMEM((2, 64, 32, 512), BF),
            pltpu.VMEM((2, GROUP, 256, 128), BF),
            pltpu.VMEM((128, 512), BF),
            pltpu.VMEM(grad_shape.shape, F32),
            dma((2, 8)),
            dma((7,)),
        ],
        compiler_params=pltpu.CompilerParams(vmem_limit_bytes=60 * 1024 * 1024),
        cost_estimate=pl.CostEstimate(
            flops=600_000_000, bytes_accessed=10_000_000, transcendentals=0
        ),
    )(side, last, col, sgrad)


def solution(mesh):
    in_specs = (
        P("dp", None, "pencil", None),
        P("dp", None, "pencil", None),
        P(None, "pencil", None, None),
        P(),
        P(),
    )
    out_specs = (P("dp", None, "pencil", None), P("dp", "pencil", None, None))
    return jax.shard_map(
        functools.partial(shards, mesh.shape["dp"]),
        mesh=mesh,
        in_specs=in_specs,
        out_specs=out_specs,
        check_vma=False,
    )
```

```python
import functools
import math

import jax
import jax.numpy as jnp
import ml_dtypes
import numpy as np
from jax import lax
from jax.experimental import pallas as pl
from jax.experimental.pallas import tpu as pltpu
from jax.sharding import PartitionSpec as P

TWO_PI = 2.0 * math.pi
MESH = pl.DeviceIdType.MESH
BF = jnp.bfloat16
F32 = jnp.float32
GROUP = 8
TN = (((0,), (0,)), ((), ()))
NT = (((1,), (1,)), ((), ()))
NN = (((1,), (0,)), ((), ()))


def dot(a, b, dims=NN):
    return lax.dot_general(a, b, dims, preferred_element_type=F32)


def tables():
    w = np.arange(512)
    g, half, j4 = np.meshgrid(np.arange(8), np.arange(2), np.arange(4), indexing="ij")
    j = ((half * 8 + g) * 4 + j4).reshape(8, 8)
    phase = (j[:, :, None] * w % 512) * (TWO_PI / 512)
    col = np.stack([np.cos(phase), np.sin(phase)], axis=1).reshape(128, 512)
    k = np.arange(64)
    f = np.where(k < 32, k, 448 + k)
    h = np.arange(512)
    phase = (h[:, None] * f[None, :] % 512) * (TWO_PI / 512)
    ca, sa = np.cos(phase), np.sin(phase)
    r = np.stack([ca, sa], axis=1).reshape(2, 8, 32, 128)
    eye = np.eye(4)
    fwd = np.einsum("xshn,cd->xschdn", r, eye).reshape(2, 1024, 512)
    first = np.stack([ca, -sa], axis=1)
    second = np.stack([-sa, -ca], axis=1)
    inv = np.stack([first, second], axis=1).reshape(2, 8, 32, 2, 128)
    inv = np.einsum("xshqn,cd->xcnsqdh", inv, eye).reshape(2, 512, 2048)
    perm = np.einsum("ad,be,cf->abcfed", np.eye(4), np.eye(16), np.eye(8)).reshape(512, 512)
    return [np.asarray(t, np.float32).astype(ml_dtypes.bfloat16) for t in (col, fwd, inv, perm)]


def derivative(z):
    a = jnp.abs(z)
    e = jnp.exp(z * z * -0.5)
    d = 1.0 + (0.3275911 / math.sqrt(2.0)) * a
    t = pl.reciprocal(d, approx=True)
    t = t * (2.0 - d * t)
    poly = 1.061405429 * 0.5
    for c in (-1.453152027, 1.421413741, -0.284496736, 0.254829592):
        poly = poly * t + 0.5 * c
    q = e * (poly * t - a * (1.0 / math.sqrt(TWO_PI)))
    return jnp.where(z >= 0.0, 1.0 - q, q)


PEERS = ((2, 0), (2, 1), (1, 0), (3, 0), (1, 1), (3, 1), (0, 1))


def kernel(
    dps,
    clips, cot, weight, pw, bias, col_h, fwd_h, inv_h, perm_h,
    side, last, sgrad,
    xv, cv, wv, col, fwd, inv, perm,
    send, recv, relay, zs, dz, xp, xr, ya,
    xbf, xb, xbr, gbf, gb, gbr, dd, y3, kf, kb, bcol,
    in_sem, clip_sem, a2a_send, a2a_recv, relay_send, relay_recv, x_send, x_recv, dp_send, dp_recv, out_sem,
):
    pen = lax.axis_index("pencil")
    dpi = lax.axis_index("dp")
    half = pen // GROUP
    me = pen % GROUP
    other = 1 - half
    partner = other * GROUP + me
    per = 512 // dps
    kper = 64 // dps

    def clip_piece(b, n):
        at = pl.ds(n * 8, 8)
        return pltpu.make_async_copy(clips.at[b, at], xv.at[b, at], clip_sem.at[b, n])

    def load(src, dst, pieces, i):
        size = dst.shape[0] // pieces
        for n in range(pieces):
            at = pl.ds(n * size, size)
            pltpu.make_async_copy(src.at[at], dst.at[at], in_sem.at[i]).start()
        return pltpu.make_async_copy(dst, dst, in_sem.at[i]).wait

    col_wait = load(col_h, col, 1, 0)
    for b in range(2):
        for n in range(8):
            clip_piece(b, n).start()

    def peer_of(dy, dc):
        return (me // 2 + dy) % 4 * 2 + (me % 2 + dc) % 2

    barrier = pltpu.get_barrier_semaphore()
    for dy, dc in PEERS:
        peer = half * GROUP + peer_of(dy, dc)
        pl.semaphore_signal(barrier, inc=1, device_id={"pencil": peer}, device_id_type=MESH)
    pl.semaphore_signal(barrier, inc=1, device_id={"pencil": partner}, device_id_type=MESH)

    def greet_dp(r, carry):
        pl.semaphore_signal(barrier, inc=1, device_id={"dp": (dpi + r) % dps}, device_id_type=MESH)
        return carry

    if dps > 1:
        lax.fori_loop(1, dps, greet_dp, 0)

    lane = lax.broadcasted_iota(jnp.int32, (1, 128), 1)
    low = lane < 64
    sign = jnp.where(low, 1.0, -1.0).astype(F32)

    def slots(b, phase):
        return recv.at[phase, b] if phase < 3 else last.at[b]

    def columns(values, b, phase):
        def step(n, carry):
            if values is xv:
                clip_piece(b, n).wait()
            rows = values[b, pl.ds(pl.multiple_of(n * 8, 8), 8)].reshape(256, 512)
            part = dot(col[...], rows, NT)
            for i in range(2):
                piece = part[:, i * 128 : (i + 1) * 128].reshape(8, 16, 128).astype(BF)
                at = pl.multiple_of((2 * n + i) * 16, 16)
                send[phase, b, :, pl.ds(at, 16), :] = piece
            return carry

        lax.fori_loop(0, 8, step, 0, unroll=2)

    def send_one(b, phase, dy, dc):
        to = peer_of(dy, dc)
        if dy == 2:
            dst, via = relay.at[phase, b, dc], peer_of((1, 3)[dc], 0)
            sems = relay_send.at[phase, b], relay_recv.at[phase, b, dc]
        else:
            dst, via = slots(b, phase).at[me], to
            sems = a2a_send.at[phase, b], a2a_recv.at[phase, b]
        pltpu.make_async_remote_copy(
            src_ref=send.at[phase, b, to],
            dst_ref=dst,
            send_sem=sems[0],
            recv_sem=sems[1],
            device_id={"pencil": half * GROUP + via},
            device_id_type=MESH,
        ).start()

    def forward(b, phase):
        for dc in range(2):
            ref = relay.at[phase, b, dc]
            pltpu.make_async_copy(ref, ref, relay_recv.at[phase, b, dc]).wait()
            pltpu.make_async_remote_copy(
                src_ref=ref,
                dst_ref=slots(b, phase).at[peer_of((3, 1)[dc], 0)],
                send_sem=a2a_send.at[phase, b],
                recv_sem=a2a_recv.at[phase, b],
                device_id={"pencil": half * GROUP + peer_of((1, 3)[dc], dc)},
                device_id_type=MESH,
            ).start()

    def keep_own(b, phase):
        pltpu.make_async_copy(
            send.at[phase, b, me], slots(b, phase).at[me], a2a_recv.at[phase, b]
        ).start()

    def scatter(b, phase):
        for dy, dc in PEERS:
            send_one(b, phase, dy, dc)
        keep_own(b, phase)

    def arrived(b, phase):
        whole = slots(b, phase)
        pltpu.make_async_copy(whole, whole, a2a_recv.at[phase, b]).wait()

    def rows_forward(b, phase, which):
        arrived(b, phase)
        lhs = jnp.concatenate([recv[phase, b, s] for s in range(GROUP)], axis=1)
        pieces = []
        for c4 in range(4):
            part = dot(lhs, fwd[:, c4 * 128 : (c4 + 1) * 128]).reshape(16, 2, 8, 128)
            cosine = part[:, 0].reshape(128, 128)
            sine = part[:, 1].reshape(128, 128)
            pieces.append((cosine * sign - pltpu.roll(sine, 64, 1)).astype(BF))
        spec = dot(jnp.concatenate(pieces, axis=0), perm[...], TN).astype(BF)
        xp[which, b, 0] = spec[:, :256]
        xp[which, b, 1] = spec[:, 256:]
        pltpu.make_async_remote_copy(
            src_ref=xp.at[which, b, other],
            dst_ref=xr.at[which, b],
            send_sem=x_send.at[which, b],
            recv_sem=x_recv.at[which, b],
            device_id={"pencil": partner},
            device_id_type=MESH,
        ).start()

    def x_wait(which, b, ref):
        pltpu.make_async_copy(ref, ref, x_recv.at[which, b]).wait()

    def spectrum(which, b):
        x_wait(which, b, xr.at[which, b])
        return xp[which, b, half].astype(F32) + xr[which, b].astype(F32)

    def to_owner(src, dst, i, b):
        def rows_of(d):
            return src.at[b, pl.ds(pl.multiple_of(d * per, per), per)]

        def step(r, carry):
            to = (dpi + r) % dps
            pltpu.make_async_remote_copy(
                src_ref=rows_of(to),
                dst_ref=dst.at[b, dpi],
                send_sem=dp_send.at[i, b],
                recv_sem=dp_recv.at[i, b],
                device_id={"dp": to},
                device_id_type=MESH,
            ).start()
            return carry

        if dps > 1:
            lax.fori_loop(1, dps, step, 0)
        pltpu.make_async_copy(rows_of(dpi), dst.at[b, dpi], dp_recv.at[i, b]).start()

    def give_partner(i, b):
        pltpu.make_async_remote_copy(
            src_ref=ya.at[i, b, half],
            dst_ref=ya.at[i, b, half],
            send_sem=x_send.at[2 + i, b],
            recv_sem=x_recv.at[2 + i, b],
            device_id={"pencil": partner},
            device_id_type=MESH,
        ).start()

    def rows_back(i, b, phase):
        x_wait(2 + i, b, ya.at[i, b, other])
        turned = dot(perm[:, :256], ya[i, b, 0], NT) + dot(perm[:, 256:], ya[i, b, 1], NT)
        turned = turned.astype(BF)
        lhs = jnp.concatenate([turned[c * 128 : (c + 1) * 128] for c in range(4)], axis=1)
        for dy, dc in PEERS + ((0, 0),):
            to = peer_of(dy, dc)
            lines = dot(lhs, inv[:, pl.ds(pl.multiple_of(to * 256, 256), 256)])
            both = jnp.concatenate(
                [lines[:, :128].reshape(16, 8, 128), lines[:, 128:].reshape(16, 8, 128)], axis=1
            )
            send[phase, b, to] = both.reshape(256, 128).astype(BF)
            if (dy, dc) == (0, 0):
                keep_own(b, phase)
            else:
                send_one(b, phase, dy, dc)

    def mix_points(values, b, matrix, add, tiles=(0, 2)):
        def step(t, carry):
            at = pl.multiple_of(t * 16, 16)
            for n in range(2):
                lanes = slice(n * 256, (n + 1) * 256)
                tile = values[b, :, pl.ds(at, 16), lanes].astype(F32)
                parts = []
                for i in range(2):
                    rows = tile[:, i * 8 : (i + 1) * 8].reshape(512, 256).astype(BF)
                    got = dot(matrix[...], rows)
                    if add is not None:
                        got = got + jnp.concatenate([add[...]] * 2, axis=1)
                        to = pl.multiple_of(t * 16 + i * 8, 8)
                        zs[b, :, pl.ds(to, 8), lanes] = got.reshape(64, 8, 256)
                    parts.append(got.reshape(64, 8, 256))
                if add is None:
                    xv[b, :, pl.ds(at, 16), lanes] = jnp.concatenate(parts, axis=1).astype(BF)
            return carry

        lax.fori_loop(*tiles, step, 0)

    row16 = lax.broadcasted_iota(jnp.int32, (16, 128), 0)
    scale = jnp.where(pen == 0, 1.0, 2.0).astype(F32) / 262144.0
    scale_lane = jnp.where(jnp.logical_and(low, pen == 0), 1.0, 2.0).astype(F32) / 262144.0

    def mix_modes(b):
        spec = spectrum(0, b)
        for ri in range(2):
            for j in range(4):
                for p in range(2):
                    if p == j // 2:
                        part = spec[ri * 64 : (ri + 1) * 64, p * 128 : (p + 1) * 128]
                        part = jnp.where(low if j % 2 == 0 else jnp.logical_not(low), part, 0.0)
                    else:
                        part = jnp.zeros((64, 128), F32)
                    xbf[p, pl.ds(ri * 4 + j, 64, stride=8), :] = part
        for p in range(2):
            xb[b, :, p * 128 : (p + 1) * 128] = xbf[p].astype(BF)
        to_owner(xb, xbr, 0, b)

        def step(n, carry):
            for i in range(8):
                pair = n * 8 + i
                at = pl.multiple_of(pair * 16, 16)
                both = jnp.concatenate(
                    [wv[2 * pair].reshape(256, 128), wv[2 * pair + 1].reshape(256, 128)], axis=1
                )
                got = dot(xb[b, pl.ds(at, 16), :], both)
                y3[pl.ds(at, 8), :] = got[:8, :128]
                y3[pl.ds(at + 8, 8), :] = got[8:, 128:]
            return carry

        lax.fori_loop(0, 4, step, 0)
        modes = []
        for j in range(4):
            real = y3[pl.ds(j, 64, stride=8), :]
            imag = y3[pl.ds(4 + j, 64, stride=8), :]
            mixed = real - sign * pltpu.roll(imag, 64, 1)
            modes.append(mixed * (scale if j == 0 else 2.0 / 262144.0))
        for p in range(2):
            first, second = modes[2 * p], modes[2 * p + 1]
            real = jnp.where(low, first, pltpu.roll(second, 64, 1))
            imag = jnp.where(low, pltpu.roll(first, 64, 1), second)
            ya[0, b, half, 0:64, p * 128 : (p + 1) * 128] = real.astype(BF)
            ya[0, b, half, 64:128, p * 128 : (p + 1) * 128] = imag.astype(BF)
        give_partner(0, b)

    def grad_modes(b):
        spec = spectrum(1, b)
        for p in range(2):
            part = spec[:, p * 128 : (p + 1) * 128]
            part = part * (scale_lane if p == 0 else 2.0 / 262144.0)
            real, imag = part[:64], part[64:]
            real_r, imag_r = pltpu.roll(real, 64, 1), pltpu.roll(imag, 64, 1)
            for i, (re, im) in enumerate(
                ((jnp.where(low, real, imag_r), jnp.where(low, imag, real_r)),
                 (jnp.where(low, real_r, imag), jnp.where(low, imag_r, real)))
            ):
                gbf[pl.ds(2 * p + i, 64, stride=8), :] = re
                gbf[pl.ds(4 + 2 * p + i, 64, stride=8), :] = im * sign
        gb[b] = gbf[...].astype(BF)
        to_owner(gb, gbr, 1, b)

        def step(n, carry):
            for i in range(8):
                pair = n * 8 + i
                at = pl.multiple_of(pair * 16, 16)
                got = dot(gb[b, pl.ds(at, 16), :], wv[pl.ds(2 * pair, 2)].reshape(512, 128), NT)
                for p in range(2):
                    dd[p, pl.ds(at, 8), :] = got[:8, p * 128 : (p + 1) * 128]
                    dd[p, pl.ds(at + 8, 8), :] = got[8:, 256 + p * 128 : 384 + p * 128]
            return carry

        lax.fori_loop(0, 4, step, 0)
        for p in range(2):
            for ri in range(2):
                first = dd[p, pl.ds(ri * 4 + 2 * p, 64, stride=8), :]
                second = dd[p, pl.ds(ri * 4 + 2 * p + 1, 64, stride=8), :]
                ya[1, b, half, ri * 64 : (ri + 1) * 64, p * 128 : (p + 1) * 128] = jnp.where(
                    low, first, second
                ).astype(BF)
        give_partner(1, b)

    def activation(b, chunks):
        def step(n, carry):
            at = pl.ds(pl.multiple_of(n * 4, 4), 4)
            lines = recv[1, b, :, pl.ds(pl.multiple_of(n * 16, 16), 16), :].reshape(128, 128)
            z = dot(lines, col[...], TN) + zs[b, at].reshape(128, 512)
            grad = cv[b, at].reshape(128, 512).astype(F32) * derivative(z)
            dz[b, at] = grad.astype(BF).reshape(4, 32, 512)
            return carry

        lax.fori_loop(*chunks, step, 0, unroll=4)

    def bypass(b, between=None):
        mix_points(dz, b, kb, None, (0, 1))
        if between is not None:
            between()
        mix_points(dz, b, kb, None, (1, 2))
        pltpu.make_async_copy(xv.at[b], side.at[b], out_sem.at[b]).start()

    def weight_grad(b):
        for i, ref in enumerate((xbr, gbr)):
            pltpu.make_async_copy(ref.at[b], ref.at[b], dp_recv.at[i, b]).wait()
        first_rows = jnp.where(row16 < 8, 1.0, 0.0).astype(F32)
        for pair in range(kper // 2):
            at = slice(pair * 16, (pair + 1) * 16)
            left = xbr[b, :, at, :].reshape(dps * 16, 256)
            right = gbr[b, :, at, :].astype(F32)
            head = (right * first_rows).astype(BF).reshape(dps * 16, 128)
            tail = (right * (1.0 - first_rows)).astype(BF).reshape(dps * 16, 128)
            got = dot(left, jnp.concatenate([head, tail], axis=1), TN)
            for i in range(2):
                part = got[:, i * 128 : (i + 1) * 128].reshape(4, 64, 128)
                sgrad[2 * pair + i] = part if b == 0 else sgrad[2 * pair + i] + part

    col_wait()
    columns(xv, 0, 0)
    pl.semaphore_wait(barrier, GROUP - 1 + 1 + dps - 1)
    scatter(0, 0)
    fwd_wait = load(fwd_h.at[half], fwd, 4, 1)
    perm_wait = load(perm_h, perm, 2, 2)
    columns(xv, 1, 0)
    forward(0, 0)
    scatter(1, 0)
    weight_wait = load(weight, wv, 16, 3)
    inv_wait = load(inv_h.at[half], inv, 4, 4)
    cot_waits = [load(cot.at[b], cv.at[b], 8, 5 + b) for b in range(2)]

    row = lax.broadcasted_iota(jnp.int32, (512, 64), 0)
    lanes64 = lax.broadcasted_iota(jnp.int32, (512, 64), 1)
    spread = jnp.where(row // 8 == lanes64, 1.0, 0.0).astype(BF)
    same = (
        lax.broadcasted_iota(jnp.int32, (512, 512), 0) % 8
        == lax.broadcasted_iota(jnp.int32, (512, 512), 1) % 8
    )
    kf[...] = jnp.where(same, dot(dot(spread, pw[...], NT).astype(BF), spread, NT), 0.0).astype(BF)
    kb[...] = jnp.where(same, dot(dot(spread, pw[...]).astype(BF), spread, NT), 0.0).astype(BF)
    biased = (spread.astype(F32) * bias[...].astype(F32)).astype(BF)
    bcol[...] = dot(biased, jnp.ones((64, 128), BF))
    forward(1, 0)
    mix_points(xv, 0, kf, bcol)

    fwd_wait()
    perm_wait()
    rows_forward(0, 0, 0)
    mix_points(xv, 1, kf, bcol)
    rows_forward(1, 0, 0)
    weight_wait()
    mix_modes(0)
    mix_modes(1)
    inv_wait()
    rows_back(0, 0, 1)
    rows_back(0, 1, 1)
    forward(0, 1)
    forward(1, 1)

    arrived(0, 1)
    cot_waits[0]()
    activation(0, (0, 16))
    columns(dz, 0, 2)
    scatter(0, 2)
    arrived(1, 1)
    cot_waits[1]()
    activation(1, (0, 4))
    forward(0, 2)
    activation(1, (4, 16))
    columns(dz, 1, 2)
    scatter(1, 2)
    bypass(0, lambda: forward(1, 2))
    rows_forward(0, 2, 1)
    bypass(1)
    rows_forward(1, 2, 1)
    grad_modes(0)
    grad_modes(1)
    rows_back(1, 0, 3)
    weight_grad(0)
    forward(0, 3)
    rows_back(1, 1, 3)
    weight_grad(1)
    forward(1, 3)

    for phase in range(4):
        for b in range(2):
            sent = send.at[phase, b, pl.ds(0, GROUP - 1)]
            pltpu.make_async_copy(sent, sent, a2a_send.at[phase, b]).wait()
            sent = relay.at[phase, b]
            pltpu.make_async_copy(sent, sent, relay_send.at[phase, b]).wait()
            ref = xr.at[0, b]
            pltpu.make_async_copy(ref, ref, x_send.at[phase, b]).wait()
    if dps > 1:
        for i, ref in enumerate((xb, gb)):
            for b in range(2):
                sent = ref.at[b, pl.ds(0, 512 - per)]
                pltpu.make_async_copy(sent, sent, dp_send.at[i, b]).wait()
    for b in range(2):
        pltpu.make_async_copy(xv.at[b], side.at[b], out_sem.at[b]).wait()
        arrived(b, 3)


def finish(side, lines, col_h, sgrad, out, weights_out, sv, lv, col, gv, side_sem, sem):
    def piece(b, n):
        at = pl.ds(n * 8, 8)
        return pltpu.make_async_copy(side.at[b, at], sv.at[b, at], side_sem.at[b, n])

    pltpu.make_async_copy(col_h, col, sem.at[0]).start()
    for b in range(2):
        for s in range(GROUP):
            pltpu.make_async_copy(lines.at[b, s], lv.at[b, s], sem.at[1 + b]).start()
        for n in range(8):
            piece(b, n).start()
    pltpu.make_async_copy(sgrad, gv, sem.at[3]).start()
    pltpu.make_async_copy(col, col, sem.at[0]).wait()
    for b in range(2):
        pltpu.make_async_copy(lv.at[b], lv.at[b], sem.at[1 + b]).wait()

        def step(n, carry, b=b):
            piece(b, n).wait()
            for i in range(2):
                at = pl.ds(pl.multiple_of(n * 8 + i * 4, 4), 4)
                rows = pl.ds(pl.multiple_of((2 * n + i) * 16, 16), 16)
                part = lv[b, :, rows, :].reshape(128, 128)
                got = dot(part, col[...], TN) + sv[b, at].reshape(128, 512).astype(F32)
                sv[b, at] = got.astype(BF).reshape(4, 32, 512)
            at = pl.ds(n * 8, 8)
            pltpu.make_async_copy(sv.at[b, at], out.at[b, at], sem.at[4 + b]).start()
            return carry

        lax.fori_loop(0, 8, step, 0, unroll=2)
    pltpu.make_async_copy(gv, gv, sem.at[3]).wait()
    away = pltpu.make_async_copy(gv, weights_out, sem.at[6])
    away.start()
    for b in range(2):
        pltpu.make_async_copy(sv.at[b], sv.at[b], sem.at[4 + b]).wait()
    away.wait()


def shards(dps, clips, cotangent, spectral_weight, point_weight, bias):
    col, fwd, inv, perm = [jnp.asarray(t) for t in tables()]
    any_spec = pl.BlockSpec(memory_space=pl.ANY)
    vmem = pl.BlockSpec(memory_space=pltpu.VMEM)
    per = 512 // dps
    dma = pltpu.SemaphoreType.DMA
    grad_shape = jax.ShapeDtypeStruct((64 // dps, 4, 64, 128), F32)
    side, last, sgrad = pl.pallas_call(
        functools.partial(kernel, dps),
        out_shape=(
            jax.ShapeDtypeStruct((2, 64, 32, 512), BF),
            jax.ShapeDtypeStruct((2, GROUP, 256, 128), BF),
            grad_shape,
        ),
        in_specs=[any_spec] * 3 + [vmem] * 2 + [any_spec] * 4,
        out_specs=(any_spec, any_spec, vmem),
        scratch_shapes=[
            pltpu.VMEM((2, 64, 32, 512), BF),
            pltpu.VMEM((2, 64, 32, 512), BF),
            pltpu.VMEM((64, 4, 64, 128), BF),
            pltpu.VMEM((128, 512), BF),
            pltpu.VMEM((1024, 512), BF),
            pltpu.VMEM((512, 2048), BF),
            pltpu.VMEM((512, 512), BF),
            pltpu.VMEM((4, 2, GROUP, 256, 128), BF),
            pltpu.VMEM((3, 2, GROUP, 256, 128), BF),
            pltpu.VMEM((4, 2, 2, 256, 128), BF),
            pltpu.VMEM((2, 64, 32, 512), F32),
            pltpu.VMEM((2, 64, 32, 512), BF),
            pltpu.VMEM((2, 2, 2, 128, 256), BF),
            pltpu.VMEM((2, 2, 128, 256), BF),
            pltpu.VMEM((2, 2, 2, 128, 256), BF),
            pltpu.VMEM((2, 512, 128), F32),
            pltpu.VMEM((2, 512, 256), BF),
            pltpu.VMEM((2, dps, per, 256), BF),
            pltpu.VMEM((512, 128), F32),
            pltpu.VMEM((2, 512, 128), BF),
            pltpu.VMEM((2, dps, per, 128), BF),
            pltpu.VMEM((2, 512, 128), F32),
            pltpu.VMEM((512, 128), F32),
            pltpu.VMEM((512, 512), BF),
            pltpu.VMEM((512, 512), BF),
            pltpu.VMEM((512, 128), F32),
            dma((7,)),
            dma((2, 8)),
            dma((4, 2)),
            dma((4, 2)),
            dma((4, 2)),
            dma((4, 2, 2)),
            dma((4, 2)),
            dma((4, 2)),
            dma((2, 2)),
            dma((2, 2)),
            dma((2,)),
        ],
        compiler_params=pltpu.CompilerParams(
            collective_id=0, has_side_effects=True, vmem_limit_bytes=60 * 1024 * 1024
        ),
        cost_estimate=pl.CostEstimate(
            flops=20_000_000_000, bytes_accessed=20_000_000, transcendentals=4_000_000
        ),
    )(clips, cotangent, spectral_weight, point_weight, bias.reshape(1, 64), col, fwd, inv, perm)
    return pl.pallas_call(
        finish,
        out_shape=(jax.ShapeDtypeStruct((2, 64, 32, 512), BF), grad_shape),
        in_specs=[any_spec] * 4,
        out_specs=(any_spec, any_spec),
        scratch_shapes=[
            pltpu.VMEM((2, 64, 32, 512), BF),
            pltpu.VMEM((2, GROUP, 256, 128), BF),
            pltpu.VMEM((128, 512), BF),
            pltpu.VMEM(grad_shape.shape, F32),
            dma((2, 8)),
            dma((7,)),
        ],
        compiler_params=pltpu.CompilerParams(vmem_limit_bytes=60 * 1024 * 1024),
        cost_estimate=pl.CostEstimate(
            flops=600_000_000, bytes_accessed=10_000_000, transcendentals=0
        ),
    )(side, last, col, sgrad)


def solution(mesh):
    in_specs = (
        P("dp", None, "pencil", None),
        P("dp", None, "pencil", None),
        P(None, "pencil", None, None),
        P(),
        P(),
    )
    out_specs = (P("dp", None, "pencil", None), P("dp", "pencil", None, None))
    return jax.shard_map(
        functools.partial(shards, mesh.shape["dp"]),
        mesh=mesh,
        in_specs=in_specs,
        out_specs=out_specs,
        check_vma=False,
    )
```

```python
import functools
import math

import jax
import jax.numpy as jnp
import ml_dtypes
import numpy as np
from jax import lax
from jax.experimental import pallas as pl
from jax.experimental.pallas import tpu as pltpu
from jax.sharding import PartitionSpec as P

TWO_PI = 2.0 * math.pi
MESH = pl.DeviceIdType.MESH
BF = jnp.bfloat16
F32 = jnp.float32
GROUP = 8
TN = (((0,), (0,)), ((), ()))
NT = (((1,), (1,)), ((), ()))
NN = (((1,), (0,)), ((), ()))


def dot(a, b, dims=NN):
    return lax.dot_general(a, b, dims, preferred_element_type=F32)


def tables():
    w = np.arange(512)
    g, half, j4 = np.meshgrid(np.arange(8), np.arange(2), np.arange(4), indexing="ij")
    j = ((half * 8 + g) * 4 + j4).reshape(8, 8)
    phase = (j[:, :, None] * w % 512) * (TWO_PI / 512)
    col = np.stack([np.cos(phase), np.sin(phase)], axis=1).reshape(128, 512)
    k = np.arange(64)
    f = np.where(k < 32, k, 448 + k)
    h = np.arange(512)
    phase = (h[:, None] * f[None, :] % 512) * (TWO_PI / 512)
    ca, sa = np.cos(phase), np.sin(phase)
    r = np.stack([ca, sa], axis=1).reshape(2, 8, 32, 128)
    eye = np.eye(4)
    fwd = np.einsum("xshn,cd->xschdn", r, eye).reshape(2, 1024, 512)
    first = np.stack([ca, -sa], axis=1)
    second = np.stack([-sa, -ca], axis=1)
    inv = np.stack([first, second], axis=1).reshape(2, 8, 32, 2, 128)
    inv = np.einsum("xshqn,cd->xcnsqdh", inv, eye).reshape(2, 512, 2048)
    perm = np.einsum("ad,be,cf->abcfed", np.eye(4), np.eye(16), np.eye(8)).reshape(512, 512)
    return [np.asarray(t, np.float32).astype(ml_dtypes.bfloat16) for t in (col, fwd, inv, perm)]


def derivative(z):
    a = jnp.abs(z)
    e = jnp.exp(z * z * -0.5)
    d = 1.0 + (0.3275911 / math.sqrt(2.0)) * a
    t = pl.reciprocal(d, approx=True)
    t = t * (2.0 - d * t)
    poly = 1.061405429 * 0.5
    for c in (-1.453152027, 1.421413741, -0.284496736, 0.254829592):
        poly = poly * t + 0.5 * c
    q = e * (poly * t - a * (1.0 / math.sqrt(TWO_PI)))
    return jnp.where(z >= 0.0, 1.0 - q, q)


PEERS = ((2, 0), (2, 1), (1, 0), (3, 0), (1, 1), (3, 1), (0, 1))


def kernel(
    dps,
    clips, cot, weight, pw, bias, col_h, fwd_h, inv_h, perm_h,
    side, last, sgrad,
    xv, cv, wv, col, fwd, inv, perm,
    send, recv, zs, dz, xp, xr, ya,
    xbf, xb, xbr, gbf, gb, gbr, dd, y3, kf, kb, bcol,
    in_sem, clip_sem, a2a_send, a2a_recv, x_send, x_recv, dp_send, dp_recv, out_sem,
):
    pen = lax.axis_index("pencil")
    dpi = lax.axis_index("dp")
    half = pen // GROUP
    me = pen % GROUP
    other = 1 - half
    partner = other * GROUP + me
    per = 512 // dps
    kper = 64 // dps

    def clip_piece(b, n):
        at = pl.ds(n * 8, 8)
        return pltpu.make_async_copy(clips.at[b, at], xv.at[b, at], clip_sem.at[b, n])

    def load(src, dst, pieces, i):
        size = dst.shape[0] // pieces
        for n in range(pieces):
            at = pl.ds(n * size, size)
            pltpu.make_async_copy(src.at[at], dst.at[at], in_sem.at[i]).start()
        return pltpu.make_async_copy(dst, dst, in_sem.at[i]).wait

    col_wait = load(col_h, col, 1, 0)
    for b in range(2):
        for n in range(8):
            clip_piece(b, n).start()

    def peer_of(dy, dc):
        return (me // 2 + dy) % 4 * 2 + (me % 2 + dc) % 2

    barrier = pltpu.get_barrier_semaphore()
    for dy, dc in PEERS:
        peer = half * GROUP + peer_of(dy, dc)
        pl.semaphore_signal(barrier, inc=1, device_id={"pencil": peer}, device_id_type=MESH)
    pl.semaphore_signal(barrier, inc=1, device_id={"pencil": partner}, device_id_type=MESH)

    def greet_dp(r, carry):
        pl.semaphore_signal(barrier, inc=1, device_id={"dp": (dpi + r) % dps}, device_id_type=MESH)
        return carry

    if dps > 1:
        lax.fori_loop(1, dps, greet_dp, 0)

    lane = lax.broadcasted_iota(jnp.int32, (1, 128), 1)
    low = lane < 64
    sign = jnp.where(low, 1.0, -1.0).astype(F32)

    def slots(b, phase):
        return last if (phase, b) == (3, 1) else recv.at[phase, b]

    def columns(values, b, phase):
        def step(n, carry):
            if values is xv:
                clip_piece(b, n).wait()
            rows = values[b, pl.ds(pl.multiple_of(n * 8, 8), 8)].reshape(256, 512)
            part = dot(col[...], rows, NT)
            for i in range(2):
                piece = part[:, i * 128 : (i + 1) * 128].reshape(8, 16, 128).astype(BF)
                at = pl.multiple_of((2 * n + i) * 16, 16)
                send[phase, b, :, pl.ds(at, 16), :] = piece
            return carry

        lax.fori_loop(0, 8, step, 0, unroll=2)

    def send_one(b, phase, to):
        pltpu.make_async_remote_copy(
            src_ref=send.at[phase, b, to],
            dst_ref=slots(b, phase).at[me],
            send_sem=a2a_send.at[phase, b],
            recv_sem=a2a_recv.at[phase, b],
            device_id={"pencil": half * GROUP + to},
            device_id_type=MESH,
        ).start()

    def keep_own(b, phase):
        pltpu.make_async_copy(
            send.at[phase, b, me], slots(b, phase).at[me], a2a_recv.at[phase, b]
        ).start()

    def scatter(b, phase):
        for dy, dc in PEERS:
            send_one(b, phase, peer_of(dy, dc))
        keep_own(b, phase)

    def arrived(b, phase):
        whole = slots(b, phase)
        pltpu.make_async_copy(whole, whole, a2a_recv.at[phase, b]).wait()

    def rows_forward(b, phase, which):
        arrived(b, phase)
        lhs = jnp.concatenate([recv[phase, b, s] for s in range(GROUP)], axis=1)
        pieces = []
        for n in range(2):
            wide = dot(lhs, fwd[:, n * 256 : (n + 1) * 256])
            for i in range(2):
                part = wide[:, i * 128 : (i + 1) * 128].reshape(16, 2, 8, 128)
                cosine = part[:, 0].reshape(128, 128)
                sine = part[:, 1].reshape(128, 128)
                pieces.append((cosine * sign - pltpu.roll(sine, 64, 1)).astype(BF))
        spec = dot(jnp.concatenate(pieces, axis=0), perm[...], TN).astype(BF)
        xp[which, b, 0] = spec[:, :256]
        xp[which, b, 1] = spec[:, 256:]
        pltpu.make_async_remote_copy(
            src_ref=xp.at[which, b, other],
            dst_ref=xr.at[which, b],
            send_sem=x_send.at[which, b],
            recv_sem=x_recv.at[which, b],
            device_id={"pencil": partner},
            device_id_type=MESH,
        ).start()

    def x_wait(which, b, ref):
        pltpu.make_async_copy(ref, ref, x_recv.at[which, b]).wait()

    def spectrum(which, b):
        x_wait(which, b, xr.at[which, b])
        return xp[which, b, half].astype(F32) + xr[which, b].astype(F32)

    def to_owner(src, dst, i):
        def step(r, carry):
            to = (dpi + r) % dps
            pltpu.make_async_remote_copy(
                src_ref=src.at[to],
                dst_ref=dst.at[dpi],
                send_sem=dp_send.at[i],
                recv_sem=dp_recv.at[i],
                device_id={"dp": to},
                device_id_type=MESH,
            ).start()
            return carry

        if dps > 1:
            lax.fori_loop(1, dps, step, 0)
        pltpu.make_async_copy(src.at[dpi], dst.at[dpi], dp_recv.at[i]).start()

    def give_partner(i, b):
        pltpu.make_async_remote_copy(
            src_ref=ya.at[i, b, half],
            dst_ref=ya.at[i, b, half],
            send_sem=x_send.at[2 + i, b],
            recv_sem=x_recv.at[2 + i, b],
            device_id={"pencil": partner},
            device_id_type=MESH,
        ).start()

    def rows_back(i, b, phase):
        x_wait(2 + i, b, ya.at[i, b, other])
        turned = dot(perm[:, :256], ya[i, b, 0], NT) + dot(perm[:, 256:], ya[i, b, 1], NT)
        turned = turned.astype(BF)
        lhs = jnp.concatenate([turned[c * 128 : (c + 1) * 128] for c in range(4)], axis=1)
        for dy, dc in PEERS + ((0, 0),):
            to = peer_of(dy, dc)
            lines = dot(lhs, inv[:, pl.ds(pl.multiple_of(to * 256, 256), 256)])
            both = jnp.concatenate(
                [lines[:, :128].reshape(16, 8, 128), lines[:, 128:].reshape(16, 8, 128)], axis=1
            )
            send[phase, b, to] = both.reshape(256, 128).astype(BF)
            if (dy, dc) == (0, 0):
                keep_own(b, phase)
            else:
                send_one(b, phase, to)

    def mix_points(values, b, matrix, add, tiles=(0, 2)):
        def step(t, carry):
            at = pl.multiple_of(t * 16, 16)
            for n in range(2):
                lanes = slice(n * 256, (n + 1) * 256)
                tile = values[b, :, pl.ds(at, 16), lanes].astype(F32)
                parts = []
                for i in range(2):
                    rows = tile[:, i * 8 : (i + 1) * 8].reshape(512, 256).astype(BF)
                    got = dot(matrix[...], rows)
                    if add is not None:
                        got = got + jnp.concatenate([add[...]] * 2, axis=1)
                        to = pl.multiple_of(t * 16 + i * 8, 8)
                        zs[b, :, pl.ds(to, 8), lanes] = got.reshape(64, 8, 256)
                    parts.append(got.reshape(64, 8, 256))
                if add is None:
                    xv[b, :, pl.ds(at, 16), lanes] = jnp.concatenate(parts, axis=1).astype(BF)
            return carry

        lax.fori_loop(*tiles, step, 0)

    row16 = lax.broadcasted_iota(jnp.int32, (16, 128), 0)
    scale = jnp.where(pen == 0, 1.0, 2.0).astype(F32) / 262144.0
    scale_lane = jnp.where(jnp.logical_and(low, pen == 0), 1.0, 2.0).astype(F32) / 262144.0

    pairs = kper // 2

    def own_rows(pair):
        return pl.ds(pl.multiple_of(pair % pairs * 16, 16), 16)

    def mix_modes(b):
        spec = spectrum(0, b)
        for ri in range(2):
            for j in range(4):
                for p in range(2):
                    if p != j // 2:
                        continue
                    part = spec[ri * 64 : (ri + 1) * 64, p * 128 : (p + 1) * 128]
                    part = jnp.where(low if j % 2 == 0 else jnp.logical_not(low), part, 0.0)
                    xbf[p, pl.ds(ri * 4 + j, 64, stride=8), :] = part
        for p in range(2):
            xb[:, b, :, p * 128 : (p + 1) * 128] = xbf[p].astype(BF).reshape(dps, per, 128)

        def step(n, carry):
            for i in range(8):
                pair = n * 8 + i
                at = pl.multiple_of(pair * 16, 16)
                both = jnp.concatenate(
                    [wv[2 * pair].reshape(256, 128), wv[2 * pair + 1].reshape(256, 128)], axis=1
                )
                got = dot(xb[pair // pairs, b, own_rows(pair), :], both)
                y3[pl.ds(at, 8), :] = got[:8, :128]
                y3[pl.ds(at + 8, 8), :] = got[8:, 128:]
            return carry

        lax.fori_loop(0, 4, step, 0)
        modes = []
        for j in range(4):
            real = y3[pl.ds(j, 64, stride=8), :]
            imag = y3[pl.ds(4 + j, 64, stride=8), :]
            mixed = real - sign * pltpu.roll(imag, 64, 1)
            modes.append(mixed * (scale if j == 0 else 2.0 / 262144.0))
        for p in range(2):
            first, second = modes[2 * p], modes[2 * p + 1]
            real = jnp.where(low, first, pltpu.roll(second, 64, 1))
            imag = jnp.where(low, pltpu.roll(first, 64, 1), second)
            ya[0, b, half, 0:64, p * 128 : (p + 1) * 128] = real.astype(BF)
            ya[0, b, half, 64:128, p * 128 : (p + 1) * 128] = imag.astype(BF)
        give_partner(0, b)

    def grad_modes(b):
        spec = spectrum(1, b)
        for p in range(2):
            part = spec[:, p * 128 : (p + 1) * 128]
            part = part * (scale_lane if p == 0 else 2.0 / 262144.0)
            real, imag = part[:64], part[64:]
            real_r, imag_r = pltpu.roll(real, 64, 1), pltpu.roll(imag, 64, 1)
            for i, (re, im) in enumerate(
                ((jnp.where(low, real, imag_r), jnp.where(low, imag, real_r)),
                 (jnp.where(low, real_r, imag), jnp.where(low, imag_r, real)))
            ):
                gbf[pl.ds(2 * p + i, 64, stride=8), :] = re
                gbf[pl.ds(4 + 2 * p + i, 64, stride=8), :] = im * sign
        gb[:, b] = gbf[...].astype(BF).reshape(dps, per, 128)

        def step(n, carry):
            for i in range(8):
                pair = n * 8 + i
                at = pl.multiple_of(pair * 16, 16)
                rhs = wv[pl.ds(2 * pair, 2)].reshape(512, 128)
                got = dot(gb[pair // pairs, b, own_rows(pair), :], rhs, NT)
                for p in range(2):
                    dd[p, pl.ds(at, 8), :] = got[:8, p * 128 : (p + 1) * 128]
                    dd[p, pl.ds(at + 8, 8), :] = got[8:, 256 + p * 128 : 384 + p * 128]
            return carry

        lax.fori_loop(0, 4, step, 0)
        for p in range(2):
            for ri in range(2):
                first = dd[p, pl.ds(ri * 4 + 2 * p, 64, stride=8), :]
                second = dd[p, pl.ds(ri * 4 + 2 * p + 1, 64, stride=8), :]
                ya[1, b, half, ri * 64 : (ri + 1) * 64, p * 128 : (p + 1) * 128] = jnp.where(
                    low, first, second
                ).astype(BF)
        give_partner(1, b)

    def activation(b, chunks):
        def step(n, carry):
            at = pl.ds(pl.multiple_of(n * 4, 4), 4)
            lines = recv[1, b, :, pl.ds(pl.multiple_of(n * 16, 16), 16), :].reshape(128, 128)
            z = dot(lines, col[...], TN) + zs[b, at].reshape(128, 512)
            grad = cv[b, at].reshape(128, 512).astype(F32) * derivative(z)
            dz[b, at] = grad.astype(BF).reshape(4, 32, 512)
            return carry

        lax.fori_loop(*chunks, step, 0, unroll=4)

    def leave(b):
        pltpu.make_async_copy(xv.at[b], side.at[b], out_sem.at[b]).start()

    def finish_first():
        arrived(0, 3)

        def step(n, carry):
            at = pl.ds(pl.multiple_of(n * 4, 4), 4)
            lines = recv[3, 0, :, pl.ds(pl.multiple_of(n * 16, 16), 16), :].reshape(128, 128)
            got = dot(lines, col[...], TN) + xv[0, at].reshape(128, 512).astype(F32)
            xv[0, at] = got.astype(BF).reshape(4, 32, 512)
            return carry

        lax.fori_loop(0, 16, step, 0, unroll=4)
        leave(0)

    def weight_grad():
        for i, ref in enumerate((xbr, gbr)):
            pltpu.make_async_copy(ref, ref, dp_recv.at[i]).wait()
        first_rows = jnp.where(row16 < 8, 1.0, 0.0).astype(F32)
        for pair in range(pairs):
            at = slice(pair * 16, (pair + 1) * 16)
            left = xbr[:, :, at, :].reshape(2 * dps * 16, 256)
            right = gbr[:, :, at, :].astype(F32)
            head = (right * first_rows).astype(BF).reshape(2 * dps * 16, 128)
            tail = (right * (1.0 - first_rows)).astype(BF).reshape(2 * dps * 16, 128)
            got = dot(left, jnp.concatenate([head, tail], axis=1), TN)
            for i in range(2):
                sgrad[2 * pair + i] = got[:, i * 128 : (i + 1) * 128].reshape(4, 64, 128)

    col_wait()
    columns(xv, 0, 0)
    pl.semaphore_wait(barrier, GROUP - 1 + 1 + dps - 1)
    scatter(0, 0)
    fwd_wait = load(fwd_h.at[half], fwd, 4, 1)
    perm_wait = load(perm_h, perm, 2, 2)
    columns(xv, 1, 0)
    scatter(1, 0)
    weight_wait = load(weight, wv, 16, 3)
    inv_wait = load(inv_h.at[half], inv, 4, 4)
    cot_waits = [load(cot.at[b], cv.at[b], 8, 5 + b) for b in range(2)]

    row = lax.broadcasted_iota(jnp.int32, (512, 64), 0)
    lanes64 = lax.broadcasted_iota(jnp.int32, (512, 64), 1)
    spread = jnp.where(row // 8 == lanes64, 1.0, 0.0).astype(BF)
    same = (
        lax.broadcasted_iota(jnp.int32, (512, 512), 0) % 8
        == lax.broadcasted_iota(jnp.int32, (512, 512), 1) % 8
    )
    for p in range(2):
        xbf[p] = jnp.zeros((512, 128), F32)
    kf[...] = jnp.where(same, dot(dot(spread, pw[...], NT).astype(BF), spread, NT), 0.0).astype(BF)
    kb[...] = jnp.where(same, dot(dot(spread, pw[...]).astype(BF), spread, NT), 0.0).astype(BF)
    biased = (spread.astype(F32) * bias[...].astype(F32)).astype(BF)
    bcol[...] = dot(biased, jnp.ones((64, 128), BF))
    mix_points(xv, 0, kf, bcol)

    fwd_wait()
    perm_wait()
    rows_forward(0, 0, 0)
    mix_points(xv, 1, kf, bcol)
    rows_forward(1, 0, 0)
    weight_wait()
    mix_modes(0)
    mix_modes(1)
    inv_wait()
    rows_back(0, 0, 1)
    to_owner(xb, xbr, 0)
    rows_back(0, 1, 1)

    for b in range(2):
        arrived(b, 1)
        cot_waits[b]()
        activation(b, (0, 16))
        columns(dz, b, 2)
        scatter(b, 2)
    rows_forward(0, 2, 1)
    mix_points(dz, 0, kb, None)
    mix_points(dz, 1, kb, None)
    leave(1)
    rows_forward(1, 2, 1)
    grad_modes(0)
    grad_modes(1)
    rows_back(1, 0, 3)
    to_owner(gb, gbr, 1)
    rows_back(1, 1, 3)
    finish_first()
    weight_grad()

    for phase in range(4):
        for b in range(2):
            sent = send.at[phase, b, pl.ds(0, GROUP - 1)]
            pltpu.make_async_copy(sent, sent, a2a_send.at[phase, b]).wait()
            ref = xr.at[0, b]
            pltpu.make_async_copy(ref, ref, x_send.at[phase, b]).wait()
    if dps > 1:
        for i, ref in enumerate((xb, gb)):
            sent = ref.at[pl.ds(0, dps - 1)]
            pltpu.make_async_copy(sent, sent, dp_send.at[i]).wait()
    for b in range(2):
        pltpu.make_async_copy(xv.at[b], side.at[b], out_sem.at[b]).wait()
    arrived(1, 3)


def finish(side, lines, col_h, sgrad, out, weights_out, sv, lv, col, gv, side_sem, sem):
    def piece(b, n):
        at = pl.ds(n * 8, 8)
        return pltpu.make_async_copy(side.at[b, at], sv.at[b, at], side_sem.at[b, n])

    def write(b, n):
        at = pl.ds(n * 8, 8)
        pltpu.make_async_copy(sv.at[b, at], out.at[b, at], sem.at[3 + b]).start()

    pltpu.make_async_copy(col_h, col, sem.at[0]).start()
    for s in range(GROUP):
        pltpu.make_async_copy(lines.at[s], lv.at[s], sem.at[1]).start()
    for b in (1, 0):
        for n in range(8):
            piece(b, n).start()
    pltpu.make_async_copy(sgrad, gv, sem.at[2]).start()
    pltpu.make_async_copy(col, col, sem.at[0]).wait()
    pltpu.make_async_copy(lv, lv, sem.at[1]).wait()

    def step(n, carry):
        piece(1, n).wait()
        for i in range(2):
            at = pl.ds(pl.multiple_of(n * 8 + i * 4, 4), 4)
            rows = pl.ds(pl.multiple_of((2 * n + i) * 16, 16), 16)
            part = lv[:, rows, :].reshape(128, 128)
            got = dot(part, col[...], TN) + sv[1, at].reshape(128, 512).astype(F32)
            sv[1, at] = got.astype(BF).reshape(4, 32, 512)
        write(1, n)
        piece(0, n).wait()
        write(0, n)
        return carry

    lax.fori_loop(0, 8, step, 0, unroll=2)
    pltpu.make_async_copy(gv, gv, sem.at[2]).wait()
    away = pltpu.make_async_copy(gv, weights_out, sem.at[5])
    away.start()
    for b in range(2):
        pltpu.make_async_copy(sv.at[b], sv.at[b], sem.at[3 + b]).wait()
    away.wait()


def shards(dps, clips, cotangent, spectral_weight, point_weight, bias):
    col, fwd, inv, perm = [jnp.asarray(t) for t in tables()]
    any_spec = pl.BlockSpec(memory_space=pl.ANY)
    vmem = pl.BlockSpec(memory_space=pltpu.VMEM)
    per = 512 // dps
    dma = pltpu.SemaphoreType.DMA
    grad_shape = jax.ShapeDtypeStruct((64 // dps, 4, 64, 128), F32)
    side, last, sgrad = pl.pallas_call(
        functools.partial(kernel, dps),
        out_shape=(
            jax.ShapeDtypeStruct((2, 64, 32, 512), BF),
            jax.ShapeDtypeStruct((GROUP, 256, 128), BF),
            grad_shape,
        ),
        in_specs=[any_spec] * 3 + [vmem] * 2 + [any_spec] * 4,
        out_specs=(any_spec, any_spec, vmem),
        scratch_shapes=[
            pltpu.VMEM((2, 64, 32, 512), BF),
            pltpu.VMEM((2, 64, 32, 512), BF),
            pltpu.VMEM((64, 4, 64, 128), BF),
            pltpu.VMEM((128, 512), BF),
            pltpu.VMEM((1024, 512), BF),
            pltpu.VMEM((512, 2048), BF),
            pltpu.VMEM((512, 512), BF),
            pltpu.VMEM((4, 2, GROUP, 256, 128), BF),
            pltpu.VMEM((4, 2, GROUP, 256, 128), BF),
            pltpu.VMEM((2, 64, 32, 512), F32),
            pltpu.VMEM((2, 64, 32, 512), BF),
            pltpu.VMEM((2, 2, 2, 128, 256), BF),
            pltpu.VMEM((2, 2, 128, 256), BF),
            pltpu.VMEM((2, 2, 2, 128, 256), BF),
            pltpu.VMEM((2, 512, 128), F32),
            pltpu.VMEM((dps, 2, per, 256), BF),
            pltpu.VMEM((dps, 2, per, 256), BF),
            pltpu.VMEM((512, 128), F32),
            pltpu.VMEM((dps, 2, per, 128), BF),
            pltpu.VMEM((dps, 2, per, 128), BF),
            pltpu.VMEM((2, 512, 128), F32),
            pltpu.VMEM((512, 128), F32),
            pltpu.VMEM((512, 512), BF),
            pltpu.VMEM((512, 512), BF),
            pltpu.VMEM((512, 128), F32),
            dma((7,)),
            dma((2, 8)),
            dma((4, 2)),
            dma((4, 2)),
            dma((4, 2)),
            dma((4, 2)),
            dma((2,)),
            dma((2,)),
            dma((2,)),
        ],
        compiler_params=pltpu.CompilerParams(
            collective_id=0, has_side_effects=True, vmem_limit_bytes=60 * 1024 * 1024
        ),
        cost_estimate=pl.CostEstimate(
            flops=20_000_000_000, bytes_accessed=20_000_000, transcendentals=4_000_000
        ),
    )(clips, cotangent, spectral_weight, point_weight, bias.reshape(1, 64), col, fwd, inv, perm)
    return pl.pallas_call(
        finish,
        out_shape=(jax.ShapeDtypeStruct((2, 64, 32, 512), BF), grad_shape),
        in_specs=[any_spec] * 4,
        out_specs=(any_spec, any_spec),
        scratch_shapes=[
            pltpu.VMEM((2, 64, 32, 512), BF),
            pltpu.VMEM((GROUP, 256, 128), BF),
            pltpu.VMEM((128, 512), BF),
            pltpu.VMEM(grad_shape.shape, F32),
            dma((2, 8)),
            dma((6,)),
        ],
        compiler_params=pltpu.CompilerParams(vmem_limit_bytes=60 * 1024 * 1024),
        cost_estimate=pl.CostEstimate(
            flops=600_000_000, bytes_accessed=10_000_000, transcendentals=0
        ),
    )(side, last, col, sgrad)


def solution(mesh):
    in_specs = (
        P("dp", None, "pencil", None),
        P("dp", None, "pencil", None),
        P(None, "pencil", None, None),
        P(),
        P(),
    )
    out_specs = (P("dp", None, "pencil", None), P("dp", "pencil", None, None))
    return jax.shard_map(
        functools.partial(shards, mesh.shape["dp"]),
        mesh=mesh,
        in_specs=in_specs,
        out_specs=out_specs,
        check_vma=False,
    )
```

```python
import functools
import math

import jax
import jax.numpy as jnp
import ml_dtypes
import numpy as np
from jax import lax
from jax.experimental import pallas as pl
from jax.experimental.pallas import tpu as pltpu
from jax.sharding import PartitionSpec as P

TWO_PI = 2.0 * math.pi
MESH = pl.DeviceIdType.MESH
BF = jnp.bfloat16
F32 = jnp.float32
GROUP = 16
TN = (((0,), (0,)), ((), ()))
NT = (((1,), (1,)), ((), ()))
NN = (((1,), (0,)), ((), ()))


def dot(a, b, dims=NN):
    return lax.dot_general(a, b, dims, preferred_element_type=F32)


def tables():
    w = np.arange(512)
    j = np.arange(64).reshape(16, 4)
    phase = (j[:, :, None] * w % 512) * (TWO_PI / 512)
    col = np.stack([np.cos(phase), np.sin(phase)], axis=1).reshape(128, 512)
    k = np.arange(64)
    f = np.where(k < 32, k, 448 + k)
    h = np.arange(512)
    phase = (h[:, None] * f[None, :] % 512) * (TWO_PI / 512)
    ca, sa = np.cos(phase), np.sin(phase)
    r = np.stack([ca, sa], axis=1).reshape(16, 32, 128)
    eye = np.eye(4)
    fwd = np.einsum("shn,cd->schdn", r, eye).reshape(2048, 512)
    first = np.stack([ca, -sa], axis=1)
    second = np.stack([-sa, -ca], axis=1)
    inv = np.stack([first, second], axis=1).reshape(16, 32, 2, 128)
    inv = np.einsum("shqn,cd->cnsqdh", inv, eye).reshape(512, 4096)
    perm = np.einsum("ad,be,cf,t->abtcfed", np.eye(4), np.eye(16), np.eye(4), np.ones(2))
    perm = perm.reshape(512, 256)
    return [np.asarray(t, np.float32).astype(ml_dtypes.bfloat16) for t in (col, fwd, inv, perm)]


def derivative(z):
    a = jnp.abs(z)
    e = jnp.exp(z * z * -0.5)
    d = 1.0 + (0.3275911 / math.sqrt(2.0)) * a
    t = pl.reciprocal(d, approx=True)
    t = t * (2.0 - d * t)
    poly = 1.061405429 * 0.5
    for c in (-1.453152027, 1.421413741, -0.284496736, 0.254829592):
        poly = poly * t + 0.5 * c
    q = e * (poly * t - a * (1.0 / math.sqrt(TWO_PI)))
    return jnp.where(z >= 0.0, 1.0 - q, q)


PEERS = tuple((dx, dy, dc) for dx in (1, 0) for dy in (2, 1, 3, 0) for dc in (1, 0))[:-1]


def kernel(
    dps,
    clips, cot, weight, pw, bias, col_h, fwd_h, inv_h, perm_h,
    side, last, sgrad,
    xv, cv, wv, col, fwd, inv, perm,
    send, recv, zs, dz, ya,
    xbf, xb, xbr, gbf, gb, gbr, dd, y3, kf, kb, bcol,
    in_sem, clip_sem, a2a_send, a2a_recv, dp_send, dp_recv, out_sem,
):
    pen = lax.axis_index("pencil")
    dpi = lax.axis_index("dp")
    per = 512 // dps
    kper = 64 // dps

    def clip_piece(b, n):
        at = pl.ds(n * 8, 8)
        return pltpu.make_async_copy(clips.at[b, at], xv.at[b, at], clip_sem.at[b, n])

    def load(src, dst, pieces, i):
        size = dst.shape[0] // pieces
        for n in range(pieces):
            at = pl.ds(n * size, size)
            pltpu.make_async_copy(src.at[at], dst.at[at], in_sem.at[i]).start()
        return pltpu.make_async_copy(dst, dst, in_sem.at[i]).wait

    col_wait = load(col_h, col, 1, 0)
    for b in range(2):
        for n in range(8):
            clip_piece(b, n).start()

    def peer_of(dx, dy, dc):
        return (pen // 8 + dx) % 2 * 8 + (pen // 2 + dy) % 4 * 2 + (pen + dc) % 2

    barrier = pltpu.get_barrier_semaphore()
    for steps in PEERS:
        peer = {"pencil": peer_of(*steps)}
        pl.semaphore_signal(barrier, inc=1, device_id=peer, device_id_type=MESH)

    def greet_dp(r, carry):
        pl.semaphore_signal(barrier, inc=1, device_id={"dp": (dpi + r) % dps}, device_id_type=MESH)
        return carry

    if dps > 1:
        lax.fori_loop(1, dps, greet_dp, 0)

    lane = lax.broadcasted_iota(jnp.int32, (1, 128), 1)
    low = lane < 64
    sign = jnp.where(low, 1.0, -1.0).astype(F32)

    def slots(b, phase):
        return last if (phase, b) == (3, 1) else recv.at[phase, b]

    def columns(values, b, phase):
        def step(n, carry):
            if values is xv:
                clip_piece(b, n).wait()
            rows = values[b, pl.ds(pl.multiple_of(n * 8, 8), 8)].reshape(256, 512)
            part = dot(col[...], rows, NT)
            pieces = [part[:, i * 128 : (i + 1) * 128].reshape(GROUP, 8, 128) for i in range(2)]
            at = pl.ds(pl.multiple_of(n * 16, 16), 16)
            send[phase, b, :, at, :] = jnp.concatenate(pieces, axis=1).astype(BF)
            return carry

        lax.fori_loop(0, 8, step, 0, unroll=2)

    def send_one(b, phase, to):
        pltpu.make_async_remote_copy(
            src_ref=send.at[phase, b, to],
            dst_ref=slots(b, phase).at[pen],
            send_sem=a2a_send.at[phase, b],
            recv_sem=a2a_recv.at[phase, b],
            device_id={"pencil": to},
            device_id_type=MESH,
        ).start()

    def keep_own(b, phase):
        pltpu.make_async_copy(
            send.at[phase, b, pen], slots(b, phase).at[pen], a2a_recv.at[phase, b]
        ).start()

    def scatter(b, phase):
        for steps in PEERS:
            send_one(b, phase, peer_of(*steps))
        keep_own(b, phase)

    def arrived(b, phase):
        whole = slots(b, phase)
        pltpu.make_async_copy(whole, whole, a2a_recv.at[phase, b]).wait()

    def spectrum(b, phase):
        arrived(b, phase)
        lhs = jnp.concatenate([recv[phase, b, s] for s in range(GROUP)], axis=1)
        upper = lax.broadcasted_iota(jnp.int32, (128, 128), 0) % 8 < 4
        pieces = []
        for n in range(2):
            wide = dot(lhs, fwd[:, n * 256 : (n + 1) * 256])
            for i in range(2):
                part = wide[:, i * 128 : (i + 1) * 128]
                sine = pltpu.roll(pltpu.roll(part, 64, 1), 124, 0)
                pieces.append(jnp.where(upper, part * sign - sine, 0.0).astype(BF))
        return dot(jnp.concatenate(pieces, axis=0), perm[...], TN)

    def to_owner(src, dst, i):
        def step(r, carry):
            to = (dpi + r) % dps
            pltpu.make_async_remote_copy(
                src_ref=src.at[to],
                dst_ref=dst.at[dpi],
                send_sem=dp_send.at[i],
                recv_sem=dp_recv.at[i],
                device_id={"dp": to},
                device_id_type=MESH,
            ).start()
            return carry

        if dps > 1:
            lax.fori_loop(1, dps, step, 0)
        pltpu.make_async_copy(src.at[dpi], dst.at[dpi], dp_recv.at[i]).start()

    def rows_back(i, b, phase):
        turned = dot(perm[...], ya[i, b], NT).astype(BF)
        lhs = jnp.concatenate([turned[c * 128 : (c + 1) * 128] for c in range(4)], axis=1)
        upper = lax.broadcasted_iota(jnp.int32, (128, 128), 0) % 8 < 4
        for steps in PEERS + ((0, 0, 0),):
            to = peer_of(*steps)
            lines = dot(lhs, inv[:, pl.ds(pl.multiple_of(to * 256, 256), 256)])
            send[phase, b, to] = jnp.where(upper, lines[:, :128], lines[:, 128:]).astype(BF)
            if steps == (0, 0, 0):
                keep_own(b, phase)
            else:
                send_one(b, phase, to)

    def field(ref, n):
        tile = ref[:, pl.ds(pl.multiple_of(n * 16, 16), 16), :].astype(F32)
        for i in range(2):
            lines = tile[:, i * 8 : (i + 1) * 8].reshape(128, 128).astype(BF)
            yield pl.ds(pl.multiple_of(n * 8 + i * 4, 4), 4), dot(lines, col[...], TN)

    def mix_points(values, b, matrix, add, tiles=(0, 2)):
        def step(t, carry):
            at = pl.multiple_of(t * 16, 16)
            for n in range(2):
                lanes = slice(n * 256, (n + 1) * 256)
                tile = values[b, :, pl.ds(at, 16), lanes].astype(F32)
                parts = []
                for i in range(2):
                    rows = tile[:, i * 8 : (i + 1) * 8].reshape(512, 256).astype(BF)
                    got = dot(matrix[...], rows)
                    if add is not None:
                        got = got + jnp.concatenate([add[...]] * 2, axis=1)
                        to = pl.multiple_of(t * 16 + i * 8, 8)
                        zs[b, :, pl.ds(to, 8), lanes] = got.reshape(64, 8, 256)
                    parts.append(got.reshape(64, 8, 256))
                if add is None:
                    xv[b, :, pl.ds(at, 16), lanes] = jnp.concatenate(parts, axis=1).astype(BF)
            return carry

        lax.fori_loop(*tiles, step, 0)

    row16 = lax.broadcasted_iota(jnp.int32, (16, 128), 0)
    scale = jnp.where(pen == 0, 1.0, 2.0).astype(F32) / 262144.0
    scale_lane = jnp.where(jnp.logical_and(low, pen == 0), 1.0, 2.0).astype(F32) / 262144.0

    pairs = kper // 2

    def own_rows(pair):
        return pl.ds(pl.multiple_of(pair % pairs * 16, 16), 16)

    def mix_modes(b):
        spec = spectrum(b, 0).astype(BF).astype(F32)
        for ri in range(2):
            for j in range(4):
                for p in range(2):
                    if p != j // 2:
                        continue
                    part = spec[ri * 64 : (ri + 1) * 64, p * 128 : (p + 1) * 128]
                    part = jnp.where(low if j % 2 == 0 else jnp.logical_not(low), part, 0.0)
                    xbf[p, pl.ds(ri * 4 + j, 64, stride=8), :] = part
        for p in range(2):
            xb[:, b, :, p * 128 : (p + 1) * 128] = xbf[p].astype(BF).reshape(dps, per, 128)

        def step(n, carry):
            for i in range(8):
                pair = n * 8 + i
                at = pl.multiple_of(pair * 16, 16)
                both = jnp.concatenate(
                    [wv[2 * pair].reshape(256, 128), wv[2 * pair + 1].reshape(256, 128)], axis=1
                )
                got = dot(xb[pair // pairs, b, own_rows(pair), :], both)
                y3[pl.ds(at, 8), :] = got[:8, :128]
                y3[pl.ds(at + 8, 8), :] = got[8:, 128:]
            return carry

        lax.fori_loop(0, 4, step, 0)
        modes = []
        for j in range(4):
            real = y3[pl.ds(j, 64, stride=8), :]
            imag = y3[pl.ds(4 + j, 64, stride=8), :]
            mixed = real - sign * pltpu.roll(imag, 64, 1)
            modes.append(mixed * (scale if j == 0 else 2.0 / 262144.0))
        for p in range(2):
            first, second = modes[2 * p], modes[2 * p + 1]
            real = jnp.where(low, first, pltpu.roll(second, 64, 1))
            imag = jnp.where(low, pltpu.roll(first, 64, 1), second)
            ya[0, b, 0:64, p * 128 : (p + 1) * 128] = real.astype(BF)
            ya[0, b, 64:128, p * 128 : (p + 1) * 128] = imag.astype(BF)
        rows_back(0, b, 1)

    def grad_modes(b):
        spec = spectrum(b, 2)
        for p in range(2):
            part = spec[:, p * 128 : (p + 1) * 128]
            part = part * (scale_lane if p == 0 else 2.0 / 262144.0)
            real, imag = part[:64], part[64:]
            real_r, imag_r = pltpu.roll(real, 64, 1), pltpu.roll(imag, 64, 1)
            for i, (re, im) in enumerate(
                ((jnp.where(low, real, imag_r), jnp.where(low, imag, real_r)),
                 (jnp.where(low, real_r, imag), jnp.where(low, imag_r, real)))
            ):
                gbf[pl.ds(2 * p + i, 64, stride=8), :] = re
                gbf[pl.ds(4 + 2 * p + i, 64, stride=8), :] = im * sign
        gb[:, b] = gbf[...].astype(BF).reshape(dps, per, 128)

        def step(n, carry):
            for i in range(8):
                pair = n * 8 + i
                at = pl.multiple_of(pair * 16, 16)
                rhs = wv[pl.ds(2 * pair, 2)].reshape(512, 128)
                got = dot(gb[pair // pairs, b, own_rows(pair), :], rhs, NT)
                for p in range(2):
                    dd[p, pl.ds(at, 8), :] = got[:8, p * 128 : (p + 1) * 128]
                    dd[p, pl.ds(at + 8, 8), :] = got[8:, 256 + p * 128 : 384 + p * 128]
            return carry

        lax.fori_loop(0, 4, step, 0)
        for p in range(2):
            for ri in range(2):
                first = dd[p, pl.ds(ri * 4 + 2 * p, 64, stride=8), :]
                second = dd[p, pl.ds(ri * 4 + 2 * p + 1, 64, stride=8), :]
                ya[1, b, ri * 64 : (ri + 1) * 64, p * 128 : (p + 1) * 128] = jnp.where(
                    low, first, second
                ).astype(BF)
        rows_back(1, b, 3)

    def activation(b, chunks):
        def step(n, carry):
            for at, got in field(recv.at[1, b], n):
                z = got + zs[b, at].reshape(128, 512)
                grad = cv[b, at].reshape(128, 512).astype(F32) * derivative(z)
                dz[b, at] = grad.astype(BF).reshape(4, 32, 512)
            return carry

        lax.fori_loop(*chunks, step, 0, unroll=2)

    def leave(b):
        pltpu.make_async_copy(xv.at[b], side.at[b], out_sem.at[b]).start()

    def finish_first():
        arrived(0, 3)

        def step(n, carry):
            for at, got in field(recv.at[3, 0], n):
                got = got + xv[0, at].reshape(128, 512).astype(F32)
                xv[0, at] = got.astype(BF).reshape(4, 32, 512)
            return carry

        lax.fori_loop(0, 8, step, 0, unroll=2)
        leave(0)

    def weight_grad():
        for i, ref in enumerate((xbr, gbr)):
            pltpu.make_async_copy(ref, ref, dp_recv.at[i]).wait()
        first_rows = jnp.where(row16 < 8, 1.0, 0.0).astype(F32)
        for pair in range(pairs):
            at = slice(pair * 16, (pair + 1) * 16)
            left = xbr[:, :, at, :].reshape(2 * dps * 16, 256)
            right = gbr[:, :, at, :].astype(F32)
            head = (right * first_rows).astype(BF).reshape(2 * dps * 16, 128)
            tail = (right * (1.0 - first_rows)).astype(BF).reshape(2 * dps * 16, 128)
            got = dot(left, jnp.concatenate([head, tail], axis=1), TN)
            for i in range(2):
                sgrad[2 * pair + i] = got[:, i * 128 : (i + 1) * 128].reshape(4, 64, 128)

    col_wait()
    columns(xv, 0, 0)
    pl.semaphore_wait(barrier, GROUP - 1 + dps - 1)
    scatter(0, 0)
    fwd_wait = load(fwd_h, fwd, 4, 1)
    perm_wait = load(perm_h, perm, 2, 2)
    columns(xv, 1, 0)
    scatter(1, 0)
    weight_wait = load(weight, wv, 16, 3)
    inv_wait = load(inv_h, inv, 8, 4)
    cot_waits = [load(cot.at[b], cv.at[b], 8, 5 + b) for b in range(2)]

    row = lax.broadcasted_iota(jnp.int32, (512, 64), 0)
    lanes64 = lax.broadcasted_iota(jnp.int32, (512, 64), 1)
    spread = jnp.where(row // 8 == lanes64, 1.0, 0.0).astype(BF)
    same = (
        lax.broadcasted_iota(jnp.int32, (512, 512), 0) % 8
        == lax.broadcasted_iota(jnp.int32, (512, 512), 1) % 8
    )
    for p in range(2):
        xbf[p] = jnp.zeros((512, 128), F32)
    kf[...] = jnp.where(same, dot(dot(spread, pw[...], NT).astype(BF), spread, NT), 0.0).astype(BF)
    kb[...] = jnp.where(same, dot(dot(spread, pw[...]).astype(BF), spread, NT), 0.0).astype(BF)
    biased = (spread.astype(F32) * bias[...].astype(F32)).astype(BF)
    bcol[...] = dot(biased, jnp.ones((64, 128), BF))
    mix_points(xv, 0, kf, bcol)

    fwd_wait()
    perm_wait()
    inv_wait()
    weight_wait()
    mix_modes(0)
    mix_points(xv, 1, kf, bcol)
    mix_modes(1)
    to_owner(xb, xbr, 0)

    for b in range(2):
        arrived(b, 1)
        cot_waits[b]()
        activation(b, (0, 8))
        columns(dz, b, 2)
        scatter(b, 2)
    grad_modes(0)
    mix_points(dz, 0, kb, None, (0, 1))
    grad_modes(1)
    to_owner(gb, gbr, 1)
    mix_points(dz, 0, kb, None, (1, 2))
    mix_points(dz, 1, kb, None)
    leave(1)
    finish_first()
    weight_grad()

    for phase in range(4):
        for b in range(2):
            sent = send.at[phase, b, pl.ds(0, GROUP - 1)]
            pltpu.make_async_copy(sent, sent, a2a_send.at[phase, b]).wait()
    if dps > 1:
        for i, ref in enumerate((xb, gb)):
            sent = ref.at[pl.ds(0, dps - 1)]
            pltpu.make_async_copy(sent, sent, dp_send.at[i]).wait()
    for b in range(2):
        pltpu.make_async_copy(xv.at[b], side.at[b], out_sem.at[b]).wait()
    arrived(1, 3)


def finish(side, lines, col_h, sgrad, out, weights_out, sv, lv, col, gv, side_sem, sem):
    def piece(b, n):
        at = pl.ds(n * 8, 8)
        return pltpu.make_async_copy(side.at[b, at], sv.at[b, at], side_sem.at[b, n])

    def write(b, n):
        at = pl.ds(n * 8, 8)
        pltpu.make_async_copy(sv.at[b, at], out.at[b, at], sem.at[3 + b]).start()

    pltpu.make_async_copy(col_h, col, sem.at[0]).start()
    for s in range(GROUP):
        pltpu.make_async_copy(lines.at[s], lv.at[s], sem.at[1]).start()
    for b in (1, 0):
        for n in range(8):
            piece(b, n).start()
    pltpu.make_async_copy(sgrad, gv, sem.at[2]).start()
    pltpu.make_async_copy(col, col, sem.at[0]).wait()
    pltpu.make_async_copy(lv, lv, sem.at[1]).wait()

    def step(n, carry):
        piece(1, n).wait()
        tile = lv[:, pl.ds(pl.multiple_of(n * 16, 16), 16), :].astype(F32)
        for i in range(2):
            at = pl.ds(pl.multiple_of(n * 8 + i * 4, 4), 4)
            part = tile[:, i * 8 : (i + 1) * 8].reshape(128, 128).astype(BF)
            got = dot(part, col[...], TN) + sv[1, at].reshape(128, 512).astype(F32)
            sv[1, at] = got.astype(BF).reshape(4, 32, 512)
        write(1, n)
        piece(0, n).wait()
        write(0, n)
        return carry

    lax.fori_loop(0, 8, step, 0, unroll=2)
    pltpu.make_async_copy(gv, gv, sem.at[2]).wait()
    away = pltpu.make_async_copy(gv, weights_out, sem.at[5])
    away.start()
    for b in range(2):
        pltpu.make_async_copy(sv.at[b], sv.at[b], sem.at[3 + b]).wait()
    away.wait()


def shards(dps, clips, cotangent, spectral_weight, point_weight, bias):
    col, fwd, inv, perm = [jnp.asarray(t) for t in tables()]
    any_spec = pl.BlockSpec(memory_space=pl.ANY)
    vmem = pl.BlockSpec(memory_space=pltpu.VMEM)
    per = 512 // dps
    dma = pltpu.SemaphoreType.DMA
    grad_shape = jax.ShapeDtypeStruct((64 // dps, 4, 64, 128), F32)
    side, last, sgrad = pl.pallas_call(
        functools.partial(kernel, dps),
        out_shape=(
            jax.ShapeDtypeStruct((2, 64, 32, 512), BF),
            jax.ShapeDtypeStruct((GROUP, 128, 128), BF),
            grad_shape,
        ),
        in_specs=[any_spec] * 3 + [vmem] * 2 + [any_spec] * 4,
        out_specs=(any_spec, any_spec, vmem),
        scratch_shapes=[
            pltpu.VMEM((2, 64, 32, 512), BF),
            pltpu.VMEM((2, 64, 32, 512), BF),
            pltpu.VMEM((64, 4, 64, 128), BF),
            pltpu.VMEM((128, 512), BF),
            pltpu.VMEM((2048, 512), BF),
            pltpu.VMEM((512, 4096), BF),
            pltpu.VMEM((512, 256), BF),
            pltpu.VMEM((4, 2, GROUP, 128, 128), BF),
            pltpu.VMEM((4, 2, GROUP, 128, 128), BF),
            pltpu.VMEM((2, 64, 32, 512), F32),
            pltpu.VMEM((2, 64, 32, 512), BF),
            pltpu.VMEM((2, 2, 128, 256), BF),
            pltpu.VMEM((2, 512, 128), F32),
            pltpu.VMEM((dps, 2, per, 256), BF),
            pltpu.VMEM((dps, 2, per, 256), BF),
            pltpu.VMEM((512, 128), F32),
            pltpu.VMEM((dps, 2, per, 128), BF),
            pltpu.VMEM((dps, 2, per, 128), BF),
            pltpu.VMEM((2, 512, 128), F32),
            pltpu.VMEM((512, 128), F32),
            pltpu.VMEM((512, 512), BF),
            pltpu.VMEM((512, 512), BF),
            pltpu.VMEM((512, 128), F32),
            dma((7,)),
            dma((2, 8)),
            dma((4, 2)),
            dma((4, 2)),
            dma((2,)),
            dma((2,)),
            dma((2,)),
        ],
        compiler_params=pltpu.CompilerParams(
            collective_id=0, has_side_effects=True, vmem_limit_bytes=60 * 1024 * 1024
        ),
        cost_estimate=pl.CostEstimate(
            flops=20_000_000_000, bytes_accessed=20_000_000, transcendentals=4_000_000
        ),
    )(clips, cotangent, spectral_weight, point_weight, bias.reshape(1, 64), col, fwd, inv, perm)
    return pl.pallas_call(
        finish,
        out_shape=(jax.ShapeDtypeStruct((2, 64, 32, 512), BF), grad_shape),
        in_specs=[any_spec] * 4,
        out_specs=(any_spec, any_spec),
        scratch_shapes=[
            pltpu.VMEM((2, 64, 32, 512), BF),
            pltpu.VMEM((GROUP, 128, 128), BF),
            pltpu.VMEM((128, 512), BF),
            pltpu.VMEM(grad_shape.shape, F32),
            dma((2, 8)),
            dma((6,)),
        ],
        compiler_params=pltpu.CompilerParams(vmem_limit_bytes=60 * 1024 * 1024),
        cost_estimate=pl.CostEstimate(
            flops=600_000_000, bytes_accessed=10_000_000, transcendentals=0
        ),
    )(side, last, col, sgrad)


def solution(mesh):
    in_specs = (
        P("dp", None, "pencil", None),
        P("dp", None, "pencil", None),
        P(None, "pencil", None, None),
        P(),
        P(),
    )
    out_specs = (P("dp", None, "pencil", None), P("dp", "pencil", None, None))
    return jax.shard_map(
        functools.partial(shards, mesh.shape["dp"]),
        mesh=mesh,
        in_specs=in_specs,
        out_specs=out_specs,
        check_vma=False,
    )
```

```python
import functools
import math

import jax
import jax.numpy as jnp
import ml_dtypes
import numpy as np
from jax import lax
from jax.experimental import pallas as pl
from jax.experimental.pallas import tpu as pltpu
from jax.sharding import PartitionSpec as P

TWO_PI = 2.0 * math.pi
MESH = pl.DeviceIdType.MESH
BF = jnp.bfloat16
F32 = jnp.float32
GROUP = 16
TN = (((0,), (0,)), ((), ()))
NT = (((1,), (1,)), ((), ()))
NN = (((1,), (0,)), ((), ()))


def dot(a, b, dims=NN):
    return lax.dot_general(a, b, dims, preferred_element_type=F32)


def tables():
    w = np.arange(512)
    j = np.arange(64).reshape(16, 4)
    phase = (j[:, :, None] * w % 512) * (TWO_PI / 512)
    col = np.stack([np.cos(phase), np.sin(phase)], axis=1).reshape(128, 512)
    k = np.arange(64)
    f = np.where(k < 32, k, 448 + k)
    h = np.arange(512)
    phase = (h[:, None] * f[None, :] % 512) * (TWO_PI / 512)
    ca, sa = np.cos(phase), np.sin(phase)
    r = np.stack([ca, sa], axis=1).reshape(16, 32, 128)
    eye = np.eye(4)
    fwd = np.einsum("shn,cd->schdn", r, eye).reshape(2048, 512)
    first = np.stack([ca, -sa], axis=1)
    second = np.stack([-sa, -ca], axis=1)
    inv = np.stack([first, second], axis=1).reshape(16, 32, 2, 128)
    inv = np.einsum("shqn,cd->cnsqdh", inv, eye).reshape(512, 4096)
    perm = np.einsum("ad,be,cf,t->abtcfed", np.eye(4), np.eye(16), np.eye(4), np.ones(2))
    perm = perm.reshape(512, 256)
    return [np.asarray(t, np.float32).astype(ml_dtypes.bfloat16) for t in (col, fwd, inv, perm)]


def derivative(z):
    e = jnp.exp2(z * z * (-0.5 / math.log(2.0))).astype(BF)
    d = 1.0 + (0.3275911 / math.sqrt(2.0)) * jnp.abs(z)
    t = pl.reciprocal(d, approx=True).astype(BF)
    z = z.astype(BF)
    poly = jnp.full_like(t, 1.061405429 * 0.5)
    for c in (-1.453152027, 1.421413741, -0.284496736, 0.254829592):
        poly = poly * t + jnp.asarray(0.5 * c, BF)
    q = e * (poly * t - jnp.abs(z) * jnp.asarray(1.0 / math.sqrt(TWO_PI), BF))
    return jnp.where(z >= 0, 1 - q, q)


PEERS = tuple((dx, dy, dc) for dx in (1, 0) for dy in (2, 1, 3, 0) for dc in (1, 0))[:-1]


def kernel(
    dps,
    clips, cot, weight, pw, bias, col_h, fwd_h, inv_h, perm_h,
    side, last, sgrad,
    xv, cv, wv, col, fwd, inv, perm,
    send, recv, zs, dz, ya,
    xbf, xb, xbr, gbf, gb, gbr, dd, y3, kf, kb, bcol,
    in_sem, clip_sem, a2a_send, a2a_recv, dp_send, dp_recv, out_sem,
):
    pen = lax.axis_index("pencil")
    dpi = lax.axis_index("dp")
    per = 512 // dps
    kper = 64 // dps

    def clip_piece(b, n):
        at = pl.ds(n * 8, 8)
        return pltpu.make_async_copy(clips.at[b, at], xv.at[b, at], clip_sem.at[b, n])

    def load(src, dst, pieces, i):
        size = dst.shape[0] // pieces
        for n in range(pieces):
            at = pl.ds(n * size, size)
            pltpu.make_async_copy(src.at[at], dst.at[at], in_sem.at[i]).start()
        return pltpu.make_async_copy(dst, dst, in_sem.at[i]).wait

    col_wait = load(col_h, col, 1, 0)
    for b in range(2):
        for n in range(8):
            clip_piece(b, n).start()

    def peer_of(dx, dy, dc):
        return (pen // 8 + dx) % 2 * 8 + (pen // 2 + dy) % 4 * 2 + (pen + dc) % 2

    barrier = pltpu.get_barrier_semaphore()
    for steps in PEERS:
        peer = {"pencil": peer_of(*steps)}
        pl.semaphore_signal(barrier, inc=1, device_id=peer, device_id_type=MESH)

    def greet_dp(r, carry):
        pl.semaphore_signal(barrier, inc=1, device_id={"dp": (dpi + r) % dps}, device_id_type=MESH)
        return carry

    if dps > 1:
        lax.fori_loop(1, dps, greet_dp, 0)

    lane = lax.broadcasted_iota(jnp.int32, (1, 128), 1)
    low = lane < 64
    sign = jnp.where(low, 1.0, -1.0).astype(F32)

    def slots(b, phase):
        return last if (phase, b) == (3, 1) else recv.at[phase, b]

    def columns(rows, b, phase, n):
        part = dot(col[...], rows, NT)
        pieces = [part[:, i * 128 : (i + 1) * 128].reshape(GROUP, 8, 128) for i in range(2)]
        at = pl.ds(pl.multiple_of(n * 16, 16), 16)
        send[phase, b, :, at, :] = jnp.concatenate(pieces, axis=1).astype(BF)

    def clip_columns(b):
        def step(n, carry):
            clip_piece(b, n).wait()
            columns(xv[b, pl.ds(pl.multiple_of(n * 8, 8), 8)].reshape(256, 512), b, 0, n)
            return carry

        lax.fori_loop(0, 8, step, 0, unroll=2)

    def send_one(b, phase, to):
        pltpu.make_async_remote_copy(
            src_ref=send.at[phase, b, to],
            dst_ref=slots(b, phase).at[pen],
            send_sem=a2a_send.at[phase, b],
            recv_sem=a2a_recv.at[phase, b],
            device_id={"pencil": to},
            device_id_type=MESH,
        ).start()

    def keep_own(b, phase):
        pltpu.make_async_copy(
            send.at[phase, b, pen], slots(b, phase).at[pen], a2a_recv.at[phase, b]
        ).start()

    def scatter(b, phase):
        for steps in PEERS:
            send_one(b, phase, peer_of(*steps))
        keep_own(b, phase)

    def arrived(b, phase):
        whole = slots(b, phase)
        pltpu.make_async_copy(whole, whole, a2a_recv.at[phase, b]).wait()

    def spectrum(b, phase):
        arrived(b, phase)
        lhs = jnp.concatenate([recv[phase, b, s] for s in range(GROUP)], axis=1)
        upper = lax.broadcasted_iota(jnp.int32, (128, 128), 0) % 8 < 4
        pieces = []
        for n in range(2):
            wide = dot(lhs, fwd[:, n * 256 : (n + 1) * 256])
            for i in range(2):
                part = wide[:, i * 128 : (i + 1) * 128]
                sine = pltpu.roll(pltpu.roll(part, 64, 1), 124, 0)
                pieces.append(jnp.where(upper, part * sign - sine, 0.0).astype(BF))
        return dot(jnp.concatenate(pieces, axis=0), perm[...], TN)

    def to_owner(src, dst, i):
        def step(r, carry):
            to = (dpi + r) % dps
            pltpu.make_async_remote_copy(
                src_ref=src.at[to],
                dst_ref=dst.at[dpi],
                send_sem=dp_send.at[i],
                recv_sem=dp_recv.at[i],
                device_id={"dp": to},
                device_id_type=MESH,
            ).start()
            return carry

        if dps > 1:
            lax.fori_loop(1, dps, step, 0)
        pltpu.make_async_copy(src.at[dpi], dst.at[dpi], dp_recv.at[i]).start()

    def rows_back(i, b, phase):
        turned = dot(perm[...], ya[i, b], NT).astype(BF)
        lhs = jnp.concatenate([turned[c * 128 : (c + 1) * 128] for c in range(4)], axis=1)
        upper = lax.broadcasted_iota(jnp.int32, (128, 128), 0) % 8 < 4
        for steps in PEERS + ((0, 0, 0),):
            to = peer_of(*steps)
            lines = dot(lhs, inv[:, pl.ds(pl.multiple_of(to * 256, 256), 256)])
            send[phase, b, to] = jnp.where(upper, lines[:, :128], lines[:, 128:]).astype(BF)
            if steps == (0, 0, 0):
                keep_own(b, phase)
            else:
                send_one(b, phase, to)

    def field(ref, n):
        tile = ref[:, pl.ds(pl.multiple_of(n * 16, 16), 16), :].astype(F32)
        for i in range(2):
            lines = tile[:, i * 8 : (i + 1) * 8].reshape(128, 128).astype(BF)
            yield pl.ds(pl.multiple_of(n * 8 + i * 4, 4), 4), dot(lines, col[...], TN)

    def mix_points(values, b, matrix, add, tiles=(0, 2)):
        def step(t, carry):
            at = pl.multiple_of(t * 16, 16)
            for n in range(2):
                lanes = slice(n * 256, (n + 1) * 256)
                tile = values[b, :, pl.ds(at, 16), lanes].astype(F32)
                parts = []
                for i in range(2):
                    rows = tile[:, i * 8 : (i + 1) * 8].reshape(512, 256).astype(BF)
                    got = dot(matrix[...], rows)
                    if add is not None:
                        got = got + jnp.concatenate([add[...]] * 2, axis=1)
                        to = pl.multiple_of(t * 16 + i * 8, 8)
                        zs[b, :, pl.ds(to, 8), lanes] = got.reshape(64, 8, 256)
                    parts.append(got.reshape(64, 8, 256))
                if add is None:
                    xv[b, :, pl.ds(at, 16), lanes] = jnp.concatenate(parts, axis=1).astype(BF)
            return carry

        lax.fori_loop(*tiles, step, 0)

    row16 = lax.broadcasted_iota(jnp.int32, (16, 128), 0)
    scale = jnp.where(pen == 0, 1.0, 2.0).astype(F32) / 262144.0
    scale_lane = jnp.where(jnp.logical_and(low, pen == 0), 1.0, 2.0).astype(F32) / 262144.0

    pairs = kper // 2

    def own_rows(pair):
        return pl.ds(pl.multiple_of(pair % pairs * 16, 16), 16)

    def mix_modes(b):
        spec = spectrum(b, 0).astype(BF).astype(F32)
        for ri in range(2):
            for j in range(4):
                for p in range(2):
                    if p != j // 2:
                        continue
                    part = spec[ri * 64 : (ri + 1) * 64, p * 128 : (p + 1) * 128]
                    part = jnp.where(low if j % 2 == 0 else jnp.logical_not(low), part, 0.0)
                    xbf[p, pl.ds(ri * 4 + j, 64, stride=8), :] = part
        for p in range(2):
            xb[:, b, :, p * 128 : (p + 1) * 128] = xbf[p].astype(BF).reshape(dps, per, 128)

        def step(n, carry):
            for i in range(8):
                pair = n * 8 + i
                at = pl.multiple_of(pair * 16, 16)
                both = jnp.concatenate(
                    [wv[2 * pair].reshape(256, 128), wv[2 * pair + 1].reshape(256, 128)], axis=1
                )
                got = dot(xb[pair // pairs, b, own_rows(pair), :], both)
                y3[pl.ds(at, 8), :] = got[:8, :128]
                y3[pl.ds(at + 8, 8), :] = got[8:, 128:]
            return carry

        lax.fori_loop(0, 4, step, 0)
        modes = []
        for j in range(4):
            real = y3[pl.ds(j, 64, stride=8), :]
            imag = y3[pl.ds(4 + j, 64, stride=8), :]
            mixed = real - sign * pltpu.roll(imag, 64, 1)
            modes.append(mixed * (scale if j == 0 else 2.0 / 262144.0))
        for p in range(2):
            first, second = modes[2 * p], modes[2 * p + 1]
            real = jnp.where(low, first, pltpu.roll(second, 64, 1))
            imag = jnp.where(low, pltpu.roll(first, 64, 1), second)
            ya[0, b, 0:64, p * 128 : (p + 1) * 128] = real.astype(BF)
            ya[0, b, 64:128, p * 128 : (p + 1) * 128] = imag.astype(BF)
        rows_back(0, b, 1)

    def grad_modes(b):
        spec = spectrum(b, 2)
        for p in range(2):
            part = spec[:, p * 128 : (p + 1) * 128]
            part = part * (scale_lane if p == 0 else 2.0 / 262144.0)
            real, imag = part[:64], part[64:]
            real_r, imag_r = pltpu.roll(real, 64, 1), pltpu.roll(imag, 64, 1)
            for i, (re, im) in enumerate(
                ((jnp.where(low, real, imag_r), jnp.where(low, imag, real_r)),
                 (jnp.where(low, real_r, imag), jnp.where(low, imag_r, real)))
            ):
                gbf[pl.ds(2 * p + i, 64, stride=8), :] = re
                gbf[pl.ds(4 + 2 * p + i, 64, stride=8), :] = im * sign
        gb[:, b] = gbf[...].astype(BF).reshape(dps, per, 128)

        def step(n, carry):
            for i in range(8):
                pair = n * 8 + i
                at = pl.multiple_of(pair * 16, 16)
                rhs = wv[pl.ds(2 * pair, 2)].reshape(512, 128)
                got = dot(gb[pair // pairs, b, own_rows(pair), :], rhs, NT)
                for p in range(2):
                    dd[p, pl.ds(at, 8), :] = got[:8, p * 128 : (p + 1) * 128]
                    dd[p, pl.ds(at + 8, 8), :] = got[8:, 256 + p * 128 : 384 + p * 128]
            return carry

        lax.fori_loop(0, 4, step, 0)
        for p in range(2):
            for ri in range(2):
                first = dd[p, pl.ds(ri * 4 + 2 * p, 64, stride=8), :]
                second = dd[p, pl.ds(ri * 4 + 2 * p + 1, 64, stride=8), :]
                ya[1, b, ri * 64 : (ri + 1) * 64, p * 128 : (p + 1) * 128] = jnp.where(
                    low, first, second
                ).astype(BF)
        rows_back(1, b, 3)

    def activation(b, chunks):
        def step(n, carry):
            grads = []
            for at, got in field(recv.at[1, b], n):
                z = got + zs[b, at].reshape(128, 512)
                grads.append(cv[b, at].reshape(128, 512) * derivative(z))
                dz[b, at] = grads[-1].reshape(4, 32, 512)
            columns(jnp.concatenate(grads, axis=0), b, 2, n)
            return carry

        lax.fori_loop(*chunks, step, 0, unroll=2)

    def leave(b):
        pltpu.make_async_copy(xv.at[b], side.at[b], out_sem.at[b]).start()

    def finish_first():
        arrived(0, 3)

        def step(n, carry):
            for at, got in field(recv.at[3, 0], n):
                got = got + xv[0, at].reshape(128, 512).astype(F32)
                xv[0, at] = got.astype(BF).reshape(4, 32, 512)
            return carry

        lax.fori_loop(0, 8, step, 0, unroll=2)
        leave(0)

    def weight_grad():
        for i, ref in enumerate((xbr, gbr)):
            pltpu.make_async_copy(ref, ref, dp_recv.at[i]).wait()
        first_rows = jnp.where(row16 < 8, 1.0, 0.0).astype(F32)
        for pair in range(pairs):
            at = slice(pair * 16, (pair + 1) * 16)
            left = xbr[:, :, at, :].reshape(2 * dps * 16, 256)
            right = gbr[:, :, at, :].astype(F32)
            head = (right * first_rows).astype(BF).reshape(2 * dps * 16, 128)
            tail = (right * (1.0 - first_rows)).astype(BF).reshape(2 * dps * 16, 128)
            got = dot(left, jnp.concatenate([head, tail], axis=1), TN)
            for i in range(2):
                sgrad[2 * pair + i] = got[:, i * 128 : (i + 1) * 128].reshape(4, 64, 128)

    col_wait()
    clip_columns(0)
    pl.semaphore_wait(barrier, GROUP - 1 + dps - 1)
    scatter(0, 0)
    fwd_wait = load(fwd_h, fwd, 4, 1)
    perm_wait = load(perm_h, perm, 2, 2)
    clip_columns(1)
    scatter(1, 0)
    weight_wait = load(weight, wv, 16, 3)
    inv_wait = load(inv_h, inv, 8, 4)
    cot_waits = [load(cot.at[b], cv.at[b], 8, 5 + b) for b in range(2)]

    row = lax.broadcasted_iota(jnp.int32, (512, 64), 0)
    lanes64 = lax.broadcasted_iota(jnp.int32, (512, 64), 1)
    spread = jnp.where(row // 8 == lanes64, 1.0, 0.0).astype(BF)
    same = (
        lax.broadcasted_iota(jnp.int32, (512, 512), 0) % 8
        == lax.broadcasted_iota(jnp.int32, (512, 512), 1) % 8
    )
    for p in range(2):
        xbf[p] = jnp.zeros((512, 128), F32)
    kf[...] = jnp.where(same, dot(dot(spread, pw[...], NT).astype(BF), spread, NT), 0.0).astype(BF)
    kb[...] = jnp.where(same, dot(dot(spread, pw[...]).astype(BF), spread, NT), 0.0).astype(BF)
    biased = (spread.astype(F32) * bias[...].astype(F32)).astype(BF)
    bcol[...] = dot(biased, jnp.ones((64, 128), BF))
    mix_points(xv, 0, kf, bcol)

    fwd_wait()
    perm_wait()
    inv_wait()
    weight_wait()
    mix_modes(0)
    mix_points(xv, 1, kf, bcol)
    mix_modes(1)
    to_owner(xb, xbr, 0)

    for b in range(2):
        arrived(b, 1)
        cot_waits[b]()
        activation(b, (0, 8))
        scatter(b, 2)
    grad_modes(0)
    mix_points(dz, 0, kb, None, (0, 1))
    grad_modes(1)
    to_owner(gb, gbr, 1)
    mix_points(dz, 0, kb, None, (1, 2))
    mix_points(dz, 1, kb, None)
    leave(1)
    finish_first()
    weight_grad()

    for phase in range(4):
        for b in range(2):
            sent = send.at[phase, b, pl.ds(0, GROUP - 1)]
            pltpu.make_async_copy(sent, sent, a2a_send.at[phase, b]).wait()
    if dps > 1:
        for i, ref in enumerate((xb, gb)):
            sent = ref.at[pl.ds(0, dps - 1)]
            pltpu.make_async_copy(sent, sent, dp_send.at[i]).wait()
    for b in range(2):
        pltpu.make_async_copy(xv.at[b], side.at[b], out_sem.at[b]).wait()
    arrived(1, 3)


def finish(side, lines, col_h, sgrad, out, weights_out, sv, lv, col, gv, side_sem, sem):
    def piece(b, n):
        at = pl.ds(n * 8, 8)
        return pltpu.make_async_copy(side.at[b, at], sv.at[b, at], side_sem.at[b, n])

    def write(b, n):
        at = pl.ds(n * 8, 8)
        pltpu.make_async_copy(sv.at[b, at], out.at[b, at], sem.at[3 + b]).start()

    pltpu.make_async_copy(col_h, col, sem.at[0]).start()
    for s in range(GROUP):
        pltpu.make_async_copy(lines.at[s], lv.at[s], sem.at[1]).start()
    for b in (1, 0):
        for n in range(8):
            piece(b, n).start()
    pltpu.make_async_copy(sgrad, gv, sem.at[2]).start()
    pltpu.make_async_copy(col, col, sem.at[0]).wait()
    pltpu.make_async_copy(lv, lv, sem.at[1]).wait()

    def step(n, carry):
        piece(1, n).wait()
        tile = lv[:, pl.ds(pl.multiple_of(n * 16, 16), 16), :].astype(F32)
        for i in range(2):
            at = pl.ds(pl.multiple_of(n * 8 + i * 4, 4), 4)
            part = tile[:, i * 8 : (i + 1) * 8].reshape(128, 128).astype(BF)
            got = dot(part, col[...], TN) + sv[1, at].reshape(128, 512).astype(F32)
            sv[1, at] = got.astype(BF).reshape(4, 32, 512)
        write(1, n)
        piece(0, n).wait()
        write(0, n)
        return carry

    lax.fori_loop(0, 8, step, 0, unroll=2)
    pltpu.make_async_copy(gv, gv, sem.at[2]).wait()
    away = pltpu.make_async_copy(gv, weights_out, sem.at[5])
    away.start()
    for b in range(2):
        pltpu.make_async_copy(sv.at[b], sv.at[b], sem.at[3 + b]).wait()
    away.wait()


def shards(dps, clips, cotangent, spectral_weight, point_weight, bias):
    col, fwd, inv, perm = [jnp.asarray(t) for t in tables()]
    any_spec = pl.BlockSpec(memory_space=pl.ANY)
    vmem = pl.BlockSpec(memory_space=pltpu.VMEM)
    per = 512 // dps
    dma = pltpu.SemaphoreType.DMA
    grad_shape = jax.ShapeDtypeStruct((64 // dps, 4, 64, 128), F32)
    side, last, sgrad = pl.pallas_call(
        functools.partial(kernel, dps),
        out_shape=(
            jax.ShapeDtypeStruct((2, 64, 32, 512), BF),
            jax.ShapeDtypeStruct((GROUP, 128, 128), BF),
            grad_shape,
        ),
        in_specs=[any_spec] * 3 + [vmem] * 2 + [any_spec] * 4,
        out_specs=(any_spec, any_spec, vmem),
        scratch_shapes=[
            pltpu.VMEM((2, 64, 32, 512), BF),
            pltpu.VMEM((2, 64, 32, 512), BF),
            pltpu.VMEM((64, 4, 64, 128), BF),
            pltpu.VMEM((128, 512), BF),
            pltpu.VMEM((2048, 512), BF),
            pltpu.VMEM((512, 4096), BF),
            pltpu.VMEM((512, 256), BF),
            pltpu.VMEM((4, 2, GROUP, 128, 128), BF),
            pltpu.VMEM((4, 2, GROUP, 128, 128), BF),
            pltpu.VMEM((2, 64, 32, 512), F32),
            pltpu.VMEM((2, 64, 32, 512), BF),
            pltpu.VMEM((2, 2, 128, 256), BF),
            pltpu.VMEM((2, 512, 128), F32),
            pltpu.VMEM((dps, 2, per, 256), BF),
            pltpu.VMEM((dps, 2, per, 256), BF),
            pltpu.VMEM((512, 128), F32),
            pltpu.VMEM((dps, 2, per, 128), BF),
            pltpu.VMEM((dps, 2, per, 128), BF),
            pltpu.VMEM((2, 512, 128), F32),
            pltpu.VMEM((512, 128), F32),
            pltpu.VMEM((512, 512), BF),
            pltpu.VMEM((512, 512), BF),
            pltpu.VMEM((512, 128), F32),
            dma((7,)),
            dma((2, 8)),
            dma((4, 2)),
            dma((4, 2)),
            dma((2,)),
            dma((2,)),
            dma((2,)),
        ],
        compiler_params=pltpu.CompilerParams(
            collective_id=0, has_side_effects=True, vmem_limit_bytes=60 * 1024 * 1024
        ),
        cost_estimate=pl.CostEstimate(
            flops=20_000_000_000, bytes_accessed=20_000_000, transcendentals=4_000_000
        ),
    )(clips, cotangent, spectral_weight, point_weight, bias.reshape(1, 64), col, fwd, inv, perm)
    return pl.pallas_call(
        finish,
        out_shape=(jax.ShapeDtypeStruct((2, 64, 32, 512), BF), grad_shape),
        in_specs=[any_spec] * 4,
        out_specs=(any_spec, any_spec),
        scratch_shapes=[
            pltpu.VMEM((2, 64, 32, 512), BF),
            pltpu.VMEM((GROUP, 128, 128), BF),
            pltpu.VMEM((128, 512), BF),
            pltpu.VMEM(grad_shape.shape, F32),
            dma((2, 8)),
            dma((6,)),
        ],
        compiler_params=pltpu.CompilerParams(vmem_limit_bytes=60 * 1024 * 1024),
        cost_estimate=pl.CostEstimate(
            flops=600_000_000, bytes_accessed=10_000_000, transcendentals=0
        ),
    )(side, last, col, sgrad)


def solution(mesh):
    in_specs = (
        P("dp", None, "pencil", None),
        P("dp", None, "pencil", None),
        P(None, "pencil", None, None),
        P(),
        P(),
    )
    out_specs = (P("dp", None, "pencil", None), P("dp", "pencil", None, None))
    return jax.shard_map(
        functools.partial(shards, mesh.shape["dp"]),
        mesh=mesh,
        in_specs=in_specs,
        out_specs=out_specs,
        check_vma=False,
    )
```

```python
import functools
import math

import jax
import jax.numpy as jnp
import ml_dtypes
import numpy as np
from jax import lax
from jax.experimental import pallas as pl
from jax.experimental.pallas import tpu as pltpu
from jax.sharding import PartitionSpec as P

TWO_PI = 2.0 * math.pi
MESH = pl.DeviceIdType.MESH
BF = jnp.bfloat16
F32 = jnp.float32
GROUP = 16
TN = (((0,), (0,)), ((), ()))
NT = (((1,), (1,)), ((), ()))
NN = (((1,), (0,)), ((), ()))


def dot(a, b, dims=NN):
    return lax.dot_general(a, b, dims, preferred_element_type=F32)


def tables():
    w = np.arange(512)
    j = np.arange(64).reshape(16, 4)
    phase = (j[:, :, None] * w % 512) * (TWO_PI / 512)
    col = np.stack([np.cos(phase), np.sin(phase)], axis=1).reshape(128, 512)
    k = np.arange(64)
    f = np.where(k < 32, k, 448 + k)
    h = np.arange(512)
    phase = (h[:, None] * f[None, :] % 512) * (TWO_PI / 512)
    ca, sa = np.cos(phase), np.sin(phase)
    r = np.stack([ca, sa], axis=1).reshape(16, 32, 128)
    eye = np.eye(4)
    fwd = np.einsum("shn,cd->schdn", r, eye).reshape(2048, 512)
    first = np.stack([ca, -sa], axis=1)
    second = np.stack([-sa, -ca], axis=1)
    inv = np.stack([first, second], axis=1).reshape(16, 32, 2, 128)
    inv = np.einsum("shqn,cd->cnsqdh", inv, eye).reshape(512, 4096)
    perm = np.einsum("ad,be,cf,t->abtcfed", np.eye(4), np.eye(16), np.eye(4), np.ones(2))
    perm = perm.reshape(512, 256)
    return [np.asarray(t, np.float32).astype(ml_dtypes.bfloat16) for t in (col, fwd, inv, perm)]


def derivative(z):
    e = jnp.exp2((z * z * (-0.5 / math.log(2.0))).astype(BF))
    d = 1.0 + (0.3275911 / math.sqrt(2.0)) * jnp.abs(z)
    t = pl.reciprocal(d.astype(BF), approx=True).astype(BF)
    z = z.astype(BF)
    poly = jnp.full_like(t, 1.061405429 * 0.5)
    for c in (-1.453152027, 1.421413741, -0.284496736, 0.254829592):
        poly = poly * t + jnp.asarray(0.5 * c, BF)
    q = e * (poly * t - jnp.abs(z) * jnp.asarray(1.0 / math.sqrt(TWO_PI), BF))
    return jnp.where(z >= 0, 1 - q, q)


PEERS = tuple((dx, dy, dc) for dx in (1, 0) for dy in (2, 1, 3, 0) for dc in (1, 0))[:-1]


def kernel(
    dps,
    clips, cot, weight, pw, bias, col_h, fwd_h, inv_h, perm_h,
    side, last, sgrad,
    xv, cv, wv, col, fwd, inv, perm,
    send, recv, zs, dz, ya,
    xbf, xb, xbr, gbf, gb, gbr, dd, y3, kf, kb, bcol,
    in_sem, clip_sem, a2a_send, a2a_recv, dp_send, dp_recv,
):
    pen = lax.axis_index("pencil")
    dpi = lax.axis_index("dp")
    per = 512 // dps
    kper = 64 // dps

    def clip_piece(b, n):
        at = pl.ds(n * 8, 8)
        return pltpu.make_async_copy(clips.at[b, at], xv.at[b, at], clip_sem.at[b, n])

    def load(src, dst, pieces, i):
        size = dst.shape[0] // pieces
        for n in range(pieces):
            at = pl.ds(n * size, size)
            pltpu.make_async_copy(src.at[at], dst.at[at], in_sem.at[i]).start()
        return pltpu.make_async_copy(dst, dst, in_sem.at[i]).wait

    col_wait = load(col_h, col, 1, 0)
    for b in range(2):
        for n in range(8):
            clip_piece(b, n).start()

    def peer_of(dx, dy, dc):
        return (pen // 8 + dx) % 2 * 8 + (pen // 2 + dy) % 4 * 2 + (pen + dc) % 2

    barrier = pltpu.get_barrier_semaphore()
    for steps in PEERS:
        peer = {"pencil": peer_of(*steps)}
        pl.semaphore_signal(barrier, inc=1, device_id=peer, device_id_type=MESH)

    def greet_dp(r, carry):
        pl.semaphore_signal(barrier, inc=1, device_id={"dp": (dpi + r) % dps}, device_id_type=MESH)
        return carry

    if dps > 1:
        lax.fori_loop(1, dps, greet_dp, 0)

    lane = lax.broadcasted_iota(jnp.int32, (1, 128), 1)
    low = lane < 64
    sign = jnp.where(low, 1.0, -1.0).astype(F32)

    def slots(b, phase):
        return last if (phase, b) == (3, 1) else recv.at[phase, b]

    def columns(rows, b, phase, n):
        part = dot(col[...], rows, NT)
        pieces = [part[:, i * 128 : (i + 1) * 128].reshape(GROUP, 8, 128) for i in range(2)]
        at = pl.ds(pl.multiple_of(n * 16, 16), 16)
        send[phase, b, :, at, :] = jnp.concatenate(pieces, axis=1).astype(BF)

    def clip_columns(b):
        def step(n, carry):
            clip_piece(b, n).wait()
            columns(xv[b, pl.ds(pl.multiple_of(n * 8, 8), 8)].reshape(256, 512), b, 0, n)
            return carry

        lax.fori_loop(0, 8, step, 0, unroll=2)

    def send_one(b, phase, to):
        pltpu.make_async_remote_copy(
            src_ref=send.at[phase, b, to],
            dst_ref=slots(b, phase).at[pen],
            send_sem=a2a_send.at[phase, b],
            recv_sem=a2a_recv.at[phase, b],
            device_id={"pencil": to},
            device_id_type=MESH,
        ).start()

    def keep_own(b, phase):
        pltpu.make_async_copy(
            send.at[phase, b, pen], slots(b, phase).at[pen], a2a_recv.at[phase, b]
        ).start()

    def scatter(b, phase):
        for steps in PEERS:
            send_one(b, phase, peer_of(*steps))
        keep_own(b, phase)

    def arrived(b, phase):
        whole = slots(b, phase)
        pltpu.make_async_copy(whole, whole, a2a_recv.at[phase, b]).wait()

    def spectrum(b, phase):
        arrived(b, phase)
        lhs = jnp.concatenate([recv[phase, b, s] for s in range(GROUP)], axis=1)
        upper = lax.broadcasted_iota(jnp.int32, (128, 128), 0) % 8 < 4
        pieces = []
        for n in range(2):
            wide = dot(lhs, fwd[:, n * 256 : (n + 1) * 256])
            for i in range(2):
                part = wide[:, i * 128 : (i + 1) * 128]
                sine = pltpu.roll(pltpu.roll(part, 64, 1), 124, 0)
                pieces.append(jnp.where(upper, part * sign - sine, 0.0).astype(BF))
        return dot(jnp.concatenate(pieces, axis=0), perm[...], TN)

    def to_owner(src, dst, i):
        def step(r, carry):
            to = (dpi + r) % dps
            pltpu.make_async_remote_copy(
                src_ref=src.at[to],
                dst_ref=dst.at[dpi],
                send_sem=dp_send.at[i],
                recv_sem=dp_recv.at[i],
                device_id={"dp": to},
                device_id_type=MESH,
            ).start()
            return carry

        if dps > 1:
            lax.fori_loop(1, dps, step, 0)
        pltpu.make_async_copy(src.at[dpi], dst.at[dpi], dp_recv.at[i]).start()

    def rows_back(i, b, phase):
        turned = dot(perm[...], ya[i, b], NT).astype(BF)
        lhs = jnp.concatenate([turned[c * 128 : (c + 1) * 128] for c in range(4)], axis=1)
        upper = lax.broadcasted_iota(jnp.int32, (128, 128), 0) % 8 < 4
        for steps in PEERS + ((0, 0, 0),):
            to = peer_of(*steps)
            lines = dot(lhs, inv[:, pl.ds(pl.multiple_of(to * 256, 256), 256)])
            send[phase, b, to] = jnp.where(upper, lines[:, :128], lines[:, 128:]).astype(BF)
            if steps == (0, 0, 0):
                keep_own(b, phase)
            else:
                send_one(b, phase, to)

    def field(ref, n):
        tile = ref[:, pl.ds(pl.multiple_of(n * 16, 16), 16), :].astype(F32)
        for i in range(2):
            lines = tile[:, i * 8 : (i + 1) * 8].reshape(128, 128).astype(BF)
            yield pl.ds(pl.multiple_of(n * 8 + i * 4, 4), 4), dot(lines, col[...], TN)

    def mix_points(values, b, matrix, add, tiles=(0, 2)):
        def step(t, carry):
            at = pl.multiple_of(t * 16, 16)
            for n in range(2):
                lanes = slice(n * 256, (n + 1) * 256)
                tile = values[b, :, pl.ds(at, 16), lanes].astype(F32)
                parts = []
                for i in range(2):
                    rows = tile[:, i * 8 : (i + 1) * 8].reshape(512, 256).astype(BF)
                    got = dot(matrix[...], rows)
                    if add is not None:
                        got = got + jnp.concatenate([add[...]] * 2, axis=1)
                        to = pl.multiple_of(t * 16 + i * 8, 8)
                        zs[b, :, pl.ds(to, 8), lanes] = got.reshape(64, 8, 256)
                    parts.append(got.reshape(64, 8, 256))
                if add is None:
                    side[b, :, pl.ds(at, 16), lanes] = jnp.concatenate(parts, axis=1).astype(BF)
            return carry

        lax.fori_loop(*tiles, step, 0)

    row16 = lax.broadcasted_iota(jnp.int32, (16, 128), 0)
    scale = jnp.where(pen == 0, 1.0, 2.0).astype(F32) / 262144.0
    scale_lane = jnp.where(jnp.logical_and(low, pen == 0), 1.0, 2.0).astype(F32) / 262144.0

    pairs = kper // 2

    def own_rows(pair):
        return pl.ds(pl.multiple_of(pair % pairs * 16, 16), 16)

    def mix_modes(b):
        spec = spectrum(b, 0).astype(BF).astype(F32)
        for ri in range(2):
            for j in range(4):
                for p in range(2):
                    if p != j // 2:
                        continue
                    part = spec[ri * 64 : (ri + 1) * 64, p * 128 : (p + 1) * 128]
                    part = jnp.where(low if j % 2 == 0 else jnp.logical_not(low), part, 0.0)
                    xbf[p, pl.ds(ri * 4 + j, 64, stride=8), :] = part
        for p in range(2):
            xb[:, b, :, p * 128 : (p + 1) * 128] = xbf[p].astype(BF).reshape(dps, per, 128)

        def step(n, carry):
            for i in range(8):
                pair = n * 8 + i
                at = pl.multiple_of(pair * 16, 16)
                both = jnp.concatenate(
                    [wv[2 * pair].reshape(256, 128), wv[2 * pair + 1].reshape(256, 128)], axis=1
                )
                got = dot(xb[pair // pairs, b, own_rows(pair), :], both)
                y3[pl.ds(at, 8), :] = got[:8, :128]
                y3[pl.ds(at + 8, 8), :] = got[8:, 128:]
            return carry

        lax.fori_loop(0, 4, step, 0)
        modes = []
        for j in range(4):
            real = y3[pl.ds(j, 64, stride=8), :]
            imag = y3[pl.ds(4 + j, 64, stride=8), :]
            mixed = real - sign * pltpu.roll(imag, 64, 1)
            modes.append(mixed * (scale if j == 0 else 2.0 / 262144.0))
        for p in range(2):
            first, second = modes[2 * p], modes[2 * p + 1]
            real = jnp.where(low, first, pltpu.roll(second, 64, 1))
            imag = jnp.where(low, pltpu.roll(first, 64, 1), second)
            ya[0, b, 0:64, p * 128 : (p + 1) * 128] = real.astype(BF)
            ya[0, b, 64:128, p * 128 : (p + 1) * 128] = imag.astype(BF)
        rows_back(0, b, 1)

    def grad_modes(b):
        spec = spectrum(b, 2)
        for p in range(2):
            part = spec[:, p * 128 : (p + 1) * 128]
            part = part * (scale_lane if p == 0 else 2.0 / 262144.0)
            real, imag = part[:64], part[64:]
            real_r, imag_r = pltpu.roll(real, 64, 1), pltpu.roll(imag, 64, 1)
            for i, (re, im) in enumerate(
                ((jnp.where(low, real, imag_r), jnp.where(low, imag, real_r)),
                 (jnp.where(low, real_r, imag), jnp.where(low, imag_r, real)))
            ):
                gbf[pl.ds(2 * p + i, 64, stride=8), :] = re
                gbf[pl.ds(4 + 2 * p + i, 64, stride=8), :] = im * sign
        gb[:, b] = gbf[...].astype(BF).reshape(dps, per, 128)

        def step(n, carry):
            for i in range(8):
                pair = n * 8 + i
                at = pl.multiple_of(pair * 16, 16)
                rhs = wv[pl.ds(2 * pair, 2)].reshape(512, 128)
                got = dot(gb[pair // pairs, b, own_rows(pair), :], rhs, NT)
                for p in range(2):
                    dd[p, pl.ds(at, 8), :] = got[:8, p * 128 : (p + 1) * 128]
                    dd[p, pl.ds(at + 8, 8), :] = got[8:, 256 + p * 128 : 384 + p * 128]
            return carry

        lax.fori_loop(0, 4, step, 0)
        for p in range(2):
            for ri in range(2):
                first = dd[p, pl.ds(ri * 4 + 2 * p, 64, stride=8), :]
                second = dd[p, pl.ds(ri * 4 + 2 * p + 1, 64, stride=8), :]
                ya[1, b, ri * 64 : (ri + 1) * 64, p * 128 : (p + 1) * 128] = jnp.where(
                    low, first, second
                ).astype(BF)
        rows_back(1, b, 3)

    def activation(b, chunks):
        def step(n, carry):
            grads = []
            for at, got in field(recv.at[1, b], n):
                z = got + zs[b, at].reshape(128, 512)
                grads.append(cv[b, at].reshape(128, 512) * derivative(z))
                dz[b, at] = grads[-1].reshape(4, 32, 512)
            columns(jnp.concatenate(grads, axis=0), b, 2, n)
            return carry

        lax.fori_loop(*chunks, step, 0, unroll=2)

    def finish_first():
        arrived(0, 3)

        def step(n, carry):
            for at, got in field(recv.at[3, 0], n):
                got = got + side[0, at].reshape(128, 512).astype(F32)
                side[0, at] = got.astype(BF).reshape(4, 32, 512)
            return carry

        lax.fori_loop(0, 8, step, 0, unroll=2)

    def weight_grad():
        for i, ref in enumerate((xbr, gbr)):
            pltpu.make_async_copy(ref, ref, dp_recv.at[i]).wait()
        first_rows = jnp.where(row16 < 8, 1.0, 0.0).astype(F32)
        for pair in range(pairs):
            at = slice(pair * 16, (pair + 1) * 16)
            left = xbr[:, :, at, :].reshape(2 * dps * 16, 256)
            right = gbr[:, :, at, :].astype(F32)
            head = (right * first_rows).astype(BF).reshape(2 * dps * 16, 128)
            tail = (right * (1.0 - first_rows)).astype(BF).reshape(2 * dps * 16, 128)
            got = dot(left, jnp.concatenate([head, tail], axis=1), TN)
            for i in range(2):
                sgrad[2 * pair + i] = got[:, i * 128 : (i + 1) * 128].reshape(4, 64, 128)

    col_wait()
    clip_columns(0)
    pl.semaphore_wait(barrier, GROUP - 1 + dps - 1)
    scatter(0, 0)
    fwd_wait = load(fwd_h, fwd, 4, 1)
    perm_wait = load(perm_h, perm, 2, 2)
    clip_columns(1)
    scatter(1, 0)
    weight_wait = load(weight, wv, 16, 3)
    inv_wait = load(inv_h, inv, 8, 4)
    cot_waits = [load(cot.at[b], cv.at[b], 8, 5 + b) for b in range(2)]

    row = lax.broadcasted_iota(jnp.int32, (512, 64), 0)
    lanes64 = lax.broadcasted_iota(jnp.int32, (512, 64), 1)
    spread = jnp.where(row // 8 == lanes64, 1.0, 0.0).astype(BF)
    same = (
        lax.broadcasted_iota(jnp.int32, (512, 512), 0) % 8
        == lax.broadcasted_iota(jnp.int32, (512, 512), 1) % 8
    )
    for p in range(2):
        xbf[p] = jnp.zeros((512, 128), F32)
    kf[...] = jnp.where(same, dot(dot(spread, pw[...], NT).astype(BF), spread, NT), 0.0).astype(BF)
    kb[...] = jnp.where(same, dot(dot(spread, pw[...]).astype(BF), spread, NT), 0.0).astype(BF)
    biased = (spread.astype(F32) * bias[...].astype(F32)).astype(BF)
    bcol[...] = dot(biased, jnp.ones((64, 128), BF))
    mix_points(xv, 0, kf, bcol)

    fwd_wait()
    perm_wait()
    inv_wait()
    weight_wait()
    mix_modes(0)
    mix_points(xv, 1, kf, bcol)
    mix_modes(1)
    to_owner(xb, xbr, 0)

    for b in range(2):
        arrived(b, 1)
        cot_waits[b]()
        activation(b, (0, 8))
        scatter(b, 2)
    grad_modes(0)
    mix_points(dz, 0, kb, None, (0, 1))
    grad_modes(1)
    to_owner(gb, gbr, 1)
    mix_points(dz, 0, kb, None, (1, 2))
    mix_points(dz, 1, kb, None)
    finish_first()
    weight_grad()

    for phase in range(4):
        for b in range(2):
            sent = send.at[phase, b, pl.ds(0, GROUP - 1)]
            pltpu.make_async_copy(sent, sent, a2a_send.at[phase, b]).wait()
    if dps > 1:
        for i, ref in enumerate((xb, gb)):
            sent = ref.at[pl.ds(0, dps - 1)]
            pltpu.make_async_copy(sent, sent, dp_send.at[i]).wait()
    arrived(1, 3)


def finish(side, lines, col_h, sgrad, out, weights_out, ov, col, sem):
    col_copy = pltpu.make_async_copy(col_h, col, sem.at[0])
    col_copy.start()
    for n in range(8):
        at = pl.ds(n * 8, 8)
        pltpu.make_async_copy(side.at[0, at], out.at[0, at], sem.at[1]).start()
    away = pltpu.make_async_copy(sgrad, weights_out, sem.at[2])
    away.start()
    col_copy.wait()

    def step(n, carry):
        tile = lines[:, pl.ds(pl.multiple_of(n * 16, 16), 16), :].astype(F32)
        for i in range(2):
            at = pl.ds(pl.multiple_of(n * 8 + i * 4, 4), 4)
            part = tile[:, i * 8 : (i + 1) * 8].reshape(128, 128).astype(BF)
            got = dot(part, col[...], TN) + side[1, at].reshape(128, 512).astype(F32)
            ov[at] = got.astype(BF).reshape(4, 32, 512)
        at = pl.ds(n * 8, 8)
        pltpu.make_async_copy(ov.at[at], out.at[1, at], sem.at[3]).start()
        return carry

    lax.fori_loop(0, 8, step, 0, unroll=2)
    pltpu.make_async_copy(side.at[0], side.at[0], sem.at[1]).wait()
    pltpu.make_async_copy(ov, ov, sem.at[3]).wait()
    away.wait()


def shards(dps, clips, cotangent, spectral_weight, point_weight, bias):
    col, fwd, inv, perm = [jnp.asarray(t) for t in tables()]
    any_spec = pl.BlockSpec(memory_space=pl.ANY)
    vmem = pl.BlockSpec(memory_space=pltpu.VMEM)
    per = 512 // dps
    dma = pltpu.SemaphoreType.DMA
    grad_shape = jax.ShapeDtypeStruct((64 // dps, 4, 64, 128), F32)
    side, last, sgrad = pl.pallas_call(
        functools.partial(kernel, dps),
        out_shape=(
            pltpu.VMEM((2, 64, 32, 512), BF),
            pltpu.VMEM((GROUP, 128, 128), BF),
            pltpu.VMEM(grad_shape.shape, F32),
        ),
        in_specs=[any_spec] * 3 + [vmem] * 2 + [any_spec] * 4,
        out_specs=(vmem, vmem, vmem),
        scratch_shapes=[
            pltpu.VMEM((2, 64, 32, 512), BF),
            pltpu.VMEM((2, 64, 32, 512), BF),
            pltpu.VMEM((64, 4, 64, 128), BF),
            pltpu.VMEM((128, 512), BF),
            pltpu.VMEM((2048, 512), BF),
            pltpu.VMEM((512, 4096), BF),
            pltpu.VMEM((512, 256), BF),
            pltpu.VMEM((4, 2, GROUP, 128, 128), BF),
            pltpu.VMEM((4, 2, GROUP, 128, 128), BF),
            pltpu.VMEM((2, 64, 32, 512), F32),
            pltpu.VMEM((2, 64, 32, 512), BF),
            pltpu.VMEM((2, 2, 128, 256), BF),
            pltpu.VMEM((2, 512, 128), F32),
            pltpu.VMEM((dps, 2, per, 256), BF),
            pltpu.VMEM((dps, 2, per, 256), BF),
            pltpu.VMEM((512, 128), F32),
            pltpu.VMEM((dps, 2, per, 128), BF),
            pltpu.VMEM((dps, 2, per, 128), BF),
            pltpu.VMEM((2, 512, 128), F32),
            pltpu.VMEM((512, 128), F32),
            pltpu.VMEM((512, 512), BF),
            pltpu.VMEM((512, 512), BF),
            pltpu.VMEM((512, 128), F32),
            dma((7,)),
            dma((2, 8)),
            dma((4, 2)),
            dma((4, 2)),
            dma((2,)),
            dma((2,)),
        ],
        compiler_params=pltpu.CompilerParams(
            collective_id=0, has_side_effects=True, vmem_limit_bytes=54 * 1024 * 1024
        ),
        cost_estimate=pl.CostEstimate(
            flops=20_000_000_000, bytes_accessed=20_000_000, transcendentals=4_000_000
        ),
    )(clips, cotangent, spectral_weight, point_weight, bias.reshape(1, 64), col, fwd, inv, perm)
    return pl.pallas_call(
        finish,
        out_shape=(jax.ShapeDtypeStruct((2, 64, 32, 512), BF), grad_shape),
        in_specs=[vmem, vmem, any_spec, vmem],
        out_specs=(any_spec, any_spec),
        scratch_shapes=[
            pltpu.VMEM((64, 32, 512), BF),
            pltpu.VMEM((128, 512), BF),
            dma((4,)),
        ],
        compiler_params=pltpu.CompilerParams(vmem_limit_bytes=16 * 1024 * 1024),
        cost_estimate=pl.CostEstimate(
            flops=600_000_000, bytes_accessed=10_000_000, transcendentals=0
        ),
    )(side, last, col, sgrad)


def solution(mesh):
    in_specs = (
        P("dp", None, "pencil", None),
        P("dp", None, "pencil", None),
        P(None, "pencil", None, None),
        P(),
        P(),
    )
    out_specs = (P("dp", None, "pencil", None), P("dp", "pencil", None, None))
    return jax.shard_map(
        functools.partial(shards, mesh.shape["dp"]),
        mesh=mesh,
        in_specs=in_specs,
        out_specs=out_specs,
        check_vma=False,
    )
```

```python
import functools
import math

import jax
import jax.numpy as jnp
import ml_dtypes
import numpy as np
from jax import lax
from jax.experimental import pallas as pl
from jax.experimental.pallas import tpu as pltpu
from jax.sharding import PartitionSpec as P

TWO_PI = 2.0 * math.pi
MESH = pl.DeviceIdType.MESH
BF = jnp.bfloat16
F32 = jnp.float32
GROUP = 16
TN = (((0,), (0,)), ((), ()))
NT = (((1,), (1,)), ((), ()))
NN = (((1,), (0,)), ((), ()))


def dot(a, b, dims=NN):
    return lax.dot_general(a, b, dims, preferred_element_type=F32)


def tables():
    w = np.arange(512)
    j = np.arange(64).reshape(16, 4)
    phase = (j[:, :, None] * w % 512) * (TWO_PI / 512)
    col = np.stack([np.cos(phase), np.sin(phase)], axis=1).reshape(128, 512)
    k = np.arange(64)
    f = np.where(k < 32, k, 448 + k)
    h = np.arange(512)
    phase = (h[:, None] * f[None, :] % 512) * (TWO_PI / 512)
    ca, sa = np.cos(phase), np.sin(phase)
    r = np.stack([ca, sa], axis=1).reshape(16, 32, 128)
    eye = np.eye(4)
    fwd = np.einsum("shn,cd->schdn", r, eye).reshape(2048, 512)
    first = np.stack([ca, -sa], axis=1)
    second = np.stack([-sa, -ca], axis=1)
    inv = np.stack([first, second], axis=1).reshape(16, 32, 2, 128)
    inv = np.einsum("shqn,cd->cnsqdh", inv, eye).reshape(512, 4096)
    perm = np.einsum("ad,be,cf,t->abtcfed", np.eye(4), np.eye(16), np.eye(4), np.ones(2))
    perm = perm.reshape(512, 256)
    return [np.asarray(t, np.float32).astype(ml_dtypes.bfloat16) for t in (col, fwd, inv, perm)]


def derivative(z):
    e = jnp.exp2((z * z * (-0.5 / math.log(2.0))).astype(BF))
    d = 1.0 + (0.3275911 / math.sqrt(2.0)) * jnp.abs(z)
    t = pl.reciprocal(d.astype(BF), approx=True).astype(BF)
    z = z.astype(BF)
    poly = jnp.full_like(t, 1.061405429 * 0.5)
    for c in (-1.453152027, 1.421413741, -0.284496736, 0.254829592):
        poly = poly * t + jnp.asarray(0.5 * c, BF)
    q = e * (poly * t - jnp.abs(z) * jnp.asarray(1.0 / math.sqrt(TWO_PI), BF))
    return jnp.where(z >= 0, 1 - q, q)


PEERS = (
    (1, 2, 0), (0, 2, 1), (1, 1, 1), (0, 1, 0), (1, 3, 0), (0, 3, 1), (1, 0, 1), (0, 2, 0),
    (1, 2, 1), (0, 1, 1), (1, 1, 0), (0, 3, 0), (1, 3, 1), (0, 0, 1), (1, 0, 0),
)


def kernel(
    dps,
    clips, cot, weight, pw, bias, col_h, fwd_h, inv_h, perm_h,
    side, last, sgrad,
    xv, cv, wv, col, fwd, inv, perm,
    send, recv, zs, dz, ya,
    xbf, xb, xbr, gbf, gb, gbr, dd, y3, kf, kb, bcol,
    in_sem, clip_sem, a2a_send, a2a_recv, dp_send, dp_recv,
):
    pen = lax.axis_index("pencil")
    dpi = lax.axis_index("dp")
    per = 512 // dps
    kper = 64 // dps

    def clip_piece(b, n):
        at = pl.ds(n * 8, 8)
        return pltpu.make_async_copy(clips.at[b, at], xv.at[b, at], clip_sem.at[b, n])

    def load(src, dst, pieces, i):
        size = dst.shape[0] // pieces
        for n in range(pieces):
            at = pl.ds(n * size, size)
            pltpu.make_async_copy(src.at[at], dst.at[at], in_sem.at[i]).start()
        return pltpu.make_async_copy(dst, dst, in_sem.at[i]).wait

    col_wait = load(col_h, col, 1, 0)
    for b in range(2):
        for n in range(8):
            clip_piece(b, n).start()

    def peer_of(dx, dy, dc):
        return (pen // 8 + dx) % 2 * 8 + (pen // 2 + dy) % 4 * 2 + (pen + dc) % 2

    barrier = pltpu.get_barrier_semaphore()
    for steps in PEERS:
        peer = {"pencil": peer_of(*steps)}
        pl.semaphore_signal(barrier, inc=1, device_id=peer, device_id_type=MESH)

    def greet_dp(r, carry):
        pl.semaphore_signal(barrier, inc=1, device_id={"dp": (dpi + r) % dps}, device_id_type=MESH)
        return carry

    if dps > 1:
        lax.fori_loop(1, dps, greet_dp, 0)

    lane = lax.broadcasted_iota(jnp.int32, (1, 128), 1)
    low = lane < 64
    sign = jnp.where(low, 1.0, -1.0).astype(F32)

    def slots(b, phase):
        return last if (phase, b) == (3, 1) else recv.at[phase, b]

    def columns(rows, b, phase, n):
        part = dot(col[...], rows, NT)
        pieces = [part[:, i * 128 : (i + 1) * 128].reshape(GROUP, 8, 128) for i in range(2)]
        at = pl.ds(pl.multiple_of(n * 16, 16), 16)
        send[phase, b, :, at, :] = jnp.concatenate(pieces, axis=1).astype(BF)

    def clip_columns(b):
        def step(n, carry):
            clip_piece(b, n).wait()
            columns(xv[b, pl.ds(pl.multiple_of(n * 8, 8), 8)].reshape(256, 512), b, 0, n)
            return carry

        lax.fori_loop(0, 8, step, 0, unroll=2)

    def send_one(b, phase, to):
        pltpu.make_async_remote_copy(
            src_ref=send.at[phase, b, to],
            dst_ref=slots(b, phase).at[pen],
            send_sem=a2a_send.at[phase, b],
            recv_sem=a2a_recv.at[phase, b],
            device_id={"pencil": to},
            device_id_type=MESH,
        ).start()

    def keep_own(b, phase):
        pltpu.make_async_copy(
            send.at[phase, b, pen], slots(b, phase).at[pen], a2a_recv.at[phase, b]
        ).start()

    def scatter(b, phase):
        for steps in PEERS:
            send_one(b, phase, peer_of(*steps))
        keep_own(b, phase)

    def arrived(b, phase):
        whole = slots(b, phase)
        pltpu.make_async_copy(whole, whole, a2a_recv.at[phase, b]).wait()

    def spectrum(b, phase):
        arrived(b, phase)
        lhs = jnp.concatenate([recv[phase, b, s] for s in range(GROUP)], axis=1)
        upper = lax.broadcasted_iota(jnp.int32, (128, 128), 0) % 8 < 4
        pieces = []
        for n in range(2):
            wide = dot(lhs, fwd[:, n * 256 : (n + 1) * 256])
            for i in range(2):
                part = wide[:, i * 128 : (i + 1) * 128]
                sine = pltpu.roll(pltpu.roll(part, 64, 1), 124, 0)
                pieces.append(jnp.where(upper, part * sign - sine, 0.0).astype(BF))
        return dot(jnp.concatenate(pieces, axis=0), perm[...], TN)

    def to_owner(src, dst, i):
        def step(r, carry):
            to = (dpi + r) % dps
            pltpu.make_async_remote_copy(
                src_ref=src.at[to],
                dst_ref=dst.at[dpi],
                send_sem=dp_send.at[i],
                recv_sem=dp_recv.at[i],
                device_id={"dp": to},
                device_id_type=MESH,
            ).start()
            return carry

        if dps > 1:
            lax.fori_loop(1, dps, step, 0)
        pltpu.make_async_copy(src.at[dpi], dst.at[dpi], dp_recv.at[i]).start()

    def rows_back(i, b, phase):
        turned = dot(perm[...], ya[i, b], NT).astype(BF)
        lhs = jnp.concatenate([turned[c * 128 : (c + 1) * 128] for c in range(4)], axis=1)
        upper = lax.broadcasted_iota(jnp.int32, (128, 128), 0) % 8 < 4
        for steps in PEERS + ((0, 0, 0),):
            to = peer_of(*steps)
            lines = dot(lhs, inv[:, pl.ds(pl.multiple_of(to * 256, 256), 256)])
            send[phase, b, to] = jnp.where(upper, lines[:, :128], lines[:, 128:]).astype(BF)
            if steps == (0, 0, 0):
                keep_own(b, phase)
            else:
                send_one(b, phase, to)

    def field(ref, n):
        tile = ref[:, pl.ds(pl.multiple_of(n * 16, 16), 16), :].astype(F32)
        for i in range(2):
            lines = tile[:, i * 8 : (i + 1) * 8].reshape(128, 128).astype(BF)
            yield pl.ds(pl.multiple_of(n * 8 + i * 4, 4), 4), dot(lines, col[...], TN)

    def mix_points(values, b, matrix, add, tiles=(0, 2)):
        def step(t, carry):
            at = pl.multiple_of(t * 16, 16)
            for n in range(2):
                lanes = slice(n * 256, (n + 1) * 256)
                tile = values[b, :, pl.ds(at, 16), lanes].astype(F32)
                parts = []
                for i in range(2):
                    rows = tile[:, i * 8 : (i + 1) * 8].reshape(512, 256).astype(BF)
                    got = dot(matrix[...], rows)
                    if add is not None:
                        got = got + jnp.concatenate([add[...]] * 2, axis=1)
                        to = pl.multiple_of(t * 16 + i * 8, 8)
                        zs[b, :, pl.ds(to, 8), lanes] = got.reshape(64, 8, 256)
                    parts.append(got.reshape(64, 8, 256))
                if add is None:
                    side[b, :, pl.ds(at, 16), lanes] = jnp.concatenate(parts, axis=1).astype(BF)
            return carry

        lax.fori_loop(*tiles, step, 0)

    row16 = lax.broadcasted_iota(jnp.int32, (16, 128), 0)
    scale = jnp.where(pen == 0, 1.0, 2.0).astype(F32) / 262144.0
    scale_lane = jnp.where(jnp.logical_and(low, pen == 0), 1.0, 2.0).astype(F32) / 262144.0

    pairs = kper // 2

    def own_rows(pair):
        return pl.ds(pl.multiple_of(pair % pairs * 16, 16), 16)

    def mix_modes(b):
        spec = spectrum(b, 0).astype(BF).astype(F32)
        for ri in range(2):
            for j in range(4):
                for p in range(2):
                    if p != j // 2:
                        continue
                    part = spec[ri * 64 : (ri + 1) * 64, p * 128 : (p + 1) * 128]
                    part = jnp.where(low if j % 2 == 0 else jnp.logical_not(low), part, 0.0)
                    xbf[p, pl.ds(ri * 4 + j, 64, stride=8), :] = part
        for p in range(2):
            xb[:, b, :, p * 128 : (p + 1) * 128] = xbf[p].astype(BF).reshape(dps, per, 128)

        def step(n, carry):
            for i in range(8):
                pair = n * 8 + i
                at = pl.multiple_of(pair * 16, 16)
                both = jnp.concatenate(
                    [wv[2 * pair].reshape(256, 128), wv[2 * pair + 1].reshape(256, 128)], axis=1
                )
                got = dot(xb[pair // pairs, b, own_rows(pair), :], both)
                y3[pl.ds(at, 8), :] = got[:8, :128]
                y3[pl.ds(at + 8, 8), :] = got[8:, 128:]
            return carry

        lax.fori_loop(0, 4, step, 0)
        modes = []
        for j in range(4):
            real = y3[pl.ds(j, 64, stride=8), :]
            imag = y3[pl.ds(4 + j, 64, stride=8), :]
            mixed = real - sign * pltpu.roll(imag, 64, 1)
            modes.append(mixed * (scale if j == 0 else 2.0 / 262144.0))
        for p in range(2):
            first, second = modes[2 * p], modes[2 * p + 1]
            real = jnp.where(low, first, pltpu.roll(second, 64, 1))
            imag = jnp.where(low, pltpu.roll(first, 64, 1), second)
            ya[0, b, 0:64, p * 128 : (p + 1) * 128] = real.astype(BF)
            ya[0, b, 64:128, p * 128 : (p + 1) * 128] = imag.astype(BF)
        rows_back(0, b, 1)

    def grad_modes(b):
        spec = spectrum(b, 2)
        for p in range(2):
            part = spec[:, p * 128 : (p + 1) * 128]
            part = part * (scale_lane if p == 0 else 2.0 / 262144.0)
            real, imag = part[:64], part[64:]
            real_r, imag_r = pltpu.roll(real, 64, 1), pltpu.roll(imag, 64, 1)
            for i, (re, im) in enumerate(
                ((jnp.where(low, real, imag_r), jnp.where(low, imag, real_r)),
                 (jnp.where(low, real_r, imag), jnp.where(low, imag_r, real)))
            ):
                gbf[pl.ds(2 * p + i, 64, stride=8), :] = re
                gbf[pl.ds(4 + 2 * p + i, 64, stride=8), :] = im * sign
        gb[:, b] = gbf[...].astype(BF).reshape(dps, per, 128)

        def step(n, carry):
            for i in range(8):
                pair = n * 8 + i
                at = pl.multiple_of(pair * 16, 16)
                rhs = wv[pl.ds(2 * pair, 2)].reshape(512, 128)
                got = dot(gb[pair // pairs, b, own_rows(pair), :], rhs, NT)
                for p in range(2):
                    dd[p, pl.ds(at, 8), :] = got[:8, p * 128 : (p + 1) * 128]
                    dd[p, pl.ds(at + 8, 8), :] = got[8:, 256 + p * 128 : 384 + p * 128]
            return carry

        lax.fori_loop(0, 4, step, 0)
        for p in range(2):
            for ri in range(2):
                first = dd[p, pl.ds(ri * 4 + 2 * p, 64, stride=8), :]
                second = dd[p, pl.ds(ri * 4 + 2 * p + 1, 64, stride=8), :]
                ya[1, b, ri * 64 : (ri + 1) * 64, p * 128 : (p + 1) * 128] = jnp.where(
                    low, first, second
                ).astype(BF)
        rows_back(1, b, 3)

    def activation(b, chunks):
        def step(n, carry):
            grads = []
            for at, got in field(recv.at[1, b], n):
                z = got + zs[b, at].reshape(128, 512)
                grads.append(cv[b, at].reshape(128, 512) * derivative(z))
                dz[b, at] = grads[-1].reshape(4, 32, 512)
            columns(jnp.concatenate(grads, axis=0), b, 2, n)
            return carry

        lax.fori_loop(*chunks, step, 0, unroll=2)

    def finish_first():
        arrived(0, 3)

        def step(n, carry):
            for at, got in field(recv.at[3, 0], n):
                got = got + side[0, at].reshape(128, 512).astype(F32)
                side[0, at] = got.astype(BF).reshape(4, 32, 512)
            return carry

        lax.fori_loop(0, 8, step, 0, unroll=2)

    def weight_grad():
        for i, ref in enumerate((xbr, gbr)):
            pltpu.make_async_copy(ref, ref, dp_recv.at[i]).wait()
        first_rows = jnp.where(row16 < 8, 1.0, 0.0).astype(F32)
        for pair in range(pairs):
            at = slice(pair * 16, (pair + 1) * 16)
            left = xbr[:, :, at, :].reshape(2 * dps * 16, 256)
            right = gbr[:, :, at, :].astype(F32)
            head = (right * first_rows).astype(BF).reshape(2 * dps * 16, 128)
            tail = (right * (1.0 - first_rows)).astype(BF).reshape(2 * dps * 16, 128)
            got = dot(left, jnp.concatenate([head, tail], axis=1), TN)
            for i in range(2):
                sgrad[2 * pair + i] = got[:, i * 128 : (i + 1) * 128].reshape(4, 64, 128)

    col_wait()
    clip_columns(0)
    pl.semaphore_wait(barrier, GROUP - 1 + dps - 1)
    scatter(0, 0)
    fwd_wait = load(fwd_h, fwd, 4, 1)
    perm_wait = load(perm_h, perm, 2, 2)
    clip_columns(1)
    scatter(1, 0)
    weight_wait = load(weight, wv, 16, 3)
    inv_wait = load(inv_h, inv, 8, 4)
    cot_waits = [load(cot.at[b], cv.at[b], 8, 5 + b) for b in range(2)]

    row = lax.broadcasted_iota(jnp.int32, (512, 64), 0)
    lanes64 = lax.broadcasted_iota(jnp.int32, (512, 64), 1)
    spread = jnp.where(row // 8 == lanes64, 1.0, 0.0).astype(BF)
    same = (
        lax.broadcasted_iota(jnp.int32, (512, 512), 0) % 8
        == lax.broadcasted_iota(jnp.int32, (512, 512), 1) % 8
    )
    for p in range(2):
        xbf[p] = jnp.zeros((512, 128), F32)
    kf[...] = jnp.where(same, dot(dot(spread, pw[...], NT).astype(BF), spread, NT), 0.0).astype(BF)
    kb[...] = jnp.where(same, dot(dot(spread, pw[...]).astype(BF), spread, NT), 0.0).astype(BF)
    biased = (spread.astype(F32) * bias[...].astype(F32)).astype(BF)
    bcol[...] = dot(biased, jnp.ones((64, 128), BF))
    mix_points(xv, 0, kf, bcol)

    fwd_wait()
    perm_wait()
    inv_wait()
    weight_wait()
    mix_modes(0)
    mix_points(xv, 1, kf, bcol)
    mix_modes(1)
    to_owner(xb, xbr, 0)

    for b in range(2):
        arrived(b, 1)
        cot_waits[b]()
        activation(b, (0, 8))
        scatter(b, 2)
    grad_modes(0)
    mix_points(dz, 0, kb, None, (0, 1))
    grad_modes(1)
    to_owner(gb, gbr, 1)
    mix_points(dz, 0, kb, None, (1, 2))
    mix_points(dz, 1, kb, None)
    finish_first()
    weight_grad()

    for phase in range(4):
        for b in range(2):
            sent = send.at[phase, b, pl.ds(0, GROUP - 1)]
            pltpu.make_async_copy(sent, sent, a2a_send.at[phase, b]).wait()
    if dps > 1:
        for i, ref in enumerate((xb, gb)):
            sent = ref.at[pl.ds(0, dps - 1)]
            pltpu.make_async_copy(sent, sent, dp_send.at[i]).wait()
    arrived(1, 3)


def finish(side, lines, col_h, sgrad, out, weights_out, ov, col, sem):
    col_copy = pltpu.make_async_copy(col_h, col, sem.at[0])
    col_copy.start()
    for n in range(8):
        at = pl.ds(n * 8, 8)
        pltpu.make_async_copy(side.at[0, at], out.at[0, at], sem.at[1]).start()
    away = pltpu.make_async_copy(sgrad, weights_out, sem.at[2])
    away.start()
    col_copy.wait()

    def step(n, carry):
        tile = lines[:, pl.ds(pl.multiple_of(n * 16, 16), 16), :].astype(F32)
        for i in range(2):
            at = pl.ds(pl.multiple_of(n * 8 + i * 4, 4), 4)
            part = tile[:, i * 8 : (i + 1) * 8].reshape(128, 128).astype(BF)
            got = dot(part, col[...], TN) + side[1, at].reshape(128, 512).astype(F32)
            ov[at] = got.astype(BF).reshape(4, 32, 512)
        at = pl.ds(n * 8, 8)
        pltpu.make_async_copy(ov.at[at], out.at[1, at], sem.at[3]).start()
        return carry

    lax.fori_loop(0, 8, step, 0, unroll=2)
    pltpu.make_async_copy(side.at[0], side.at[0], sem.at[1]).wait()
    pltpu.make_async_copy(ov, ov, sem.at[3]).wait()
    away.wait()


def shards(dps, clips, cotangent, spectral_weight, point_weight, bias):
    col, fwd, inv, perm = [jnp.asarray(t) for t in tables()]
    any_spec = pl.BlockSpec(memory_space=pl.ANY)
    vmem = pl.BlockSpec(memory_space=pltpu.VMEM)
    per = 512 // dps
    dma = pltpu.SemaphoreType.DMA
    grad_shape = jax.ShapeDtypeStruct((64 // dps, 4, 64, 128), F32)
    side, last, sgrad = pl.pallas_call(
        functools.partial(kernel, dps),
        out_shape=(
            pltpu.VMEM((2, 64, 32, 512), BF),
            pltpu.VMEM((GROUP, 128, 128), BF),
            pltpu.VMEM(grad_shape.shape, F32),
        ),
        in_specs=[any_spec] * 3 + [vmem] * 2 + [any_spec] * 4,
        out_specs=(vmem, vmem, vmem),
        scratch_shapes=[
            pltpu.VMEM((2, 64, 32, 512), BF),
            pltpu.VMEM((2, 64, 32, 512), BF),
            pltpu.VMEM((64, 4, 64, 128), BF),
            pltpu.VMEM((128, 512), BF),
            pltpu.VMEM((2048, 512), BF),
            pltpu.VMEM((512, 4096), BF),
            pltpu.VMEM((512, 256), BF),
            pltpu.VMEM((4, 2, GROUP, 128, 128), BF),
            pltpu.VMEM((4, 2, GROUP, 128, 128), BF),
            pltpu.VMEM((2, 64, 32, 512), F32),
            pltpu.VMEM((2, 64, 32, 512), BF),
            pltpu.VMEM((2, 2, 128, 256), BF),
            pltpu.VMEM((2, 512, 128), F32),
            pltpu.VMEM((dps, 2, per, 256), BF),
            pltpu.VMEM((dps, 2, per, 256), BF),
            pltpu.VMEM((512, 128), F32),
            pltpu.VMEM((dps, 2, per, 128), BF),
            pltpu.VMEM((dps, 2, per, 128), BF),
            pltpu.VMEM((2, 512, 128), F32),
            pltpu.VMEM((512, 128), F32),
            pltpu.VMEM((512, 512), BF),
            pltpu.VMEM((512, 512), BF),
            pltpu.VMEM((512, 128), F32),
            dma((7,)),
            dma((2, 8)),
            dma((4, 2)),
            dma((4, 2)),
            dma((2,)),
            dma((2,)),
        ],
        compiler_params=pltpu.CompilerParams(
            collective_id=0, has_side_effects=True, vmem_limit_bytes=54 * 1024 * 1024
        ),
        cost_estimate=pl.CostEstimate(
            flops=20_000_000_000, bytes_accessed=20_000_000, transcendentals=4_000_000
        ),
    )(clips, cotangent, spectral_weight, point_weight, bias.reshape(1, 64), col, fwd, inv, perm)
    return pl.pallas_call(
        finish,
        out_shape=(jax.ShapeDtypeStruct((2, 64, 32, 512), BF), grad_shape),
        in_specs=[vmem, vmem, any_spec, vmem],
        out_specs=(any_spec, any_spec),
        scratch_shapes=[
            pltpu.VMEM((64, 32, 512), BF),
            pltpu.VMEM((128, 512), BF),
            dma((4,)),
        ],
        compiler_params=pltpu.CompilerParams(vmem_limit_bytes=16 * 1024 * 1024),
        cost_estimate=pl.CostEstimate(
            flops=600_000_000, bytes_accessed=10_000_000, transcendentals=0
        ),
    )(side, last, col, sgrad)


def solution(mesh):
    in_specs = (
        P("dp", None, "pencil", None),
        P("dp", None, "pencil", None),
        P(None, "pencil", None, None),
        P(),
        P(),
    )
    out_specs = (P("dp", None, "pencil", None), P("dp", "pencil", None, None))
    return jax.shard_map(
        functools.partial(shards, mesh.shape["dp"]),
        mesh=mesh,
        in_specs=in_specs,
        out_specs=out_specs,
        check_vma=False,
    )
```

```python
import functools
import math

import jax
import jax.numpy as jnp
import ml_dtypes
import numpy as np
from jax import lax
from jax.experimental import pallas as pl
from jax.experimental.pallas import tpu as pltpu
from jax.sharding import PartitionSpec as P

TWO_PI = 2.0 * math.pi
MESH = pl.DeviceIdType.MESH
BF = jnp.bfloat16
F32 = jnp.float32
GROUP = 16
TN = (((0,), (0,)), ((), ()))
NT = (((1,), (1,)), ((), ()))
NN = (((1,), (0,)), ((), ()))


def dot(a, b, dims=NN):
    return lax.dot_general(a, b, dims, preferred_element_type=F32)


def tables():
    w = np.arange(512)
    j = np.arange(64).reshape(16, 4)
    phase = (j[:, :, None] * w % 512) * (TWO_PI / 512)
    col = np.stack([np.cos(phase), np.sin(phase)], axis=1).reshape(128, 512)
    k = np.arange(64)
    f = np.where(k < 32, k, 448 + k)
    h = np.arange(512)
    phase = (h[:, None] * f[None, :] % 512) * (TWO_PI / 512)
    ca, sa = np.cos(phase), np.sin(phase)
    r = np.stack([ca, sa], axis=1).reshape(16, 32, 128)
    eye = np.eye(4)
    fwd = np.einsum("shn,cd->schdn", r, eye).reshape(2048, 512)
    first = np.stack([ca, -sa], axis=1)
    second = np.stack([-sa, -ca], axis=1)
    inv = np.stack([first, second], axis=1).reshape(16, 32, 2, 128)
    inv = np.einsum("shqn,cd->cnsqdh", inv, eye).reshape(512, 4096)
    perm = np.einsum("ad,be,cf,t->abtcfed", np.eye(4), np.eye(16), np.eye(4), np.ones(2))
    perm = perm.reshape(512, 256)
    return [np.asarray(t, np.float32).astype(ml_dtypes.bfloat16) for t in (col, fwd, inv, perm)]


def derivative(z):
    e = jnp.exp2((z * z * (-0.5 / math.log(2.0))).astype(BF))
    d = 1.0 + (0.3275911 / math.sqrt(2.0)) * jnp.abs(z)
    t = pl.reciprocal(d.astype(BF), approx=True).astype(BF)
    z = z.astype(BF)
    poly = jnp.full_like(t, 1.061405429 * 0.5)
    for c in (-1.453152027, 1.421413741, -0.284496736, 0.254829592):
        poly = poly * t + jnp.asarray(0.5 * c, BF)
    q = e * (poly * t - jnp.abs(z) * jnp.asarray(1.0 / math.sqrt(TWO_PI), BF))
    return jnp.where(z >= 0, 1 - q, q)


PEERS = (
    (1, 2, 0), (0, 2, 1), (1, 1, 1), (0, 1, 0), (1, 3, 0), (0, 3, 1), (1, 0, 1), (0, 2, 0),
    (1, 2, 1), (0, 1, 1), (1, 1, 0), (0, 3, 0), (1, 3, 1), (0, 0, 1), (1, 0, 0),
)


def kernel(
    dps,
    clips, cot, weight, pw, bias, col_h, fwd_h, inv_h, perm_h,
    side, last, sgrad,
    xv, cv, wv, col, fwd, inv, perm,
    send, recv, zs, dz, ya,
    xbf, xb, xbr, gbf, gb, gbr, dd, y3, kf, kb, bcol,
    in_sem, clip_sem, a2a_send, a2a_recv, dp_send, dp_recv,
):
    pen = lax.axis_index("pencil")
    dpi = lax.axis_index("dp")
    per = 512 // dps
    kper = 64 // dps

    def clip_piece(b, n):
        at = pl.ds(n * 8, 8)
        return pltpu.make_async_copy(clips.at[b, at], xv.at[b, at], clip_sem.at[b, n])

    def load(src, dst, pieces, i):
        size = dst.shape[0] // pieces
        for n in range(pieces):
            at = pl.ds(n * size, size)
            pltpu.make_async_copy(src.at[at], dst.at[at], in_sem.at[i]).start()
        return pltpu.make_async_copy(dst, dst, in_sem.at[i]).wait

    col_wait = load(col_h, col, 1, 0)
    for b in range(2):
        for n in range(8):
            clip_piece(b, n).start()

    def peer_of(dx, dy, dc):
        return (pen // 8 + dx) % 2 * 8 + (pen // 2 + dy) % 4 * 2 + (pen + dc) % 2

    barrier = pltpu.get_barrier_semaphore()
    for steps in PEERS:
        peer = {"pencil": peer_of(*steps)}
        pl.semaphore_signal(barrier, inc=1, device_id=peer, device_id_type=MESH)

    def greet_dp(r, carry):
        pl.semaphore_signal(barrier, inc=1, device_id={"dp": (dpi + r) % dps}, device_id_type=MESH)
        return carry

    if dps > 1:
        lax.fori_loop(1, dps, greet_dp, 0)

    lane = lax.broadcasted_iota(jnp.int32, (1, 128), 1)
    low = lane < 64
    sign = jnp.where(low, 1.0, -1.0).astype(F32)

    def slots(b, phase):
        return last if (phase, b) == (3, 1) else recv.at[phase, b]

    def columns(rows, b, phase, n):
        part = dot(col[...], rows, NT)
        pieces = [part[:, i * 128 : (i + 1) * 128].reshape(GROUP, 8, 128) for i in range(2)]
        at = pl.ds(pl.multiple_of(n * 16, 16), 16)
        send[phase, b, :, at, :] = jnp.concatenate(pieces, axis=1).astype(BF)

    def clip_columns(b):
        def step(n, carry):
            clip_piece(b, n).wait()
            columns(xv[b, pl.ds(pl.multiple_of(n * 8, 8), 8)].reshape(256, 512), b, 0, n)
            return carry

        lax.fori_loop(0, 8, step, 0, unroll=2)

    def send_one(b, phase, to, rows=pl.ds(0, 128)):
        pltpu.make_async_remote_copy(
            src_ref=send.at[phase, b, to, rows],
            dst_ref=slots(b, phase).at[pen, rows],
            send_sem=a2a_send.at[phase, b],
            recv_sem=a2a_recv.at[phase, b],
            device_id={"pencil": to},
            device_id_type=MESH,
        ).start()

    def keep_own(b, phase):
        pltpu.make_async_copy(
            send.at[phase, b, pen], slots(b, phase).at[pen], a2a_recv.at[phase, b]
        ).start()

    def scatter(b, phase):
        for steps in PEERS:
            send_one(b, phase, peer_of(*steps))
        keep_own(b, phase)

    def arrived(b, phase):
        whole = slots(b, phase)
        pltpu.make_async_copy(whole, whole, a2a_recv.at[phase, b]).wait()

    def spectrum(b, phase):
        arrived(b, phase)
        lhs = jnp.concatenate([recv[phase, b, s] for s in range(GROUP)], axis=1)
        upper = lax.broadcasted_iota(jnp.int32, (128, 128), 0) % 8 < 4
        pieces = []
        for n in range(2):
            wide = dot(lhs, fwd[:, n * 256 : (n + 1) * 256])
            for i in range(2):
                part = wide[:, i * 128 : (i + 1) * 128]
                sine = pltpu.roll(pltpu.roll(part, 64, 1), 124, 0)
                pieces.append(jnp.where(upper, part * sign - sine, 0.0).astype(BF))
        return dot(jnp.concatenate(pieces, axis=0), perm[...], TN)

    def to_owner(src, dst, i):
        def step(r, carry):
            to = (dpi + r) % dps
            pltpu.make_async_remote_copy(
                src_ref=src.at[to],
                dst_ref=dst.at[dpi],
                send_sem=dp_send.at[i],
                recv_sem=dp_recv.at[i],
                device_id={"dp": to},
                device_id_type=MESH,
            ).start()
            return carry

        if dps > 1:
            lax.fori_loop(1, dps, step, 0)
        pltpu.make_async_copy(src.at[dpi], dst.at[dpi], dp_recv.at[i]).start()

    def rows_back(i, b, phase):
        turned = dot(perm[...], ya[i, b], NT).astype(BF)
        lhs = jnp.concatenate([turned[c * 128 : (c + 1) * 128] for c in range(4)], axis=1)
        upper = lax.broadcasted_iota(jnp.int32, (128, 128), 0) % 8 < 4
        for steps in PEERS + ((0, 0, 0),):
            to = peer_of(*steps)
            lines = dot(lhs, inv[:, pl.ds(pl.multiple_of(to * 256, 256), 256)])
            send[phase, b, to] = jnp.where(upper, lines[:, :128], lines[:, 128:]).astype(BF)
            if steps == (0, 0, 0):
                keep_own(b, phase)
            else:
                send_one(b, phase, to)

    def field(ref, n):
        tile = ref[:, pl.ds(pl.multiple_of(n * 16, 16), 16), :].astype(F32)
        for i in range(2):
            lines = tile[:, i * 8 : (i + 1) * 8].reshape(128, 128).astype(BF)
            yield pl.ds(pl.multiple_of(n * 8 + i * 4, 4), 4), dot(lines, col[...], TN)

    def mix_points(values, b, matrix, add, tiles=(0, 2)):
        def step(t, carry):
            at = pl.multiple_of(t * 16, 16)
            for n in range(2):
                lanes = slice(n * 256, (n + 1) * 256)
                tile = values[b, :, pl.ds(at, 16), lanes].astype(F32)
                parts = []
                for i in range(2):
                    rows = tile[:, i * 8 : (i + 1) * 8].reshape(512, 256).astype(BF)
                    got = dot(matrix[...], rows)
                    if add is not None:
                        got = got + jnp.concatenate([add[...]] * 2, axis=1)
                        to = pl.multiple_of(t * 16 + i * 8, 8)
                        zs[b, :, pl.ds(to, 8), lanes] = got.reshape(64, 8, 256)
                    parts.append(got.reshape(64, 8, 256))
                if add is None:
                    side[b, :, pl.ds(at, 16), lanes] = jnp.concatenate(parts, axis=1).astype(BF)
            return carry

        lax.fori_loop(*tiles, step, 0)

    row16 = lax.broadcasted_iota(jnp.int32, (16, 128), 0)
    scale = jnp.where(pen == 0, 1.0, 2.0).astype(F32) / 262144.0
    scale_lane = jnp.where(jnp.logical_and(low, pen == 0), 1.0, 2.0).astype(F32) / 262144.0

    pairs = kper // 2

    def own_rows(pair):
        return pl.ds(pl.multiple_of(pair % pairs * 16, 16), 16)

    def mix_modes(b):
        spec = spectrum(b, 0).astype(BF).astype(F32)
        for ri in range(2):
            for j in range(4):
                for p in range(2):
                    if p != j // 2:
                        continue
                    part = spec[ri * 64 : (ri + 1) * 64, p * 128 : (p + 1) * 128]
                    part = jnp.where(low if j % 2 == 0 else jnp.logical_not(low), part, 0.0)
                    xbf[p, pl.ds(ri * 4 + j, 64, stride=8), :] = part
        for p in range(2):
            xb[:, b, :, p * 128 : (p + 1) * 128] = xbf[p].astype(BF).reshape(dps, per, 128)

        def step(n, carry):
            for i in range(8):
                pair = n * 8 + i
                at = pl.multiple_of(pair * 16, 16)
                both = jnp.concatenate(
                    [wv[2 * pair].reshape(256, 128), wv[2 * pair + 1].reshape(256, 128)], axis=1
                )
                got = dot(xb[pair // pairs, b, own_rows(pair), :], both)
                y3[pl.ds(at, 8), :] = got[:8, :128]
                y3[pl.ds(at + 8, 8), :] = got[8:, 128:]
            return carry

        lax.fori_loop(0, 4, step, 0)
        modes = []
        for j in range(4):
            real = y3[pl.ds(j, 64, stride=8), :]
            imag = y3[pl.ds(4 + j, 64, stride=8), :]
            mixed = real - sign * pltpu.roll(imag, 64, 1)
            modes.append(mixed * (scale if j == 0 else 2.0 / 262144.0))
        for p in range(2):
            first, second = modes[2 * p], modes[2 * p + 1]
            real = jnp.where(low, first, pltpu.roll(second, 64, 1))
            imag = jnp.where(low, pltpu.roll(first, 64, 1), second)
            ya[0, b, 0:64, p * 128 : (p + 1) * 128] = real.astype(BF)
            ya[0, b, 64:128, p * 128 : (p + 1) * 128] = imag.astype(BF)
        rows_back(0, b, 1)

    def grad_modes(b):
        spec = spectrum(b, 2)
        for p in range(2):
            part = spec[:, p * 128 : (p + 1) * 128]
            part = part * (scale_lane if p == 0 else 2.0 / 262144.0)
            real, imag = part[:64], part[64:]
            real_r, imag_r = pltpu.roll(real, 64, 1), pltpu.roll(imag, 64, 1)
            for i, (re, im) in enumerate(
                ((jnp.where(low, real, imag_r), jnp.where(low, imag, real_r)),
                 (jnp.where(low, real_r, imag), jnp.where(low, imag_r, real)))
            ):
                gbf[pl.ds(2 * p + i, 64, stride=8), :] = re
                gbf[pl.ds(4 + 2 * p + i, 64, stride=8), :] = im * sign
        gb[:, b] = gbf[...].astype(BF).reshape(dps, per, 128)

        def step(n, carry):
            for i in range(8):
                pair = n * 8 + i
                at = pl.multiple_of(pair * 16, 16)
                rhs = wv[pl.ds(2 * pair, 2)].reshape(512, 128)
                got = dot(gb[pair // pairs, b, own_rows(pair), :], rhs, NT)
                for p in range(2):
                    dd[p, pl.ds(at, 8), :] = got[:8, p * 128 : (p + 1) * 128]
                    dd[p, pl.ds(at + 8, 8), :] = got[8:, 256 + p * 128 : 384 + p * 128]
            return carry

        lax.fori_loop(0, 4, step, 0)
        for p in range(2):
            for ri in range(2):
                first = dd[p, pl.ds(ri * 4 + 2 * p, 64, stride=8), :]
                second = dd[p, pl.ds(ri * 4 + 2 * p + 1, 64, stride=8), :]
                ya[1, b, ri * 64 : (ri + 1) * 64, p * 128 : (p + 1) * 128] = jnp.where(
                    low, first, second
                ).astype(BF)
        rows_back(1, b, 3)

    def activation(b, chunks):
        def step(n, carry):
            grads = []
            for at, got in field(recv.at[1, b], n):
                z = got + zs[b, at].reshape(128, 512)
                grads.append(cv[b, at].reshape(128, 512) * derivative(z))
                dz[b, at] = grads[-1].reshape(4, 32, 512)
            columns(jnp.concatenate(grads, axis=0), b, 2, n)
            return carry

        lax.fori_loop(*chunks, step, 0, unroll=2)

    def finish_first():
        arrived(0, 3)

        def step(n, carry):
            for at, got in field(recv.at[3, 0], n):
                got = got + side[0, at].reshape(128, 512).astype(F32)
                side[0, at] = got.astype(BF).reshape(4, 32, 512)
            return carry

        lax.fori_loop(0, 8, step, 0, unroll=2)

    def weight_grad():
        for i, ref in enumerate((xbr, gbr)):
            pltpu.make_async_copy(ref, ref, dp_recv.at[i]).wait()
        first_rows = jnp.where(row16 < 8, 1.0, 0.0).astype(F32)
        for pair in range(pairs):
            at = slice(pair * 16, (pair + 1) * 16)
            left = xbr[:, :, at, :].reshape(2 * dps * 16, 256)
            right = gbr[:, :, at, :].astype(F32)
            head = (right * first_rows).astype(BF).reshape(2 * dps * 16, 128)
            tail = (right * (1.0 - first_rows)).astype(BF).reshape(2 * dps * 16, 128)
            got = dot(left, jnp.concatenate([head, tail], axis=1), TN)
            for i in range(2):
                sgrad[2 * pair + i] = got[:, i * 128 : (i + 1) * 128].reshape(4, 64, 128)

    col_wait()
    clip_columns(0)
    pl.semaphore_wait(barrier, GROUP - 1 + dps - 1)
    scatter(0, 0)
    fwd_wait = load(fwd_h, fwd, 4, 1)
    perm_wait = load(perm_h, perm, 2, 2)
    clip_columns(1)
    scatter(1, 0)
    weight_wait = load(weight, wv, 16, 3)
    inv_wait = load(inv_h, inv, 8, 4)
    cot_waits = [load(cot.at[b], cv.at[b], 8, 5 + b) for b in range(2)]

    row = lax.broadcasted_iota(jnp.int32, (512, 64), 0)
    lanes64 = lax.broadcasted_iota(jnp.int32, (512, 64), 1)
    spread = jnp.where(row // 8 == lanes64, 1.0, 0.0).astype(BF)
    same = (
        lax.broadcasted_iota(jnp.int32, (512, 512), 0) % 8
        == lax.broadcasted_iota(jnp.int32, (512, 512), 1) % 8
    )
    for p in range(2):
        xbf[p] = jnp.zeros((512, 128), F32)
    kf[...] = jnp.where(same, dot(dot(spread, pw[...], NT).astype(BF), spread, NT), 0.0).astype(BF)
    kb[...] = jnp.where(same, dot(dot(spread, pw[...]).astype(BF), spread, NT), 0.0).astype(BF)
    biased = (spread.astype(F32) * bias[...].astype(F32)).astype(BF)
    bcol[...] = dot(biased, jnp.ones((64, 128), BF))
    mix_points(xv, 0, kf, bcol)

    fwd_wait()
    perm_wait()
    inv_wait()
    weight_wait()
    mix_modes(0)
    mix_modes(1)
    mix_points(xv, 1, kf, bcol)

    cot_waits[0]()
    arrived(0, 1)
    activation(0, (0, 8))
    scatter(0, 2)
    to_owner(xb, xbr, 0)
    cot_waits[1]()
    arrived(1, 1)
    for n in range(2):
        activation(1, (4 * n, 4 * n + 4))
        for steps in PEERS:
            send_one(1, 2, peer_of(*steps), pl.ds(n * 64, 64))
    keep_own(1, 2)
    grad_modes(0)
    mix_points(dz, 0, kb, None, (0, 1))
    grad_modes(1)
    to_owner(gb, gbr, 1)
    mix_points(dz, 0, kb, None, (1, 2))
    mix_points(dz, 1, kb, None)
    finish_first()
    weight_grad()

    for phase in range(4):
        for b in range(2):
            sent = send.at[phase, b, pl.ds(0, GROUP - 1)]
            pltpu.make_async_copy(sent, sent, a2a_send.at[phase, b]).wait()
    if dps > 1:
        for i, ref in enumerate((xb, gb)):
            sent = ref.at[pl.ds(0, dps - 1)]
            pltpu.make_async_copy(sent, sent, dp_send.at[i]).wait()
    arrived(1, 3)


def finish(side, lines, col_h, sgrad, out, weights_out, ov, col, sem):
    col_copy = pltpu.make_async_copy(col_h, col, sem.at[0])
    col_copy.start()
    for n in range(8):
        at = pl.ds(n * 8, 8)
        pltpu.make_async_copy(side.at[0, at], out.at[0, at], sem.at[1]).start()
    away = pltpu.make_async_copy(sgrad, weights_out, sem.at[2])
    away.start()
    col_copy.wait()

    def step(n, carry):
        tile = lines[:, pl.ds(pl.multiple_of(n * 16, 16), 16), :].astype(F32)
        for i in range(2):
            at = pl.ds(pl.multiple_of(n * 8 + i * 4, 4), 4)
            part = tile[:, i * 8 : (i + 1) * 8].reshape(128, 128).astype(BF)
            got = dot(part, col[...], TN) + side[1, at].reshape(128, 512).astype(F32)
            ov[at] = got.astype(BF).reshape(4, 32, 512)
        at = pl.ds(n * 8, 8)
        pltpu.make_async_copy(ov.at[at], out.at[1, at], sem.at[3]).start()
        return carry

    lax.fori_loop(0, 8, step, 0, unroll=2)
    pltpu.make_async_copy(side.at[0], side.at[0], sem.at[1]).wait()
    pltpu.make_async_copy(ov, ov, sem.at[3]).wait()
    away.wait()


def shards(dps, clips, cotangent, spectral_weight, point_weight, bias):
    col, fwd, inv, perm = [jnp.asarray(t) for t in tables()]
    any_spec = pl.BlockSpec(memory_space=pl.ANY)
    vmem = pl.BlockSpec(memory_space=pltpu.VMEM)
    per = 512 // dps
    dma = pltpu.SemaphoreType.DMA
    grad_shape = jax.ShapeDtypeStruct((64 // dps, 4, 64, 128), F32)
    side, last, sgrad = pl.pallas_call(
        functools.partial(kernel, dps),
        out_shape=(
            pltpu.VMEM((2, 64, 32, 512), BF),
            pltpu.VMEM((GROUP, 128, 128), BF),
            pltpu.VMEM(grad_shape.shape, F32),
        ),
        in_specs=[any_spec] * 3 + [vmem] * 2 + [any_spec] * 4,
        out_specs=(vmem, vmem, vmem),
        scratch_shapes=[
            pltpu.VMEM((2, 64, 32, 512), BF),
            pltpu.VMEM((2, 64, 32, 512), BF),
            pltpu.VMEM((64, 4, 64, 128), BF),
            pltpu.VMEM((128, 512), BF),
            pltpu.VMEM((2048, 512), BF),
            pltpu.VMEM((512, 4096), BF),
            pltpu.VMEM((512, 256), BF),
            pltpu.VMEM((4, 2, GROUP, 128, 128), BF),
            pltpu.VMEM((4, 2, GROUP, 128, 128), BF),
            pltpu.VMEM((2, 64, 32, 512), F32),
            pltpu.VMEM((2, 64, 32, 512), BF),
            pltpu.VMEM((2, 2, 128, 256), BF),
            pltpu.VMEM((2, 512, 128), F32),
            pltpu.VMEM((dps, 2, per, 256), BF),
            pltpu.VMEM((dps, 2, per, 256), BF),
            pltpu.VMEM((512, 128), F32),
            pltpu.VMEM((dps, 2, per, 128), BF),
            pltpu.VMEM((dps, 2, per, 128), BF),
            pltpu.VMEM((2, 512, 128), F32),
            pltpu.VMEM((512, 128), F32),
            pltpu.VMEM((512, 512), BF),
            pltpu.VMEM((512, 512), BF),
            pltpu.VMEM((512, 128), F32),
            dma((7,)),
            dma((2, 8)),
            dma((4, 2)),
            dma((4, 2)),
            dma((2,)),
            dma((2,)),
        ],
        compiler_params=pltpu.CompilerParams(
            collective_id=0, has_side_effects=True, vmem_limit_bytes=54 * 1024 * 1024
        ),
        cost_estimate=pl.CostEstimate(
            flops=20_000_000_000, bytes_accessed=20_000_000, transcendentals=4_000_000
        ),
    )(clips, cotangent, spectral_weight, point_weight, bias.reshape(1, 64), col, fwd, inv, perm)
    return pl.pallas_call(
        finish,
        out_shape=(jax.ShapeDtypeStruct((2, 64, 32, 512), BF), grad_shape),
        in_specs=[vmem, vmem, any_spec, vmem],
        out_specs=(any_spec, any_spec),
        scratch_shapes=[
            pltpu.VMEM((64, 32, 512), BF),
            pltpu.VMEM((128, 512), BF),
            dma((4,)),
        ],
        compiler_params=pltpu.CompilerParams(vmem_limit_bytes=16 * 1024 * 1024),
        cost_estimate=pl.CostEstimate(
            flops=600_000_000, bytes_accessed=10_000_000, transcendentals=0
        ),
    )(side, last, col, sgrad)


def solution(mesh):
    in_specs = (
        P("dp", None, "pencil", None),
        P("dp", None, "pencil", None),
        P(None, "pencil", None, None),
        P(),
        P(),
    )
    out_specs = (P("dp", None, "pencil", None), P("dp", "pencil", None, None))
    return jax.shard_map(
        functools.partial(shards, mesh.shape["dp"]),
        mesh=mesh,
        in_specs=in_specs,
        out_specs=out_specs,
        check_vma=False,
    )
```

```python
import functools
import math

import jax
import jax.numpy as jnp
import ml_dtypes
import numpy as np
from jax import lax
from jax.experimental import pallas as pl
from jax.experimental.pallas import tpu as pltpu
from jax.sharding import PartitionSpec as P

TWO_PI = 2.0 * math.pi
MESH = pl.DeviceIdType.MESH
BF = jnp.bfloat16
F32 = jnp.float32
GROUP = 16
TN = (((0,), (0,)), ((), ()))
NT = (((1,), (1,)), ((), ()))
NN = (((1,), (0,)), ((), ()))


def dot(a, b, dims=NN):
    return lax.dot_general(a, b, dims, preferred_element_type=F32)


def tables():
    w = np.arange(512)
    j = np.arange(64).reshape(16, 4)
    phase = (j[:, :, None] * w % 512) * (TWO_PI / 512)
    col = np.stack([np.cos(phase), np.sin(phase)], axis=1).reshape(128, 512)
    k = np.arange(64)
    f = np.where(k < 32, k, 448 + k)
    h = np.arange(512)
    phase = (h[:, None] * f[None, :] % 512) * (TWO_PI / 512)
    ca, sa = np.cos(phase), np.sin(phase)
    r = np.stack([ca, sa], axis=1).reshape(16, 32, 128)
    eye = np.eye(4)
    fwd = np.einsum("shn,cd->schdn", r, eye).reshape(2048, 512)
    first = np.stack([ca, -sa], axis=1)
    second = np.stack([-sa, -ca], axis=1)
    inv = np.stack([first, second], axis=1).reshape(16, 32, 2, 128)
    inv = np.einsum("shqn,cd->cnsqdh", inv, eye).reshape(512, 4096)
    perm = np.einsum("ad,be,cf,t->abtcfed", np.eye(4), np.eye(16), np.eye(4), np.ones(2))
    perm = perm.reshape(512, 256)
    return [np.asarray(t, np.float32).astype(ml_dtypes.bfloat16) for t in (col, fwd, inv, perm)]


def derivative(z):
    e = jnp.exp2((z * z * (-0.5 / math.log(2.0))).astype(BF))
    d = 1.0 + (0.3275911 / math.sqrt(2.0)) * jnp.abs(z)
    t = pl.reciprocal(d.astype(BF), approx=True).astype(BF)
    z = z.astype(BF)
    poly = jnp.full_like(t, 1.061405429 * 0.5)
    for c in (-1.453152027, 1.421413741, -0.284496736, 0.254829592):
        poly = poly * t + jnp.asarray(0.5 * c, BF)
    q = e * (poly * t - jnp.abs(z) * jnp.asarray(1.0 / math.sqrt(TWO_PI), BF))
    return jnp.where(z >= 0, 1 - q, q)


PEERS = (
    (1, 2, 0), (0, 2, 1), (1, 1, 1), (0, 1, 0), (1, 3, 0), (0, 3, 1), (1, 0, 1), (0, 2, 0),
    (1, 2, 1), (0, 1, 1), (1, 1, 0), (0, 3, 0), (1, 3, 1), (0, 0, 1), (1, 0, 0),
)


def kernel(
    dps,
    clips, cot, weight, pw, bias, col_h, fwd_h, inv_h, perm_h,
    side, last, sgrad,
    xv, cv, wv, col, fwd, inv, perm,
    send, recv, zs, dz, ya,
    xbf, xb, xbr, gbf, gb, gbr, dd, y3, kf, kb, bcol,
    in_sem, clip_sem, a2a_send, a2a_recv, dp_send, dp_recv,
):
    pen = lax.axis_index("pencil")
    dpi = lax.axis_index("dp")
    per = 512 // dps
    kper = 64 // dps

    def clip_piece(b, n):
        at = pl.ds(n * 8, 8)
        return pltpu.make_async_copy(clips.at[b, at], xv.at[b, at], clip_sem.at[b, n])

    def load(src, dst, pieces, i):
        size = dst.shape[0] // pieces
        for n in range(pieces):
            at = pl.ds(n * size, size)
            pltpu.make_async_copy(src.at[at], dst.at[at], in_sem.at[i]).start()
        return pltpu.make_async_copy(dst, dst, in_sem.at[i]).wait

    col_wait = load(col_h, col, 1, 0)
    for b in range(2):
        for n in range(8):
            clip_piece(b, n).start()

    def peer_of(dx, dy, dc):
        return (pen // 8 + dx) % 2 * 8 + (pen // 2 + dy) % 4 * 2 + (pen + dc) % 2

    barrier = pltpu.get_barrier_semaphore()
    for steps in PEERS:
        peer = {"pencil": peer_of(*steps)}
        pl.semaphore_signal(barrier, inc=1, device_id=peer, device_id_type=MESH)

    def greet_dp(r, carry):
        pl.semaphore_signal(barrier, inc=1, device_id={"dp": (dpi + r) % dps}, device_id_type=MESH)
        return carry

    if dps > 1:
        lax.fori_loop(1, dps, greet_dp, 0)

    lane = lax.broadcasted_iota(jnp.int32, (1, 128), 1)
    low = lane < 64
    sign = jnp.where(low, 1.0, -1.0).astype(F32)

    def slots(b, phase):
        return last if (phase, b) == (3, 1) else recv.at[phase, b]

    def columns(rows, b, phase, n):
        part = dot(col[...], rows, NT)
        pieces = [part[:, i * 128 : (i + 1) * 128].reshape(GROUP, 8, 128) for i in range(2)]
        at = pl.ds(pl.multiple_of(n * 16, 16), 16)
        send[phase, b, :, at, :] = jnp.concatenate(pieces, axis=1).astype(BF)

    def clip_columns(b):
        def step(n, carry):
            clip_piece(b, n).wait()
            columns(xv[b, pl.ds(pl.multiple_of(n * 8, 8), 8)].reshape(256, 512), b, 0, n)
            return carry

        lax.fori_loop(0, 8, step, 0, unroll=2)

    def send_one(b, phase, to):
        pltpu.make_async_remote_copy(
            src_ref=send.at[phase, b, to],
            dst_ref=slots(b, phase).at[pen],
            send_sem=a2a_send.at[phase, b],
            recv_sem=a2a_recv.at[phase, b],
            device_id={"pencil": to},
            device_id_type=MESH,
        ).start()

    def keep_own(b, phase):
        pltpu.make_async_copy(
            send.at[phase, b, pen], slots(b, phase).at[pen], a2a_recv.at[phase, b]
        ).start()

    def scatter(b, phase):
        for steps in PEERS:
            send_one(b, phase, peer_of(*steps))
        keep_own(b, phase)

    def arrived(b, phase):
        whole = slots(b, phase)
        pltpu.make_async_copy(whole, whole, a2a_recv.at[phase, b]).wait()

    def spectrum(b, phase):
        arrived(b, phase)
        lhs = jnp.concatenate([recv[phase, b, s] for s in range(GROUP)], axis=1)
        upper = lax.broadcasted_iota(jnp.int32, (128, 128), 0) % 8 < 4
        pieces = []
        for n in range(2):
            wide = dot(lhs, fwd[:, n * 256 : (n + 1) * 256])
            for i in range(2):
                part = wide[:, i * 128 : (i + 1) * 128]
                sine = pltpu.roll(pltpu.roll(part, 64, 1), 124, 0)
                pieces.append(jnp.where(upper, part * sign - sine, 0.0).astype(BF))
        return dot(jnp.concatenate(pieces, axis=0), perm[...], TN)

    def to_owner(src, dst, i):
        def step(r, carry):
            to = (dpi + r) % dps
            pltpu.make_async_remote_copy(
                src_ref=src.at[to],
                dst_ref=dst.at[dpi],
                send_sem=dp_send.at[i],
                recv_sem=dp_recv.at[i],
                device_id={"dp": to},
                device_id_type=MESH,
            ).start()
            return carry

        if dps > 1:
            lax.fori_loop(1, dps, step, 0)
        pltpu.make_async_copy(src.at[dpi], dst.at[dpi], dp_recv.at[i]).start()

    def rows_back(i, b, phase):
        turned = dot(perm[...], ya[i, b], NT).astype(BF)
        lhs = jnp.concatenate([turned[c * 128 : (c + 1) * 128] for c in range(4)], axis=1)
        upper = lax.broadcasted_iota(jnp.int32, (128, 128), 0) % 8 < 4
        for steps in PEERS + ((0, 0, 0),):
            to = peer_of(*steps)
            lines = dot(lhs, inv[:, pl.ds(pl.multiple_of(to * 256, 256), 256)])
            send[phase, b, to] = jnp.where(upper, lines[:, :128], lines[:, 128:]).astype(BF)
            if steps == (0, 0, 0):
                keep_own(b, phase)
            else:
                send_one(b, phase, to)

    def field(ref, n):
        tile = ref[:, pl.ds(pl.multiple_of(n * 16, 16), 16), :].astype(F32)
        for i in range(2):
            lines = tile[:, i * 8 : (i + 1) * 8].reshape(128, 128).astype(BF)
            yield pl.ds(pl.multiple_of(n * 8 + i * 4, 4), 4), dot(lines, col[...], TN)

    def mix_points(values, b, matrix, add, tiles=(0, 2)):
        def step(t, carry):
            at = pl.multiple_of(t * 16, 16)
            for n in range(2):
                lanes = slice(n * 256, (n + 1) * 256)
                tile = values[b, :, pl.ds(at, 16), lanes].astype(F32)
                parts = []
                for i in range(2):
                    rows = tile[:, i * 8 : (i + 1) * 8].reshape(512, 256).astype(BF)
                    got = dot(matrix[...], rows)
                    if add is not None:
                        got = got + jnp.concatenate([add[...]] * 2, axis=1)
                        to = pl.multiple_of(t * 16 + i * 8, 8)
                        zs[b, :, pl.ds(to, 8), lanes] = got.reshape(64, 8, 256)
                    parts.append(got.reshape(64, 8, 256))
                if add is None:
                    side[b, :, pl.ds(at, 16), lanes] = jnp.concatenate(parts, axis=1).astype(BF)
            return carry

        lax.fori_loop(*tiles, step, 0)

    row16 = lax.broadcasted_iota(jnp.int32, (16, 128), 0)
    scale = jnp.where(pen == 0, 1.0, 2.0).astype(F32) / 262144.0
    scale_lane = jnp.where(jnp.logical_and(low, pen == 0), 1.0, 2.0).astype(F32) / 262144.0

    pairs = kper // 2

    def own_rows(pair):
        return pl.ds(pl.multiple_of(pair % pairs * 16, 16), 16)

    def mix_modes(b):
        spec = spectrum(b, 0).astype(BF).astype(F32)
        for ri in range(2):
            for j in range(4):
                for p in range(2):
                    if p != j // 2:
                        continue
                    part = spec[ri * 64 : (ri + 1) * 64, p * 128 : (p + 1) * 128]
                    part = jnp.where(low if j % 2 == 0 else jnp.logical_not(low), part, 0.0)
                    xbf[p, pl.ds(ri * 4 + j, 64, stride=8), :] = part
        for p in range(2):
            xb[:, b, :, p * 128 : (p + 1) * 128] = xbf[p].astype(BF).reshape(dps, per, 128)

        def step(n, carry):
            for i in range(8):
                pair = n * 8 + i
                at = pl.multiple_of(pair * 16, 16)
                both = jnp.concatenate(
                    [wv[2 * pair].reshape(256, 128), wv[2 * pair + 1].reshape(256, 128)], axis=1
                )
                got = dot(xb[pair // pairs, b, own_rows(pair), :], both)
                y3[pl.ds(at, 8), :] = got[:8, :128]
                y3[pl.ds(at + 8, 8), :] = got[8:, 128:]
            return carry

        lax.fori_loop(0, 4, step, 0)
        modes = []
        for j in range(4):
            real = y3[pl.ds(j, 64, stride=8), :]
            imag = y3[pl.ds(4 + j, 64, stride=8), :]
            mixed = real - sign * pltpu.roll(imag, 64, 1)
            modes.append(mixed * (scale if j == 0 else 2.0 / 262144.0))
        for p in range(2):
            first, second = modes[2 * p], modes[2 * p + 1]
            real = jnp.where(low, first, pltpu.roll(second, 64, 1))
            imag = jnp.where(low, pltpu.roll(first, 64, 1), second)
            ya[0, b, 0:64, p * 128 : (p + 1) * 128] = real.astype(BF)
            ya[0, b, 64:128, p * 128 : (p + 1) * 128] = imag.astype(BF)
        rows_back(0, b, 1)

    def grad_modes(b):
        spec = spectrum(b, 2)
        for p in range(2):
            part = spec[:, p * 128 : (p + 1) * 128]
            part = part * (scale_lane if p == 0 else 2.0 / 262144.0)
            real, imag = part[:64], part[64:]
            real_r, imag_r = pltpu.roll(real, 64, 1), pltpu.roll(imag, 64, 1)
            for i, (re, im) in enumerate(
                ((jnp.where(low, real, imag_r), jnp.where(low, imag, real_r)),
                 (jnp.where(low, real_r, imag), jnp.where(low, imag_r, real)))
            ):
                gbf[pl.ds(2 * p + i, 64, stride=8), :] = re
                gbf[pl.ds(4 + 2 * p + i, 64, stride=8), :] = im * sign
        gb[:, b] = gbf[...].astype(BF).reshape(dps, per, 128)

        def step(n, carry):
            for i in range(8):
                pair = n * 8 + i
                at = pl.multiple_of(pair * 16, 16)
                rhs = wv[pl.ds(2 * pair, 2)].reshape(512, 128)
                got = dot(gb[pair // pairs, b, own_rows(pair), :], rhs, NT)
                for p in range(2):
                    dd[p, pl.ds(at, 8), :] = got[:8, p * 128 : (p + 1) * 128]
                    dd[p, pl.ds(at + 8, 8), :] = got[8:, 256 + p * 128 : 384 + p * 128]
            return carry

        lax.fori_loop(0, 4, step, 0)
        for p in range(2):
            for ri in range(2):
                first = dd[p, pl.ds(ri * 4 + 2 * p, 64, stride=8), :]
                second = dd[p, pl.ds(ri * 4 + 2 * p + 1, 64, stride=8), :]
                ya[1, b, ri * 64 : (ri + 1) * 64, p * 128 : (p + 1) * 128] = jnp.where(
                    low, first, second
                ).astype(BF)
        rows_back(1, b, 3)

    def activation(b, chunks):
        def step(n, carry):
            grads = []
            for at, got in field(recv.at[1, b], n):
                z = got + zs[b, at].reshape(128, 512)
                grads.append(cv[b, at].reshape(128, 512) * derivative(z))
                dz[b, at] = grads[-1].reshape(4, 32, 512)
            columns(jnp.concatenate(grads, axis=0), b, 2, n)
            return carry

        lax.fori_loop(*chunks, step, 0, unroll=2)

    def finish_first():
        arrived(0, 3)

        def step(n, carry):
            for at, got in field(recv.at[3, 0], n):
                got = got + side[0, at].reshape(128, 512).astype(F32)
                side[0, at] = got.astype(BF).reshape(4, 32, 512)
            return carry

        lax.fori_loop(0, 8, step, 0, unroll=2)

    def weight_grad():
        for i, ref in enumerate((xbr, gbr)):
            pltpu.make_async_copy(ref, ref, dp_recv.at[i]).wait()
        first_rows = jnp.where(row16 < 8, 1.0, 0.0).astype(F32)
        for pair in range(pairs):
            at = slice(pair * 16, (pair + 1) * 16)
            left = xbr[:, :, at, :].reshape(2 * dps * 16, 256)
            right = gbr[:, :, at, :].astype(F32)
            head = (right * first_rows).astype(BF).reshape(2 * dps * 16, 128)
            tail = (right * (1.0 - first_rows)).astype(BF).reshape(2 * dps * 16, 128)
            got = dot(left, jnp.concatenate([head, tail], axis=1), TN)
            for i in range(2):
                sgrad[2 * pair + i] = got[:, i * 128 : (i + 1) * 128].reshape(4, 64, 128)

    col_wait()
    clip_columns(0)
    pl.semaphore_wait(barrier, GROUP - 1 + dps - 1)
    scatter(0, 0)
    fwd_wait = load(fwd_h, fwd, 4, 1)
    perm_wait = load(perm_h, perm, 2, 2)
    clip_columns(1)
    scatter(1, 0)
    weight_wait = load(weight, wv, 16, 3)
    inv_wait = load(inv_h, inv, 8, 4)
    cot_waits = [load(cot.at[b], cv.at[b], 8, 5 + b) for b in range(2)]

    row = lax.broadcasted_iota(jnp.int32, (512, 64), 0)
    lanes64 = lax.broadcasted_iota(jnp.int32, (512, 64), 1)
    spread = jnp.where(row // 8 == lanes64, 1.0, 0.0).astype(BF)
    same = (
        lax.broadcasted_iota(jnp.int32, (512, 512), 0) % 8
        == lax.broadcasted_iota(jnp.int32, (512, 512), 1) % 8
    )
    for p in range(2):
        xbf[p] = jnp.zeros((512, 128), F32)
    kf[...] = jnp.where(same, dot(dot(spread, pw[...], NT).astype(BF), spread, NT), 0.0).astype(BF)
    kb[...] = jnp.where(same, dot(dot(spread, pw[...]).astype(BF), spread, NT), 0.0).astype(BF)
    biased = (spread.astype(F32) * bias[...].astype(F32)).astype(BF)
    bcol[...] = dot(biased, jnp.ones((64, 128), BF))
    mix_points(xv, 0, kf, bcol)

    fwd_wait()
    perm_wait()
    inv_wait()
    weight_wait()
    mix_modes(0)
    mix_modes(1)
    mix_points(xv, 1, kf, bcol)

    cot_waits[0]()
    arrived(0, 1)
    activation(0, (0, 8))
    scatter(0, 2)
    to_owner(xb, xbr, 0)
    cot_waits[1]()
    arrived(1, 1)
    activation(1, (0, 8))
    scatter(1, 2)
    grad_modes(0)
    mix_points(dz, 0, kb, None, (0, 1))
    grad_modes(1)
    to_owner(gb, gbr, 1)
    mix_points(dz, 0, kb, None, (1, 2))
    mix_points(dz, 1, kb, None)
    finish_first()
    weight_grad()

    for phase in range(4):
        for b in range(2):
            sent = send.at[phase, b, pl.ds(0, GROUP - 1)]
            pltpu.make_async_copy(sent, sent, a2a_send.at[phase, b]).wait()
    if dps > 1:
        for i, ref in enumerate((xb, gb)):
            sent = ref.at[pl.ds(0, dps - 1)]
            pltpu.make_async_copy(sent, sent, dp_send.at[i]).wait()
    arrived(1, 3)


def finish(side, lines, col_h, sgrad, out, weights_out, ov, col, sem):
    col_copy = pltpu.make_async_copy(col_h, col, sem.at[0])
    col_copy.start()
    for n in range(8):
        at = pl.ds(n * 8, 8)
        pltpu.make_async_copy(side.at[0, at], out.at[0, at], sem.at[1]).start()
    away = pltpu.make_async_copy(sgrad, weights_out, sem.at[2])
    away.start()
    col_copy.wait()

    def step(n, carry):
        tile = lines[:, pl.ds(pl.multiple_of(n * 16, 16), 16), :].astype(F32)
        for i in range(2):
            at = pl.ds(pl.multiple_of(n * 8 + i * 4, 4), 4)
            part = tile[:, i * 8 : (i + 1) * 8].reshape(128, 128).astype(BF)
            got = dot(part, col[...], TN) + side[1, at].reshape(128, 512).astype(F32)
            ov[at] = got.astype(BF).reshape(4, 32, 512)
        at = pl.ds(n * 8, 8)
        pltpu.make_async_copy(ov.at[at], out.at[1, at], sem.at[3]).start()
        return carry

    lax.fori_loop(0, 8, step, 0, unroll=2)
    pltpu.make_async_copy(side.at[0], side.at[0], sem.at[1]).wait()
    pltpu.make_async_copy(ov, ov, sem.at[3]).wait()
    away.wait()


def shards(dps, clips, cotangent, spectral_weight, point_weight, bias):
    col, fwd, inv, perm = [jnp.asarray(t) for t in tables()]
    any_spec = pl.BlockSpec(memory_space=pl.ANY)
    vmem = pl.BlockSpec(memory_space=pltpu.VMEM)
    per = 512 // dps
    dma = pltpu.SemaphoreType.DMA
    grad_shape = jax.ShapeDtypeStruct((64 // dps, 4, 64, 128), F32)
    side, last, sgrad = pl.pallas_call(
        functools.partial(kernel, dps),
        out_shape=(
            pltpu.VMEM((2, 64, 32, 512), BF),
            pltpu.VMEM((GROUP, 128, 128), BF),
            pltpu.VMEM(grad_shape.shape, F32),
        ),
        in_specs=[any_spec] * 3 + [vmem] * 2 + [any_spec] * 4,
        out_specs=(vmem, vmem, vmem),
        scratch_shapes=[
            pltpu.VMEM((2, 64, 32, 512), BF),
            pltpu.VMEM((2, 64, 32, 512), BF),
            pltpu.VMEM((64, 4, 64, 128), BF),
            pltpu.VMEM((128, 512), BF),
            pltpu.VMEM((2048, 512), BF),
            pltpu.VMEM((512, 4096), BF),
            pltpu.VMEM((512, 256), BF),
            pltpu.VMEM((4, 2, GROUP, 128, 128), BF),
            pltpu.VMEM((4, 2, GROUP, 128, 128), BF),
            pltpu.VMEM((2, 64, 32, 512), F32),
            pltpu.VMEM((2, 64, 32, 512), BF),
            pltpu.VMEM((2, 2, 128, 256), BF),
            pltpu.VMEM((2, 512, 128), F32),
            pltpu.VMEM((dps, 2, per, 256), BF),
            pltpu.VMEM((dps, 2, per, 256), BF),
            pltpu.VMEM((512, 128), F32),
            pltpu.VMEM((dps, 2, per, 128), BF),
            pltpu.VMEM((dps, 2, per, 128), BF),
            pltpu.VMEM((2, 512, 128), F32),
            pltpu.VMEM((512, 128), F32),
            pltpu.VMEM((512, 512), BF),
            pltpu.VMEM((512, 512), BF),
            pltpu.VMEM((512, 128), F32),
            dma((7,)),
            dma((2, 8)),
            dma((4, 2)),
            dma((4, 2)),
            dma((2,)),
            dma((2,)),
        ],
        compiler_params=pltpu.CompilerParams(
            collective_id=0, has_side_effects=True, vmem_limit_bytes=54 * 1024 * 1024
        ),
        cost_estimate=pl.CostEstimate(
            flops=20_000_000_000, bytes_accessed=20_000_000, transcendentals=4_000_000
        ),
    )(clips, cotangent, spectral_weight, point_weight, bias.reshape(1, 64), col, fwd, inv, perm)
    return pl.pallas_call(
        finish,
        out_shape=(jax.ShapeDtypeStruct((2, 64, 32, 512), BF), grad_shape),
        in_specs=[vmem, vmem, any_spec, vmem],
        out_specs=(any_spec, any_spec),
        scratch_shapes=[
            pltpu.VMEM((64, 32, 512), BF),
            pltpu.VMEM((128, 512), BF),
            dma((4,)),
        ],
        compiler_params=pltpu.CompilerParams(vmem_limit_bytes=16 * 1024 * 1024),
        cost_estimate=pl.CostEstimate(
            flops=600_000_000, bytes_accessed=10_000_000, transcendentals=0
        ),
    )(side, last, col, sgrad)


def solution(mesh):
    in_specs = (
        P("dp", None, "pencil", None),
        P("dp", None, "pencil", None),
        P(None, "pencil", None, None),
        P(),
        P(),
    )
    out_specs = (P("dp", None, "pencil", None), P("dp", "pencil", None, None))
    return jax.shard_map(
        functools.partial(shards, mesh.shape["dp"]),
        mesh=mesh,
        in_specs=in_specs,
        out_specs=out_specs,
        check_vma=False,
    )
```
